128 devices in a mesh: dp: 32 (over y_lo, x, z), tensor: 4 (over y_hi, core).
Axes of the slice: x: 4, y: 4 (y_hi: 2, y_lo: 2; y = y_hi * 2 + y_lo), z: 4, core: 2. Of those that a mesh axis runs over, the one named last changes fastest.
Arguments:
- tokens: bfloat16 [32, 512, 768], P('dp', 'tensor'), may hold values from -6 to 6
- segments: int32 [32, 512], P('dp'), may hold values from 0 to 1, as said below
- q_weight: bfloat16 [768, 768], P('dp', 'tensor'), may hold values from -0.21875 to 0.21875
- k_weight: bfloat16 [768, 768], P('dp', 'tensor'), may hold values from -0.21875 to 0.21875
- v_weight: bfloat16 [768, 768], P('dp', 'tensor'), may hold values from -0.21875 to 0.21875
- up_weight: bfloat16 [768, 3072], P('dp', 'tensor'), may hold values from -0.21875 to 0.21875
- out_weight: bfloat16 [768, 768], P('dp', 'tensor'), may hold values from -1.75 to 1.75
- down_weight: bfloat16 [768, 3072], P('dp', 'tensor'), may hold values from -0.109375 to 0.109375
- q_bias: float32 [768], P(('dp', 'tensor')), may hold values from -4 to 4
- v_bias: float32 [768], P(('dp', 'tensor')), may hold values from -1.5 to 1.5
- out_bias: float32 [768], P(('dp', 'tensor')), may hold values from -4 to 4
- up_bias: float32 [3072], P(('dp', 'tensor')), may hold values from -6 to 6
- down_bias: float32 [768], P(('dp', 'tensor')), may hold values from -4 to 4
- norm1_gain: float32 [768], P(('dp', 'tensor')), may hold values from 0.5 to 1.5
- norm1_shift: float32 [768], P(('dp', 'tensor')), may hold values from -3 to 3
- norm2_gain: float32 [768], P(('dp', 'tensor')), may hold values from 0.5 to 1.5
- norm2_shift: float32 [768], P(('dp', 'tensor')), may hold values from -3 to 3
- cotangent: bfloat16 [32, 512, 768], P('dp', 'tensor'), may hold values from -6 to 6
Outputs:
- layer_output: bfloat16 [32, 512, 768], P('dp', 'tensor')
- input_grad: float32 [32, 512, 768], P('dp', 'tensor')
- q_weight_grad: float32 [768, 768], P('dp', 'tensor')
- k_weight_grad: float32 [768, 768], P('dp', 'tensor')
- v_weight_grad: float32 [768, 768], P('dp', 'tensor')
- up_weight_grad: float32 [768, 3072], P('dp', 'tensor')
- out_weight_grad: float32 [768, 768], P('dp', 'tensor')
- down_weight_grad: float32 [768, 3072], P('dp', 'tensor')
- q_bias_grad: float32 [768], P(('dp', 'tensor'))
- v_bias_grad: float32 [768], P(('dp', 'tensor'))
- out_bias_grad: float32 [768], P(('dp', 'tensor'))
- up_bias_grad: float32 [3072], P(('dp', 'tensor'))
- down_bias_grad: float32 [768], P(('dp', 'tensor'))
- norm1_gain_grad: float32 [768], P(('dp', 'tensor'))
- norm1_shift_grad: float32 [768], P(('dp', 'tensor'))
- norm2_gain_grad: float32 [768], P(('dp', 'tensor'))
- norm2_shift_grad: float32 [768], P(('dp', 'tensor'))
The draws below stay inside these ranges and needn't reach their ends.
Inputs may be any that keep to these rules, and one draw needn't show every extreme that they name: `segments`: along each sequence the numbers never fall and begin at 0; tokens with equal numbers in one sequence form one document piece, and attention stays within it. A piece that lies between two others has at least 512 * 200 // 512 tokens.
All inputs are finite; a program needn't handle non-finite values.
Results may differ from the reference program's by a relative error of at most 0.025.
Values may be sent and summed in bfloat16 or wider, within the bound.
No kernel may reach another device: no remote copies, remote signals or barrier semaphores. Data moves between devices by JAX's collectives and lax.ppermute only.
A program may use at most 64 MiB of HBM per device.

```python
import math
import jax
import jax.numpy as jnp
from jax import lax

HEADS = 12
HEAD_DIM = 64
D = 768
FF = 3072
LEN = 512
SEQ_DEV = 1
SEQS = 32


def draw_segments(key, part):
    key = jax.random.fold_in(key, 7)
    key_first, key_second, key_whole, key_pick = jax.random.split(key, 4)
    least_piece = LEN * 200 // 512
    first_cut = jax.random.randint(key_first, (SEQS,), 1, LEN - least_piece)
    room = LEN - first_cut - least_piece
    second_cut = first_cut + least_piece + jax.random.randint(key_second, (SEQS,), 0, room)
    whole_cut = jax.random.randint(key_whole, (SEQS,), LEN - LEN // 8, LEN)
    chosen = jax.random.randint(key_pick, (SEQS // SEQ_DEV,), 0, SEQ_DEV)
    sequence_index = jnp.arange(SEQS)
    picked = sequence_index % SEQ_DEV == chosen[sequence_index // SEQ_DEV]
    cut_one = jnp.where(picked, whole_cut, first_cut)
    cut_two = jnp.where(picked, LEN, second_cut)
    places = jnp.arange(LEN)
    flags = (places[None, :] >= cut_one[:, None]).astype(jnp.int32) + (places[None, :] >= cut_two[:, None]).astype(jnp.int32)
    return flags.astype(jnp.int32)


def block_levels(rng, shape, cuts, least, high):
    def one(axis_at, blocks):
        steps = jax.random.uniform(jax.random.fold_in(jax.random.fold_in(rng, 6), axis_at), (blocks,), jnp.float32, least / len(cuts), high / len(cuts))
        return jnp.repeat(jnp.exp(steps), shape[axis_at] // blocks).reshape((-1,) + (1,) * (len(shape) - axis_at - 1))

    loudness = one(*cuts[0])
    for cut in cuts[1:]:
        loudness = loudness * one(*cut)
    return loudness


def normal_values(key, extent, scale, most, shards=(), dtype=jnp.bfloat16):
    entries = jax.random.normal(key, extent, jnp.float32) * scale
    if len(shards) > 0:
        entries = block_levels(key, extent, shards, -0.22, 0.18) * entries
    return jnp.clip(entries, min=-most, max=most).astype(dtype)


def setup_inputs(seed: int = 0) -> dict:
    splits = jax.random.split(jax.random.key(seed), 19)
    return {
        "tokens": normal_values(splits[0], (SEQS, LEN, D), 1.0, 6.0, ((0, 32), (1, 4))),
        "segments": draw_segments(jax.random.fold_in(splits[18], 71), 0),
        "q_weight": normal_values(splits[2], (D, D), D ** -0.5, 0.21875, ((0, 32), (1, 4))),
        "k_weight": normal_values(splits[3], (D, D), D ** -0.5, 0.21875, ((0, 32), (1, 4))),
        "v_weight": normal_values(splits[4], (D, D), D ** -0.5, 0.21875, ((0, 32), (1, 4))),
        "up_weight": normal_values(splits[5], (D, FF), D ** -0.5, 0.21875, ((0, 32), (1, 4))),
        "out_weight": normal_values(splits[6], (D, D), (D // 64) ** -0.5, 1.75, ((0, 32), (1, 4))),
        "down_weight": normal_values(splits[7], (D, FF), FF ** -0.5, 0.109375, ((0, 32), (1, 4))),
        "q_bias": normal_values(splits[8], (D,), 0.3, 4.0, ((0, 128),), jnp.float32),
        "v_bias": normal_values(splits[9], (D,), 0.1, 1.5, ((0, 128),), jnp.float32),
        "out_bias": normal_values(splits[10], (D,), 0.3, 4.0, ((0, 128),), jnp.float32),
        "up_bias": normal_values(splits[11], (FF,), 0.5, 6.0, ((0, 128),), jnp.float32),
        "down_bias": normal_values(splits[12], (D,), 0.3, 4.0, ((0, 128),), jnp.float32),
        "norm1_gain": jnp.clip(1.0 + 0.1 * jax.random.normal(splits[13], (D,), jnp.float32), 0.5, 1.5),
        "norm1_shift": normal_values(splits[14], (D,), 0.2, 3.0, ((0, 128),), jnp.float32),
        "norm2_gain": jnp.clip(1.0 + 0.1 * jax.random.normal(splits[15], (D,), jnp.float32), 0.5, 1.5),
        "norm2_shift": normal_values(splits[16], (D,), 0.2, 3.0, ((0, 128),), jnp.float32),
        "cotangent": normal_values(splits[17], (SEQS, LEN, D), 1.0, 6.0, ((0, 32), (1, 4))),
    }


@jax.custom_vjp
def low(v):
    return lax.optimization_barrier(v.astype(jnp.bfloat16)).astype(jnp.float32)

@jax.custom_vjp
def low_back(v):
    return v

def low_keep(v):
    return (low(v), None)

def low_pass(kept, grad):
    return (grad,)

def back_keep(v):
    return (v, None)

def back_low(kept, grad):
    return (low(grad),)
low.defvjp(low_keep, low_pass)
low_back.defvjp(back_keep, back_low)
NORM_EPSILON = 1e-12
MASKED_SCORE = -1000000000.0
ROOT_HALF = 0.7071067811865476
HIGHEST = lax.Precision.HIGHEST

def matmul(left, right):
    return jnp.dot(left, right, precision=HIGHEST)

def layer_norm(values, gain, shift):
    center = values - lax.optimization_barrier(jnp.mean(values, axis=-1, keepdims=True))
    spread = lax.optimization_barrier(jnp.mean(center * center, axis=-1, keepdims=True))
    return center * lax.rsqrt(spread + NORM_EPSILON) * gain + shift

def gelu_exact(values):
    return 0.5 * values * (1.0 + lax.erf(values * ROOT_HALF))

def forward(params, inputs, segment_ids):
    q_weight, k_weight, v_weight, up_weight, out_weight, down_weight, q_bias, v_bias, out_bias, up_bias, down_bias, norm1_gain, norm1_shift, norm2_gain, norm2_shift = params
    blocks = inputs.shape[0]
    flattened = inputs.reshape(blocks * LEN, D)
    queries = low_back(low(matmul(flattened, q_weight) + q_bias)).reshape(blocks, LEN, HEADS, HEAD_DIM)
    key_rows = low_back(low(matmul(flattened, k_weight))).reshape(blocks, LEN, HEADS, HEAD_DIM)
    value_rows = low_back(low(matmul(flattened, v_weight) + v_bias)).reshape(blocks, LEN, HEADS, HEAD_DIM)
    scores = low_back(HEAD_DIM ** (-0.5) * jnp.einsum('bqhd,bkhd->bhqk', queries, key_rows, precision=HIGHEST))
    same_doc = segment_ids[:, None, :, None] == segment_ids[:, None, None, :]
    scores = jnp.where(same_doc, scores, MASKED_SCORE)
    shifted = jnp.exp(scores - lax.optimization_barrier(jnp.max(scores, axis=-1, keepdims=True)))
    attention = low(shifted / lax.optimization_barrier(jnp.sum(shifted, axis=-1, keepdims=True)))
    mixed_rows = jnp.einsum('bhqk,bkhd->bqhd', attention, value_rows, precision=HIGHEST)
    mixed_rows = low_back(low(mixed_rows)).reshape(blocks * LEN, D)
    attended = low_back(matmul(mixed_rows, out_weight.T) + out_bias)
    hidden = layer_norm(flattened + attended, norm1_gain, norm1_shift)
    upward = low_back(matmul(low(hidden), up_weight) + up_bias)
    active = low(gelu_exact(upward))
    branch = low_back(matmul(active, down_weight.T) + down_bias)
    result = layer_norm(hidden + branch, norm2_gain, norm2_shift)
    return result.reshape(blocks, LEN, D)

def reference(tokens, segments, q_weight, k_weight, v_weight, up_weight, out_weight, down_weight, q_bias, v_bias, out_bias, up_bias, down_bias, norm1_gain, norm1_shift, norm2_gain, norm2_shift, cotangent):
    params = tuple((array_in.astype(jnp.float32) for array_in in (q_weight, k_weight, v_weight, up_weight, out_weight, down_weight, q_bias, v_bias, out_bias, up_bias, down_bias, norm1_gain, norm1_shift, norm2_gain, norm2_shift)))
    group = math.gcd(SEQS, 8)
    step_count = SEQS // group
    inputs = tokens.astype(jnp.float32).reshape(step_count, group, LEN, D)
    segment_blocks = segments.reshape(step_count, group, LEN)
    grad_blocks = cotangent.astype(jnp.float32).reshape(step_count, group, LEN, D)

    def one_block(totals, block):
        inputs_block, segment_block, grad_block = block

        def local_forward(weights_now, inputs_now):
            return forward(weights_now, inputs_now, segment_block)
        output_block, pullback = jax.vjp(local_forward, params, inputs_block)
        weight_grads, input_grads = pullback(grad_block)
        totals = jax.tree.map(lambda left, right: left + right, totals, weight_grads)
        return (totals, (output_block.astype(jnp.bfloat16), input_grads))
    totals, (outputs, input_grads) = lax.scan(one_block, jax.tree.map(jnp.zeros_like, params), (inputs, segment_blocks, grad_blocks))
    return (outputs.reshape(SEQS, LEN, D), input_grads.reshape(SEQS, LEN, D), totals[0], totals[1], totals[2], totals[3], totals[4], totals[5], totals[6], totals[7], totals[8], totals[9], totals[10], totals[11], totals[12], totals[13], totals[14])
```

```python
import jax
import jax.numpy as jnp
from jax import lax
from jax.sharding import PartitionSpec as P

HEAD_DIM = 64


NORM_EPSILON = 1e-12
MASKED_SCORE = -1000000000.0
ROOT_HALF = 0.7071067811865476
INV_ROOT_TAU = 0.3989422804014327
LOW = jnp.bfloat16
FULL = jnp.float32


def contract(left, right, left_dim, right_dim):
    return lax.dot_general(
        left, right, (((left_dim,), (right_dim,)), ((), ())), preferred_element_type=jnp.float32
    )


def gelu_exact(values):
    return 0.5 * values * (1.0 + lax.erf(values * ROOT_HALF))


def gelu_slope(values):
    return (
        0.5 * (1.0 + lax.erf(values * ROOT_HALF))
        + values * jnp.exp(-0.5 * values * values) * INV_ROOT_TAU
    )


def norm_forward(values, gain, shift):
    center = values - jnp.mean(values, axis=-1, keepdims=True)
    scale_inv = lax.rsqrt(jnp.mean(center * center, axis=-1, keepdims=True) + NORM_EPSILON)
    normed = center * scale_inv
    return (normed * gain + shift, normed, scale_inv)


def norm_backward(upstream, normed, scale_inv, gain):
    scaled = upstream * gain
    return scale_inv * (
        scaled
        - jnp.mean(scaled, axis=-1, keepdims=True)
        - normed * jnp.mean(scaled * normed, axis=-1, keepdims=True)
    )


def swap(values, mask):
    return lax.ppermute(values, "tensor", [(i, i ^ mask) for i in range(4)])


def after(values, *others):
    return lax.optimization_barrier((values, *others))[0]


def spread(block):
    count = lax.axis_size("dp")
    stacked = jnp.broadcast_to(block[None], (count, *block.shape))
    return lax.all_to_all(stacked, "dp", 0, 0, tiled=True).reshape(-1, block.shape[1])


def gathered_sum(values):
    count = lax.axis_size("dp")
    blocks = values.astype(LOW).reshape(count, values.shape[0] // count, values.shape[1])
    got = lax.all_to_all(blocks, "dp", 0, 0, tiled=True)
    return got


def halves(values):
    high = lax.reduce_precision(values, 8, 7)
    return (high.astype(LOW), (values - high).astype(LOW))


def core_sum(part):
    half = part.shape[0] // 2
    got = swap(part[half:].astype(LOW), 1)
    return part[:half] + got.astype(FULL)


def far_sum(total):
    quarter = total.shape[0] // 2
    sent = total.astype(LOW)
    sent = jnp.concatenate([sent[quarter:], sent[:quarter]], axis=0)
    return swap(sent, 2)


def core_join(rows):
    return jnp.concatenate([rows, swap(rows, 1)], axis=0)


def ordered_segments(segment_row, my_index):
    quarters = segment_row.reshape(4, -1)
    core = my_index % 2 == 1
    quarters = jnp.where(core, quarters[jnp.array([1, 0, 3, 2])], quarters)
    far = my_index // 2 == 1
    quarters = jnp.where(far, quarters[jnp.array([2, 3, 0, 1])], quarters)
    return jnp.concatenate([quarters[0], quarters[2], quarters[1], quarters[3]])


def attend_forward(qkv_rows, same_doc, head_count, head_cols):
    outputs = []
    kept = []
    for head in range(head_count):
        offset = head * HEAD_DIM
        query = qkv_rows[:, offset : offset + HEAD_DIM]
        key = qkv_rows[:, head_cols + offset : head_cols + offset + HEAD_DIM]
        value = qkv_rows[:, 2 * head_cols + offset : 2 * head_cols + offset + HEAD_DIM]
        scores = jnp.where(
            same_doc, HEAD_DIM ** (-0.5) * contract(query, key, 1, 1), MASKED_SCORE
        )
        highest = jnp.max(scores, axis=-1, keepdims=True)
        shifted = jnp.exp(scores - highest)
        row_total = jnp.sum(shifted, axis=-1, keepdims=True)
        probs_low = (shifted / row_total).astype(LOW)
        outputs.append(jnp.dot(probs_low, value, preferred_element_type=FULL))
        kept.append(highest + jnp.log(row_total))
    return (jnp.concatenate(outputs, axis=1).astype(LOW), kept)


def attend_backward(qkv_rows, same_doc, kept, grad_rows, head_count, head_cols):
    query_grads = []
    key_grads = []
    value_grads = []
    for head in range(head_count):
        offset = head * HEAD_DIM
        query = qkv_rows[:, offset : offset + HEAD_DIM]
        key = qkv_rows[:, head_cols + offset : head_cols + offset + HEAD_DIM]
        value = qkv_rows[:, 2 * head_cols + offset : 2 * head_cols + offset + HEAD_DIM]
        scores = jnp.where(
            same_doc, HEAD_DIM ** (-0.5) * contract(query, key, 1, 1), MASKED_SCORE
        )
        probs = jnp.exp(scores - kept[head])
        grad_head = grad_rows[:, offset : offset + HEAD_DIM]
        value_grads.append(contract(probs.astype(LOW), grad_head, 0, 0))
        probs_grad = contract(grad_head, value, 1, 1)
        scores_grad = probs * (probs_grad - jnp.sum(probs * probs_grad, axis=-1, keepdims=True))
        scores_low = scores_grad.astype(LOW)
        query_grads.append(
            HEAD_DIM ** (-0.5) * jnp.dot(scores_low, key, preferred_element_type=FULL)
        )
        key_grads.append(HEAD_DIM ** (-0.5) * contract(scores_low, query, 0, 0))
    return jnp.concatenate(query_grads + key_grads + value_grads, axis=1).astype(LOW)


def shards(
    tokens,
    segments,
    q_weight,
    k_weight,
    v_weight,
    up_weight,
    out_weight,
    down_weight,
    q_bias,
    v_bias,
    out_bias,
    up_bias,
    down_bias,
    norm1_gain,
    norm1_shift,
    norm2_gain,
    norm2_shift,
    cotangent,
):
    my_index = lax.axis_index("tensor")
    local_len, width = tokens.shape[1:]
    head_cols = q_weight.shape[1]
    head_count = head_cols // HEAD_DIM
    tokens = tokens[0]
    cotangent = cotangent[0]

    vector_rows = q_bias.shape[0]
    columns = jnp.stack(
        [q_bias, v_bias, out_bias, down_bias, norm1_gain, norm1_shift, norm2_gain, norm2_shift],
        axis=1,
    )
    columns = jnp.concatenate([columns, up_bias.reshape(vector_rows, 4)], axis=1)
    column_count = columns.shape[1]
    high, low = halves(columns)
    packed = jnp.pad(
        jnp.concatenate([high, low], axis=1), ((0, 2), (0, 128 - 2 * column_count))
    )
    near = [packed] + [swap(packed, mask) for mask in (1, 2, 3)]
    tokens_far = swap(tokens, 2)
    up_full = spread(up_weight)

    near = [block[:vector_rows] for block in near]
    core = my_index % 2 == 1
    near = [
        jnp.where(core, near[1], near[0]),
        jnp.where(core, near[0], near[1]),
        jnp.where(core, near[3], near[2]),
        jnp.where(core, near[2], near[3]),
    ]
    far = my_index // 2 == 1
    near = jnp.concatenate(
        [
            jnp.where(far, near[2], near[0]),
            jnp.where(far, near[3], near[1]),
            jnp.where(far, near[0], near[2]),
            jnp.where(far, near[1], near[3]),
        ],
        axis=0,
    )
    first_block = jnp.concatenate([q_weight, k_weight, v_weight, out_weight, near], axis=1)
    first_block, tokens_pair = lax.optimization_barrier(
        (first_block, jnp.concatenate([tokens, tokens_far], axis=0), up_full)
    )[:2]
    tokens_full = core_join(tokens_pair)
    cotangent_far = swap(after(cotangent, tokens_far), 2)
    first_full = spread(first_block)
    qkv_weight = first_full[:, : 3 * head_cols]
    out_full = first_full[:, 3 * head_cols : 4 * head_cols]
    vectors = first_full[:, 4 * head_cols :].astype(FULL)
    vectors = vectors[:, :column_count] + vectors[:, column_count : 2 * column_count]
    rows = vectors[:, :8].T
    gain_first, shift_first, gain_second, shift_second = rows[4], rows[5], rows[6], rows[7]
    bias_out, bias_down = rows[2], rows[3]
    own = lax.dynamic_slice_in_dim(vectors, my_index * head_cols, head_cols, axis=0)
    bias_up = own[:, 8:12].reshape(-1)
    qkv_bias = jnp.concatenate([own[:, 0], jnp.zeros((head_cols,), FULL), own[:, 1]])

    segment_row = ordered_segments(segments[0], my_index)
    same_doc = segment_row[:, None] == segment_row[None, :]
    qkv_rows = (jnp.dot(tokens_full, qkv_weight, preferred_element_type=FULL) + qkv_bias).astype(
        LOW
    )
    mixed_rows, kept = attend_forward(qkv_rows, same_doc, head_count, head_cols)
    attn_chip = core_sum(contract(mixed_rows, out_full, 1, 1))
    attn_far = far_sum(attn_chip)
    down_full = spread(after(down_weight, attn_chip))
    attn_chip, attn_far, down_full = lax.optimization_barrier((attn_chip, attn_far, down_full))
    first, normed_first, inv_first = norm_forward(
        tokens_pair.astype(FULL) + (attn_chip + attn_far.astype(FULL)) + bias_out,
        gain_first,
        shift_first,
    )
    hidden_full = core_join(first.astype(LOW))
    upward = jnp.dot(hidden_full, up_full, preferred_element_type=FULL) + bias_up
    active = gelu_exact(upward).astype(LOW)
    branch_chip = core_sum(contract(active, down_full, 1, 1))
    branch = branch_chip + far_sum(branch_chip).astype(FULL)
    layer_output, normed_second, inv_second = norm_forward(
        first + branch + bias_down, gain_second, shift_second
    )

    cotangent_pair = jnp.concatenate([cotangent, cotangent_far], axis=0).astype(FULL)
    second_grad = norm_backward(cotangent_pair, normed_second, inv_second, gain_second)
    cotangent_own = cotangent_pair[:local_len]
    grad_gain_second = jnp.sum(cotangent_own * normed_second[:local_len], axis=0)
    grad_shift_second = jnp.sum(cotangent_own, axis=0)
    branch_low = second_grad.astype(LOW)
    grad_bias_down = jnp.sum(branch_low[:local_len].astype(FULL), axis=0)
    branch_full = core_join(branch_low)
    active_grad = jnp.dot(branch_full, down_full, preferred_element_type=FULL)
    upward_grad = (active_grad * gelu_slope(upward)).astype(LOW)
    hidden_chip = core_sum(contract(upward_grad, up_full, 1, 1))
    grad_down = contract(branch_full, active, 0, 0)
    hidden_far = far_sum(hidden_chip)
    down_blocks = gathered_sum(after(grad_down, hidden_chip))
    hidden_chip, hidden_far, down_blocks = lax.optimization_barrier(
        (hidden_chip, hidden_far, down_blocks)
    )
    grad_bias_up = jnp.sum(upward_grad.astype(FULL), axis=0)
    grad_up = contract(hidden_full, upward_grad, 0, 0)
    first_grad = second_grad + (hidden_chip + hidden_far.astype(FULL))
    resid_grad = norm_backward(first_grad, normed_first, inv_first, gain_first)
    first_own = first_grad[:local_len]
    grad_gain_first = jnp.sum(first_own * normed_first[:local_len], axis=0)
    grad_shift_first = jnp.sum(first_own, axis=0)
    attended_low = resid_grad.astype(LOW)
    grad_bias_out = jnp.sum(attended_low[:local_len].astype(FULL), axis=0)
    attended_full = core_join(attended_low)
    mixed_grad = jnp.dot(attended_full, out_full, preferred_element_type=FULL).astype(LOW)
    qkv_grad = attend_backward(qkv_rows, same_doc, kept, mixed_grad, head_count, head_cols)

    grad_bias_query = jnp.sum(qkv_grad[:, :head_cols].astype(FULL), axis=0)
    grad_bias_value = jnp.sum(qkv_grad[:, 2 * head_cols :].astype(FULL), axis=0)
    sharded = jnp.concatenate(
        [grad_bias_query[None], grad_bias_value[None], grad_bias_up.reshape(head_cols, 4).T], axis=0
    )
    sharded = lax.dynamic_update_slice_in_dim(
        jnp.zeros((6, width), FULL), sharded, my_index * head_cols, 1
    )
    vector_sums = jnp.concatenate(
        [
            grad_bias_out[None],
            grad_bias_down[None],
            grad_gain_first[None],
            grad_shift_first[None],
            grad_gain_second[None],
            grad_shift_second[None],
            sharded,
        ],
        axis=0,
    )
    vector_near = [swap(vector_sums, mask) for mask in (1, 2, 3)]
    input_chip = core_sum(contract(qkv_grad, qkv_weight, 1, 1))
    input_far = swap(input_chip[local_len:].astype(LOW), 2)
    up_blocks = gathered_sum(after(grad_up, qkv_grad))
    vector_sums = vector_sums + vector_near[0] + vector_near[1] + vector_near[2]
    grad_qkv = contract(tokens_full, qkv_grad, 0, 0)
    grad_out = contract(attended_full, mixed_rows, 0, 0)
    high, low = halves(vector_sums.T)
    last_block = jnp.concatenate(
        [
            grad_qkv.astype(LOW),
            grad_out.astype(LOW),
            high,
            low,
            jnp.zeros((width, 128 - 2 * column_count), LOW),
        ],
        axis=1,
    )
    last_blocks = gathered_sum(after(last_block, up_blocks))
    input_grad = resid_grad[:local_len] + (input_chip[:local_len] + input_far.astype(FULL))

    down_sum = jnp.sum(down_blocks.astype(FULL), axis=0)
    up_sum = jnp.sum(up_blocks.astype(FULL), axis=0)
    last_sum = jnp.sum(last_blocks.astype(FULL), axis=0)
    columns = last_sum[:, 4 * head_cols :]
    columns = columns[:, :column_count] + columns[:, column_count : 2 * column_count]
    columns = lax.dynamic_slice_in_dim(columns, my_index * vector_rows, vector_rows, axis=0)
    return (
        layer_output[:local_len].astype(LOW)[None],
        input_grad[None],
        last_sum[:, :head_cols],
        last_sum[:, head_cols : 2 * head_cols],
        last_sum[:, 2 * head_cols : 3 * head_cols],
        up_sum,
        last_sum[:, 3 * head_cols : 4 * head_cols],
        down_sum,
        columns[:, 6],
        columns[:, 7],
        columns[:, 0],
        columns[:, 8:12].reshape(-1),
        columns[:, 1],
        columns[:, 2],
        columns[:, 3],
        columns[:, 4],
        columns[:, 5],
    )


def solution(mesh):
    matrix = P("dp", "tensor")
    vector = P(("dp", "tensor"))
    rows = P("dp", "tensor", None)
    return jax.shard_map(
        shards,
        mesh=mesh,
        in_specs=(rows, P("dp", None)) + (matrix,) * 6 + (vector,) * 9 + (rows,),
        out_specs=(rows, rows) + (matrix,) * 6 + (vector,) * 9,
        check_vma=False,
    )
```

```python
import jax
import jax.numpy as jnp
from jax import lax
from jax.sharding import PartitionSpec as P

HEAD_DIM = 64


NORM_EPSILON = 1e-12
MASKED_SCORE = -1000000000.0
ROOT_HALF = 0.7071067811865476
INV_ROOT_TAU = 0.3989422804014327
LOW = jnp.bfloat16
FULL = jnp.float32


def contract(left, right, left_dim, right_dim):
    return lax.dot_general(
        left, right, (((left_dim,), (right_dim,)), ((), ())), preferred_element_type=jnp.float32
    )


def gelu_exact(values):
    return 0.5 * values * (1.0 + lax.erf(values * ROOT_HALF))


def gelu_slope(values):
    return (
        0.5 * (1.0 + lax.erf(values * ROOT_HALF))
        + values * jnp.exp(-0.5 * values * values) * INV_ROOT_TAU
    )


def norm_forward(values, gain, shift):
    center = values - jnp.mean(values, axis=-1, keepdims=True)
    scale_inv = lax.rsqrt(jnp.mean(center * center, axis=-1, keepdims=True) + NORM_EPSILON)
    normed = center * scale_inv
    return (normed * gain + shift, normed, scale_inv)


def norm_backward(upstream, normed, scale_inv, gain):
    scaled = upstream * gain
    return scale_inv * (
        scaled
        - jnp.mean(scaled, axis=-1, keepdims=True)
        - normed * jnp.mean(scaled * normed, axis=-1, keepdims=True)
    )


def swap(values, mask):
    return lax.ppermute(values, "tensor", [(i, i ^ mask) for i in range(4)])


def after(values, *others):
    return lax.optimization_barrier((values, *others))[0]


def spread(block):
    count = lax.axis_size("dp")
    stacked = jnp.broadcast_to(block[None], (count, *block.shape))
    return lax.all_to_all(stacked, "dp", 0, 0, tiled=True).reshape(-1, block.shape[1])


def gathered_sum(values):
    count = lax.axis_size("dp")
    blocks = values.astype(LOW).reshape(count, values.shape[0] // count, values.shape[1])
    got = lax.all_to_all(blocks, "dp", 0, 0, tiled=True)
    return got


def halves(values):
    high = lax.reduce_precision(values, 8, 7)
    return (high.astype(LOW), (values - high).astype(LOW))


def core_sum(part):
    half = part.shape[0] // 2
    got = swap(part[half:].astype(LOW), 1)
    return part[:half] + got.astype(FULL)


def far_sum(total):
    quarter = total.shape[0] // 2
    sent = total.astype(LOW)
    sent = jnp.concatenate([sent[quarter:], sent[:quarter]], axis=0)
    return swap(sent, 2)


def core_join(rows):
    return jnp.concatenate([rows, swap(rows, 1)], axis=0)


def ordered_segments(segment_row, my_index):
    quarters = segment_row.reshape(4, -1)
    core = my_index % 2 == 1
    quarters = jnp.where(core, quarters[jnp.array([1, 0, 3, 2])], quarters)
    far = my_index // 2 == 1
    quarters = jnp.where(far, quarters[jnp.array([2, 3, 0, 1])], quarters)
    return jnp.concatenate([quarters[0], quarters[2], quarters[1], quarters[3]])


def attend_forward(qkv_rows, same_doc, head_count, head_cols):
    outputs = []
    kept = []
    for head in range(head_count):
        offset = head * HEAD_DIM
        query = qkv_rows[:, offset : offset + HEAD_DIM]
        key = qkv_rows[:, head_cols + offset : head_cols + offset + HEAD_DIM]
        value = qkv_rows[:, 2 * head_cols + offset : 2 * head_cols + offset + HEAD_DIM]
        scores = jnp.where(
            same_doc, HEAD_DIM ** (-0.5) * contract(query, key, 1, 1), MASKED_SCORE
        )
        highest = jnp.max(scores, axis=-1, keepdims=True)
        shifted = jnp.exp(scores - highest)
        row_total = jnp.sum(shifted, axis=-1, keepdims=True)
        probs_low = (shifted / row_total).astype(LOW)
        outputs.append(jnp.dot(probs_low, value, preferred_element_type=FULL))
        kept.append(highest + jnp.log(row_total))
    return (jnp.concatenate(outputs, axis=1).astype(LOW), kept)


def attend_backward(qkv_rows, same_doc, kept, grad_rows, head_count, head_cols):
    query_grads = []
    key_grads = []
    value_grads = []
    for head in range(head_count):
        offset = head * HEAD_DIM
        query = qkv_rows[:, offset : offset + HEAD_DIM]
        key = qkv_rows[:, head_cols + offset : head_cols + offset + HEAD_DIM]
        value = qkv_rows[:, 2 * head_cols + offset : 2 * head_cols + offset + HEAD_DIM]
        scores = jnp.where(
            same_doc, HEAD_DIM ** (-0.5) * contract(query, key, 1, 1), MASKED_SCORE
        )
        probs = jnp.exp(scores - kept[head])
        grad_head = grad_rows[:, offset : offset + HEAD_DIM]
        value_grads.append(contract(probs.astype(LOW), grad_head, 0, 0))
        probs_grad = contract(grad_head, value, 1, 1)
        scores_grad = probs * (probs_grad - jnp.sum(probs * probs_grad, axis=-1, keepdims=True))
        scores_low = scores_grad.astype(LOW)
        query_grads.append(
            HEAD_DIM ** (-0.5) * jnp.dot(scores_low, key, preferred_element_type=FULL)
        )
        key_grads.append(HEAD_DIM ** (-0.5) * contract(scores_low, query, 0, 0))
    return jnp.concatenate(query_grads + key_grads + value_grads, axis=1).astype(LOW)


def shards(
    tokens,
    segments,
    q_weight,
    k_weight,
    v_weight,
    up_weight,
    out_weight,
    down_weight,
    q_bias,
    v_bias,
    out_bias,
    up_bias,
    down_bias,
    norm1_gain,
    norm1_shift,
    norm2_gain,
    norm2_shift,
    cotangent,
):
    my_index = lax.axis_index("tensor")
    local_len, width = tokens.shape[1:]
    head_cols = q_weight.shape[1]
    head_count = head_cols // HEAD_DIM
    tokens = tokens[0]
    cotangent = cotangent[0]

    vector_rows = q_bias.shape[0]
    columns = jnp.stack(
        [q_bias, v_bias, out_bias, down_bias, norm1_gain, norm1_shift, norm2_gain, norm2_shift],
        axis=1,
    )
    columns = jnp.concatenate([columns, up_bias.reshape(vector_rows, 4)], axis=1)
    column_count = columns.shape[1]
    high, low = halves(columns)
    packed = jnp.pad(
        jnp.concatenate([high, low], axis=1), ((0, 2), (0, 128 - 2 * column_count))
    )
    first_full = spread(jnp.concatenate([q_weight, k_weight, v_weight, out_weight], axis=1))
    near = [packed] + [swap(packed, mask) for mask in (1, 2, 3)]
    tokens_far = swap(tokens, 2)

    near = [block[:vector_rows] for block in near]
    core = my_index % 2 == 1
    near = [
        jnp.where(core, near[1], near[0]),
        jnp.where(core, near[0], near[1]),
        jnp.where(core, near[3], near[2]),
        jnp.where(core, near[2], near[3]),
    ]
    far = my_index // 2 == 1
    near = jnp.concatenate(
        [
            jnp.where(far, near[2], near[0]),
            jnp.where(far, near[3], near[1]),
            jnp.where(far, near[0], near[2]),
            jnp.where(far, near[1], near[3]),
        ],
        axis=0,
    )
    vectors = spread(near)
    tokens_pair = jnp.concatenate([tokens, tokens_far], axis=0)
    tokens_full = core_join(tokens_pair)
    cotangent_far = swap(after(cotangent, tokens_far), 2)
    second_full = spread(
        after(jnp.concatenate([up_weight, down_weight], axis=1), near, tokens_far)
    )
    first_full, vectors, tokens_full, cotangent_far = lax.optimization_barrier(
        (first_full, vectors, tokens_full, cotangent_far)
    )
    hidden_cols = up_weight.shape[1]
    up_full, down_full = second_full[:, :hidden_cols], second_full[:, hidden_cols:]
    qkv_weight = first_full[:, : 3 * head_cols]
    out_full = first_full[:, 3 * head_cols : 4 * head_cols]
    vectors = vectors.astype(FULL)
    vectors = vectors[:, :column_count] + vectors[:, column_count : 2 * column_count]
    rows = vectors[:, :8].T
    gain_first, shift_first, gain_second, shift_second = rows[4], rows[5], rows[6], rows[7]
    bias_out, bias_down = rows[2], rows[3]
    own = lax.dynamic_slice_in_dim(vectors, my_index * head_cols, head_cols, axis=0)
    bias_up = own[:, 8:12].reshape(-1)
    qkv_bias = jnp.concatenate([own[:, 0], jnp.zeros((head_cols,), FULL), own[:, 1]])

    segment_row = ordered_segments(segments[0], my_index)
    same_doc = segment_row[:, None] == segment_row[None, :]
    qkv_rows = (jnp.dot(tokens_full, qkv_weight, preferred_element_type=FULL) + qkv_bias).astype(
        LOW
    )
    mixed_rows, kept = attend_forward(qkv_rows, same_doc, head_count, head_cols)
    attn_chip = core_sum(contract(mixed_rows, out_full, 1, 1))
    attn_far = far_sum(attn_chip)
    first, normed_first, inv_first = norm_forward(
        tokens_pair.astype(FULL) + (attn_chip + attn_far.astype(FULL)) + bias_out,
        gain_first,
        shift_first,
    )
    hidden_full = core_join(first.astype(LOW))
    upward = jnp.dot(hidden_full, up_full, preferred_element_type=FULL) + bias_up
    active = gelu_exact(upward).astype(LOW)
    branch_chip = core_sum(contract(active, down_full, 1, 1))
    branch = branch_chip + far_sum(branch_chip).astype(FULL)
    layer_output, normed_second, inv_second = norm_forward(
        first + branch + bias_down, gain_second, shift_second
    )

    cotangent_pair = jnp.concatenate([cotangent, cotangent_far], axis=0).astype(FULL)
    second_grad = norm_backward(cotangent_pair, normed_second, inv_second, gain_second)
    cotangent_own = cotangent_pair[:local_len]
    grad_gain_second = jnp.sum(cotangent_own * normed_second[:local_len], axis=0)
    grad_shift_second = jnp.sum(cotangent_own, axis=0)
    branch_low = second_grad.astype(LOW)
    grad_bias_down = jnp.sum(branch_low[:local_len].astype(FULL), axis=0)
    branch_full = core_join(branch_low)
    active_grad = jnp.dot(branch_full, down_full, preferred_element_type=FULL)
    upward_grad = (active_grad * gelu_slope(upward)).astype(LOW)
    hidden_chip = core_sum(contract(upward_grad, up_full, 1, 1))
    hidden_far = far_sum(hidden_chip)
    grad_down = contract(branch_full, active, 0, 0)
    grad_up = contract(hidden_full, upward_grad, 0, 0)
    grad_bias_up = jnp.sum(upward_grad.astype(FULL), axis=0)
    pair_blocks = gathered_sum(
        jnp.concatenate(
            [after(grad_up, hidden_chip).astype(LOW), after(grad_down, hidden_chip).astype(LOW)],
            axis=1,
        )
    )
    first_grad = second_grad + (hidden_chip + hidden_far.astype(FULL))
    resid_grad = norm_backward(first_grad, normed_first, inv_first, gain_first)
    first_own = first_grad[:local_len]
    grad_gain_first = jnp.sum(first_own * normed_first[:local_len], axis=0)
    grad_shift_first = jnp.sum(first_own, axis=0)
    attended_low = resid_grad.astype(LOW)
    grad_bias_out = jnp.sum(attended_low[:local_len].astype(FULL), axis=0)
    attended_full = core_join(attended_low)
    mixed_grad = jnp.dot(attended_full, out_full, preferred_element_type=FULL).astype(LOW)
    qkv_grad = attend_backward(qkv_rows, same_doc, kept, mixed_grad, head_count, head_cols)

    grad_bias_query = jnp.sum(qkv_grad[:, :head_cols].astype(FULL), axis=0)
    grad_bias_value = jnp.sum(qkv_grad[:, 2 * head_cols :].astype(FULL), axis=0)
    sharded = jnp.concatenate(
        [grad_bias_query[None], grad_bias_value[None], grad_bias_up.reshape(head_cols, 4).T], axis=0
    )
    sharded = lax.dynamic_update_slice_in_dim(
        jnp.zeros((6, width), FULL), sharded, my_index * head_cols, 1
    )
    vector_sums = jnp.concatenate(
        [
            grad_bias_out[None],
            grad_bias_down[None],
            grad_gain_first[None],
            grad_shift_first[None],
            grad_gain_second[None],
            grad_shift_second[None],
            sharded,
        ],
        axis=0,
    )
    vector_near = [swap(vector_sums, mask) for mask in (1, 2, 3)]
    input_chip = core_sum(contract(qkv_grad, qkv_weight, 1, 1))
    input_far = swap(input_chip[local_len:].astype(LOW), 2)
    vector_sums = vector_sums + vector_near[0] + vector_near[1] + vector_near[2]
    grad_qkv = contract(tokens_full, qkv_grad, 0, 0)
    grad_out = contract(attended_full, mixed_rows, 0, 0)
    high, low = halves(vector_sums.T)
    last_block = jnp.concatenate(
        [
            grad_qkv.astype(LOW),
            grad_out.astype(LOW),
            high,
            low,
            jnp.zeros((width, 128 - 2 * column_count), LOW),
        ],
        axis=1,
    )
    last_blocks = gathered_sum(last_block)
    input_grad = resid_grad[:local_len] + (input_chip[:local_len] + input_far.astype(FULL))

    pair_sum = jnp.sum(pair_blocks.astype(FULL), axis=0)
    up_sum, down_sum = pair_sum[:, :hidden_cols], pair_sum[:, hidden_cols:]
    last_sum = jnp.sum(last_blocks.astype(FULL), axis=0)
    columns = last_sum[:, 4 * head_cols :]
    columns = columns[:, :column_count] + columns[:, column_count : 2 * column_count]
    columns = lax.dynamic_slice_in_dim(columns, my_index * vector_rows, vector_rows, axis=0)
    return (
        layer_output[:local_len].astype(LOW)[None],
        input_grad[None],
        last_sum[:, :head_cols],
        last_sum[:, head_cols : 2 * head_cols],
        last_sum[:, 2 * head_cols : 3 * head_cols],
        up_sum,
        last_sum[:, 3 * head_cols : 4 * head_cols],
        down_sum,
        columns[:, 6],
        columns[:, 7],
        columns[:, 0],
        columns[:, 8:12].reshape(-1),
        columns[:, 1],
        columns[:, 2],
        columns[:, 3],
        columns[:, 4],
        columns[:, 5],
    )


def solution(mesh):
    matrix = P("dp", "tensor")
    vector = P(("dp", "tensor"))
    rows = P("dp", "tensor", None)
    return jax.shard_map(
        shards,
        mesh=mesh,
        in_specs=(rows, P("dp", None)) + (matrix,) * 6 + (vector,) * 9 + (rows,),
        out_specs=(rows, rows) + (matrix,) * 6 + (vector,) * 9,
        check_vma=False,
    )
```

```python
import functools

import jax
import jax.numpy as jnp
import numpy as np
from jax import lax
from jax.experimental import pallas as pl
from jax.experimental.pallas import tpu as pltpu
from jax.sharding import PartitionSpec as P

HEAD_DIM = 64
TILE = 128
GROUP = 256


NORM_EPSILON = 1e-12
MASKED_SCORE = -1000000000.0
ROOT_HALF = 0.7071067811865476
INV_ROOT_TAU = 0.3989422804014327
LOW = jnp.bfloat16
FULL = jnp.float32
VMEM_LIMIT = 48 * 1024 * 1024


def contract(left, right, left_dim, right_dim):
    return lax.dot_general(
        left, right, (((left_dim,), (right_dim,)), ((), ())), preferred_element_type=jnp.float32
    )


def gelu_exact(values):
    return 0.5 * values * (1.0 + lax.erf(values * ROOT_HALF))


def gelu_slope(values):
    return (
        0.5 * (1.0 + lax.erf(values * ROOT_HALF))
        + values * jnp.exp(-0.5 * values * values) * INV_ROOT_TAU
    )


def norm_forward(values, gain, shift):
    center = values - jnp.mean(values, axis=-1, keepdims=True)
    scale_inv = lax.rsqrt(jnp.mean(center * center, axis=-1, keepdims=True) + NORM_EPSILON)
    normed = center * scale_inv
    return (normed * gain + shift, normed, scale_inv)


def norm_backward(upstream, normed, scale_inv, gain):
    scaled = upstream * gain
    return scale_inv * (
        scaled
        - jnp.mean(scaled, axis=-1, keepdims=True)
        - normed * jnp.mean(scaled * normed, axis=-1, keepdims=True)
    )


def swap(values, mask):
    return lax.ppermute(values, "tensor", [(i, i ^ mask) for i in range(4)])


def after(values, *others):
    return lax.optimization_barrier((values, *others))[0]


def spread(block):
    count = lax.axis_size("dp")
    stacked = jnp.broadcast_to(block[None], (count, *block.shape))
    return lax.all_to_all(stacked, "dp", 0, 0, tiled=True).reshape(-1, block.shape[1])


def scattered(values):
    count = lax.axis_size("dp")
    blocks = values.reshape(count, values.shape[0] // count, values.shape[1])
    return lax.all_to_all(blocks, "dp", 0, 0, tiled=True)


def halves(values):
    high = lax.reduce_precision(values, 8, 7)
    return (high.astype(LOW), (values - high).astype(LOW))


def core_sum(part):
    half = part.shape[0] // 2
    got = swap(part[half:].astype(LOW), 1)
    return part[:half] + got.astype(FULL)


def far_sum(total):
    quarter = total.shape[0] // 2
    sent = total.astype(LOW)
    sent = jnp.concatenate([sent[quarter:], sent[:quarter]], axis=0)
    return swap(sent, 2)


def core_join(rows):
    return jnp.concatenate([rows, swap(rows, 1)], axis=0)


def ordered_segments(segment_row, my_index):
    quarters = segment_row.reshape(4, -1)
    core = my_index % 2 == 1
    quarters = jnp.where(core, quarters[jnp.array([1, 0, 3, 2])], quarters)
    far = my_index // 2 == 1
    quarters = jnp.where(far, quarters[jnp.array([2, 3, 0, 1])], quarters)
    return jnp.concatenate([quarters[0], quarters[2], quarters[1], quarters[3]])


def call(body, out_shapes, *operands, smem=0):
    specs = [pl.BlockSpec(memory_space=pltpu.SMEM)] * smem
    specs += [pl.BlockSpec(memory_space=pltpu.VMEM)] * (len(operands) - smem)
    return pl.pallas_call(
        body,
        out_shape=[jax.ShapeDtypeStruct(shape, kind) for shape, kind in out_shapes],
        in_specs=specs,
        out_specs=[pl.BlockSpec(memory_space=pltpu.VMEM)] * len(out_shapes),
        compiler_params=pltpu.CompilerParams(vmem_limit_bytes=VMEM_LIMIT),
        cost_estimate=pl.CostEstimate(flops=1000, bytes_accessed=1000, transcendentals=0),
    )(*operands)


def lanes(shape, dim=1):
    return lax.broadcasted_iota(jnp.int32, shape, dim)


def head_tile(head):
    return head // 2


def head_mask(head, shape, dim=1):
    index = lanes(shape, dim)
    return index >= HEAD_DIM if head % 2 else index < HEAD_DIM


def only(values, mask):
    return jnp.where(mask, values, jnp.zeros_like(values))


def packed_out(weight_ref):
    rows = weight_ref.shape[0]
    parts = [
        weight_ref[:, GROUP * i + TILE : GROUP * (i + 1)].astype(FULL) for i in range(3)
    ]
    low = head_mask(0, (rows, TILE))
    first = jnp.where(low, pltpu.roll(parts[0], HEAD_DIM, 1), parts[1])
    second = jnp.where(low, pltpu.roll(parts[2], HEAD_DIM, 1), 0.0)
    return jnp.concatenate([first, second], axis=1).astype(LOW)


def lined_heads(rows):
    first, second = rows[:, :TILE], rows[:, TILE:]
    return [pltpu.roll(first, HEAD_DIM, 1), first, pltpu.roll(second, HEAD_DIM, 1)]


def transposed(values):
    return jnp.transpose(values.astype(FULL))


def expand_matrix(count):
    shape = (count, 4 * count)
    return jnp.where(lanes(shape) // 4 == lanes(shape, 0), 1.0, 0.0).astype(LOW)


def forward_kernel(
    index_ref,
    near_ref,
    other_ref,
    weight_ref,
    segment_ref,
    qkv_ref,
    mixed_ref,
    log_ref,
    send_ref,
    keep_ref,
    vector_ref,
    up_bias_ref,
):
    index = index_ref[0]
    half = near_ref.shape[0]
    columns = 3 * HEAD_DIM
    width = weight_ref.shape[0]
    held = weight_ref[:, 3 * GROUP :].astype(FULL)
    flat = jnp.transpose(held)
    vector_ref[...] = flat[:8] + flat[12:20]
    own = weight_ref[pl.ds(pl.multiple_of(index * columns, 64), columns), 3 * GROUP :].astype(FULL)
    own = jnp.concatenate([own, jnp.zeros((GROUP - columns, TILE), FULL)], axis=0)
    own = jnp.transpose(own)
    expand = expand_matrix(columns)
    wide = jnp.dot(own[:24, :].astype(LOW)[:, :GROUP], jnp.concatenate(
        [expand, jnp.zeros((GROUP - columns, 4 * columns), LOW)], axis=0
    ), preferred_element_type=FULL)
    up_bias = jnp.zeros((1, 4 * columns), FULL)
    place = lanes((1, 4 * columns)) % 4
    for step in range(4):
        row = wide[8 + step : 9 + step] + wide[20 + step : 21 + step]
        up_bias = jnp.where(place == step, row, up_bias)
    up_bias_ref[...] = up_bias
    bias = jnp.concatenate(
        [
            own[0:1] + own[12:13],
            jnp.zeros((1, GROUP), FULL),
            own[1:2] + own[13:14],
        ],
        axis=1,
    )
    keep = lanes((1, 3 * GROUP)) % GROUP < columns
    for at, rows_ref in ((0, near_ref), (half, other_ref)):
        got = jnp.dot(rows_ref[...], weight_ref[:, : 3 * GROUP], preferred_element_type=FULL)
        qkv_ref[at : at + half, :] = jnp.where(keep, got + bias, 0.0).astype(LOW)

    length = 2 * half
    row_segments = segment_ref[...]
    column_segments = jnp.transpose(
        jnp.broadcast_to(row_segments.astype(FULL), (TILE, length))
    )[:, :1].astype(jnp.int32)
    same = column_segments == row_segments
    mixed_tiles = [None, None]
    for head in range(3):
        at = TILE * head_tile(head)
        mask = head_mask(head, (length, TILE))
        key = only(qkv_ref[:, GROUP + at : GROUP + at + TILE], mask) * jnp.asarray(0.125, LOW)
        scores = contract(key, qkv_ref[:, at : at + TILE], 1, 1)
        scores = jnp.where(same, scores, MASKED_SCORE)
        highest = jnp.max(scores, axis=0, keepdims=True)
        shifted = jnp.exp(scores - highest)
        total = jnp.sum(shifted, axis=0, keepdims=True)
        probs = (shifted * (1.0 / total)).astype(LOW)
        log_ref[head : head + 1, :] = highest + jnp.log(total)
        value = only(qkv_ref[:, 2 * GROUP + at : 2 * GROUP + at + TILE], mask)
        got = jnp.dot(transposed(value).astype(LOW), probs, preferred_element_type=FULL)
        tile = head_tile(head)
        mixed_tiles[tile] = got if mixed_tiles[tile] is None else mixed_tiles[tile] + got
    log_ref[3:, :] = jnp.zeros((5, length), FULL)
    for tile in range(2):
        mixed_ref[:, TILE * tile : TILE * (tile + 1)] = jnp.transpose(mixed_tiles[tile]).astype(LOW)
    out = packed_out(weight_ref)
    keep_ref[...] = contract(mixed_ref[:half, :], out, 1, 1)
    send_ref[...] = contract(mixed_ref[half:, :], out, 1, 1).astype(LOW)


def backward_kernel(
    index_ref,
    near_ref,
    other_ref,
    qkv_ref,
    log_ref,
    weight_ref,
    segment_ref,
    sums_ref,
    up_sum_ref,
    grad_ref,
    send_ref,
    keep_ref,
    vector_ref,
    mixed_grad,
    key_grad,
    value_grad,
    columns_held,
):
    index = index_ref[0]
    half = near_ref.shape[0]
    length = 2 * half
    columns = 3 * HEAD_DIM
    out = packed_out(weight_ref)
    mixed_grad[:half, :] = jnp.dot(near_ref[...], out, preferred_element_type=FULL).astype(LOW)
    mixed_grad[half:, :] = jnp.dot(other_ref[...], out, preferred_element_type=FULL).astype(LOW)
    row_segments = segment_ref[...]
    column_segments = jnp.transpose(
        jnp.broadcast_to(row_segments.astype(FULL), (TILE, length))
    )[:, :1].astype(jnp.int32)
    same = column_segments == row_segments
    sums = []
    for tile in range(2):
        at = TILE * tile
        query_grad = jnp.zeros((TILE, length), FULL)
        for head in (0, 1) if tile == 0 else (2,):
            mask = head_mask(head, (length, TILE))
            scale = jnp.asarray(0.125, LOW)
            key = only(qkv_ref[:, GROUP + at : GROUP + at + TILE], mask) * scale
            query = only(qkv_ref[:, at : at + TILE], mask)
            value = only(qkv_ref[:, 2 * GROUP + at : 2 * GROUP + at + TILE], mask)
            grad = only(mixed_grad[:, at : at + TILE], mask)
            scores = contract(key, query, 1, 1)
            probs = jnp.exp(
                jnp.where(same, scores, MASKED_SCORE) - log_ref[head : head + 1, :]
            )
            probs_grad = contract(value, grad, 1, 1)
            inner = jnp.sum(probs * probs_grad, axis=0, keepdims=True)
            scores_grad = (probs * (probs_grad - inner)).astype(LOW)
            got = jnp.dot(probs.astype(LOW), grad, preferred_element_type=FULL)
            got_key = jnp.dot(scores_grad, query * scale, preferred_element_type=FULL)
            if head % 2 == 0:
                value_grad[...] = got
                key_grad[...] = got_key
            else:
                value_grad[...] += got
                key_grad[...] += got_key
            query_grad += jnp.dot(
                transposed(key).astype(LOW), scores_grad, preferred_element_type=FULL
            )
        query_low = jnp.transpose(query_grad).astype(LOW)
        value_low = value_grad[...].astype(LOW)
        grad_ref[:, at : at + TILE] = query_low
        grad_ref[:, GROUP + at : GROUP + at + TILE] = key_grad[...].astype(LOW)
        grad_ref[:, 2 * GROUP + at : 2 * GROUP + at + TILE] = value_low
        sums.append(
            (
                jnp.sum(query_low.astype(FULL), axis=0, keepdims=True),
                jnp.sum(value_low.astype(FULL), axis=0, keepdims=True),
            )
        )
    wide = weight_ref[:, : 3 * GROUP]
    keep_ref[...] = contract(grad_ref[:half, :], wide, 1, 1)
    send_ref[...] = contract(grad_ref[half:, :], wide, 1, 1).astype(LOW)

    up_row = up_sum_ref[...]
    place = lanes((8, 4 * columns))
    spaced = jnp.where(place % 4 == lanes((8, 4 * columns), 0), up_row, 0.0)
    high = spaced.astype(LOW)
    low = (spaced - high.astype(FULL)).astype(LOW)
    expand = expand_matrix(columns)
    up_rows = contract(high, expand, 1, 1) + contract(low, expand, 1, 1)
    up_rows = jnp.concatenate([up_rows, jnp.zeros((8, GROUP - columns), FULL)], axis=1)
    query_sum = jnp.concatenate([sums[0][0], sums[1][0]], axis=1)
    value_sum = jnp.concatenate([sums[0][1], sums[1][1]], axis=1)
    at_row = lanes((8, GROUP), 0)
    late = jnp.where(at_row == 6, query_sum, jnp.where(at_row == 7, value_sum, 0.0))
    stacked = jnp.concatenate([late, up_rows, jnp.zeros((TILE - 16, GROUP), FULL)], axis=0)
    columns_held[...] = jnp.zeros_like(columns_held)
    columns_held[pl.ds(pl.multiple_of(index * columns, 64), columns), :] = jnp.transpose(stacked)[
        :columns
    ]
    placed = jnp.transpose(columns_held[...])[:16]
    given = sums_ref[...]
    vector_ref[:8, :] = placed[:8] + given
    vector_ref[8:, :] = placed[8:]


def weights_kernel(tokens_near, tokens_other, near_ref, other_ref, grad_ref, mixed_ref, out_ref):
    half = near_ref.shape[0]
    width = near_ref.shape[1]
    got = contract(tokens_near[...], grad_ref[:half, :], 0, 0) + contract(
        tokens_other[...], grad_ref[half:, :], 0, 0
    )
    out_grad = contract(near_ref[...], mixed_ref[:half, :], 0, 0) + contract(
        other_ref[...], mixed_ref[half:, :], 0, 0
    )
    high = head_mask(1, (width, TILE))
    for part, lined in enumerate(lined_heads(out_grad)):
        at = GROUP * part
        out_ref[:, at : at + TILE] = got[:, at : at + TILE].astype(LOW)
        out_ref[:, at + TILE : at + GROUP] = jnp.where(
            high, lined, got[:, at + TILE : at + GROUP]
        ).astype(LOW)
    out_ref[:, 3 * GROUP :] = jnp.zeros((width, TILE), LOW)


def packing(vector_rows):
    place = np.arange(12 * vector_rows)
    many = 8 * vector_rows
    row = np.where(place < many, place % vector_rows, (place - many) // 4)
    column = np.where(place < many, place // vector_rows, 8 + (place - many) % 4)
    rows = (row[None, :] == np.arange(vector_rows)[:, None]).astype(np.float32)
    columns = (column[:, None] == np.arange(12)[None, :]).astype(np.float32)
    return (rows, columns)


def shards(
    tokens,
    segments,
    q_weight,
    k_weight,
    v_weight,
    up_weight,
    out_weight,
    down_weight,
    q_bias,
    v_bias,
    out_bias,
    up_bias,
    down_bias,
    norm1_gain,
    norm1_shift,
    norm2_gain,
    norm2_shift,
    cotangent,
):
    my_index = lax.axis_index("tensor")
    local_len, width = tokens.shape[1:]
    half = 2 * local_len
    length = 4 * local_len
    head_cols = q_weight.shape[1]
    hidden_cols = up_weight.shape[1]
    tokens = tokens[0]
    cotangent = cotangent[0]
    index = my_index.reshape(1)

    vector_rows = q_bias.shape[0]
    row_place, column_place = packing(vector_rows)
    flat = jnp.concatenate(
        [
            q_bias,
            v_bias,
            out_bias,
            down_bias,
            norm1_gain,
            norm1_shift,
            norm2_gain,
            norm2_shift,
            up_bias,
        ]
    )
    high, low = halves(flat)
    spaced = jnp.concatenate([high * row_place.astype(LOW), low * row_place.astype(LOW)], axis=1)
    spaced = jnp.pad(spaced, ((0, 2), (0, 0)))
    select = np.zeros((2 * flat.shape[0], TILE), np.float32)
    select[: flat.shape[0], :12] = column_place
    select[flat.shape[0] :, 12:24] = column_place
    packed = jnp.dot(spaced, select.astype(LOW), preferred_element_type=FULL).astype(LOW)
    near = [packed] + [swap(packed, mask) for mask in (1, 2, 3)]
    tokens_far = swap(tokens, 2)
    near = [block[:vector_rows] for block in near]
    core = my_index % 2 == 1
    near = [
        jnp.where(core, near[1], near[0]),
        jnp.where(core, near[0], near[1]),
        jnp.where(core, near[3], near[2]),
        jnp.where(core, near[2], near[3]),
    ]
    far = my_index // 2 == 1
    near = jnp.concatenate(
        [
            jnp.where(far, near[2], near[0]),
            jnp.where(far, near[3], near[1]),
            jnp.where(far, near[0], near[2]),
            jnp.where(far, near[1], near[3]),
        ],
        axis=0,
    )
    pads = [out_weight[:, HEAD_DIM * i : HEAD_DIM * (i + 1)] for i in range(3)]
    first_block = jnp.concatenate(
        [q_weight, pads[0], k_weight, pads[1], v_weight, pads[2], near], axis=1
    )
    first_full = spread(first_block)
    tokens_pair = jnp.concatenate([tokens, tokens_far], axis=0)
    tokens_core = swap(tokens_pair, 1)
    cotangent_far = swap(after(cotangent, tokens_far), 2)
    segment_row = ordered_segments(segments[0], my_index)[None]
    second_block = jnp.concatenate([up_weight, down_weight], axis=1)
    first_full, second_block, tokens_core, cotangent_far, segment_row = lax.optimization_barrier(
        (first_full, second_block, tokens_core, cotangent_far, segment_row)
    )
    second_full = spread(second_block)
    up_full, down_full = second_full[:, :hidden_cols], second_full[:, hidden_cols:]

    qkv_rows, mixed_rows, log_totals, attn_send, attn_keep, rows, bias_up = call(
        forward_kernel,
        [
            ((length, 3 * GROUP), LOW),
            ((length, GROUP), LOW),
            ((8, length), FULL),
            ((half, width), LOW),
            ((half, width), FULL),
            ((8, width), FULL),
            ((1, hidden_cols), FULL),
        ],
        index,
        tokens_pair,
        tokens_core,
        first_full,
        segment_row,
        smem=1,
    )
    gain_first, shift_first, gain_second, shift_second = rows[4], rows[5], rows[6], rows[7]
    bias_out, bias_down = rows[2], rows[3]
    attn_chip = attn_keep + swap(attn_send, 1).astype(FULL)
    attn_far = far_sum(attn_chip)
    first, normed_first, inv_first = norm_forward(
        tokens_pair.astype(FULL) + (attn_chip + attn_far.astype(FULL)) + bias_out,
        gain_first,
        shift_first,
    )
    hidden_full = core_join(first.astype(LOW))
    upward = jnp.dot(hidden_full, up_full, preferred_element_type=FULL) + bias_up
    active = gelu_exact(upward).astype(LOW)
    branch_chip = core_sum(contract(active, down_full, 1, 1))
    branch = branch_chip + far_sum(branch_chip).astype(FULL)
    layer_output, normed_second, inv_second = norm_forward(
        first + branch + bias_down, gain_second, shift_second
    )

    cotangent_pair = jnp.concatenate([cotangent, cotangent_far], axis=0).astype(FULL)
    second_grad = norm_backward(cotangent_pair, normed_second, inv_second, gain_second)
    cotangent_own = cotangent_pair[:local_len]
    grad_gain_second = jnp.sum(cotangent_own * normed_second[:local_len], axis=0)
    grad_shift_second = jnp.sum(cotangent_own, axis=0)
    branch_low = second_grad.astype(LOW)
    grad_bias_down = jnp.sum(branch_low[:local_len].astype(FULL), axis=0)
    branch_full = core_join(branch_low)
    active_grad = jnp.dot(branch_full, down_full, preferred_element_type=FULL)
    upward_grad = (active_grad * gelu_slope(upward)).astype(LOW)
    hidden_chip = core_sum(contract(upward_grad, up_full, 1, 1))
    hidden_far = far_sum(hidden_chip)
    grad_down = contract(branch_full, active, 0, 0)
    grad_up = contract(hidden_full, upward_grad, 0, 0)
    grad_bias_up = jnp.sum(upward_grad.astype(FULL), axis=0)
    pair_blocks = scattered(
        jnp.concatenate(
            [after(grad_up, hidden_chip).astype(LOW), after(grad_down, hidden_chip).astype(LOW)],
            axis=1,
        )
    )
    first_grad = second_grad + (hidden_chip + hidden_far.astype(FULL))
    resid_grad = norm_backward(first_grad, normed_first, inv_first, gain_first)
    first_own = first_grad[:local_len]
    grad_gain_first = jnp.sum(first_own * normed_first[:local_len], axis=0)
    grad_shift_first = jnp.sum(first_own, axis=0)
    attended_low = resid_grad.astype(LOW)
    grad_bias_out = jnp.sum(attended_low[:local_len].astype(FULL), axis=0)
    attended_core = swap(attended_low, 1)
    zero_row = jnp.zeros((width,), FULL)
    given = jnp.stack(
        [
            grad_bias_out,
            grad_bias_down,
            grad_gain_first,
            grad_shift_first,
            grad_gain_second,
            grad_shift_second,
            zero_row,
            zero_row,
        ]
    )
    qkv_grad, input_send, input_keep, vector_sums = pl.pallas_call(
        backward_kernel,
        out_shape=[
            jax.ShapeDtypeStruct((length, 3 * GROUP), LOW),
            jax.ShapeDtypeStruct((half, width), LOW),
            jax.ShapeDtypeStruct((half, width), FULL),
            jax.ShapeDtypeStruct((16, width), FULL),
        ],
        in_specs=[pl.BlockSpec(memory_space=pltpu.SMEM)]
        + [pl.BlockSpec(memory_space=pltpu.VMEM)] * 8,
        out_specs=[pl.BlockSpec(memory_space=pltpu.VMEM)] * 4,
        scratch_shapes=[
            pltpu.VMEM((length, GROUP), LOW),
            pltpu.VMEM((length, TILE), FULL),
            pltpu.VMEM((length, TILE), FULL),
            pltpu.VMEM((width, TILE), FULL),
        ],
        compiler_params=pltpu.CompilerParams(vmem_limit_bytes=VMEM_LIMIT),
        cost_estimate=pl.CostEstimate(flops=1000, bytes_accessed=1000, transcendentals=0),
    )(
        index,
        attended_low,
        attended_core,
        qkv_rows,
        log_totals,
        first_full,
        segment_row,
        given,
        grad_bias_up[None],
    )
    vector_near = [swap(vector_sums, mask) for mask in (1, 2, 3)]
    input_got = swap(input_send, 1)
    (last_block,) = call(
        weights_kernel,
        [((width, 3 * GROUP + TILE), LOW)],
        tokens_pair,
        tokens_core,
        attended_low,
        attended_core,
        qkv_grad,
        mixed_rows,
    )
    vector_sums = vector_sums + vector_near[0] + vector_near[1] + vector_near[2]
    high, low = halves(vector_sums[:12].T)
    last_block = lax.dynamic_update_slice(
        last_block, jnp.concatenate([high, low], axis=1), (0, 3 * GROUP)
    )
    input_chip = input_keep + input_got.astype(FULL)
    input_far = swap(input_chip[local_len:].astype(LOW), 2)
    last_blocks = scattered(after(last_block, input_chip))
    input_grad = resid_grad[:local_len] + (input_chip[:local_len] + input_far.astype(FULL))

    pair_sum = jnp.sum(pair_blocks.astype(FULL), axis=0)
    up_sum, down_sum = pair_sum[:, :hidden_cols], pair_sum[:, hidden_cols:]
    last_sum = jnp.sum(last_blocks.astype(FULL), axis=0)
    columns = last_sum[:, 3 * GROUP :]
    columns = columns[:, :12] + columns[:, 12:24]
    columns = lax.dynamic_slice_in_dim(columns, my_index * vector_rows, vector_rows, axis=0)
    return (
        layer_output[:local_len].astype(LOW)[None],
        input_grad[None],
        last_sum[:, :head_cols],
        last_sum[:, GROUP : GROUP + head_cols],
        last_sum[:, 2 * GROUP : 2 * GROUP + head_cols],
        up_sum,
        jnp.concatenate(
            [last_sum[:, GROUP * i + head_cols : GROUP * (i + 1)] for i in range(3)], axis=1
        ),
        down_sum,
        columns[:, 6],
        columns[:, 7],
        columns[:, 0],
        columns[:, 8:12].reshape(-1),
        columns[:, 1],
        columns[:, 2],
        columns[:, 3],
        columns[:, 4],
        columns[:, 5],
    )


def solution(mesh):
    matrix = P("dp", "tensor")
    vector = P(("dp", "tensor"))
    rows = P("dp", "tensor", None)
    return jax.shard_map(
        shards,
        mesh=mesh,
        in_specs=(rows, P("dp", None)) + (matrix,) * 6 + (vector,) * 9 + (rows,),
        out_specs=(rows, rows) + (matrix,) * 6 + (vector,) * 9,
        check_vma=False,
    )
```

```python
import functools

import jax
import jax.numpy as jnp
from jax import lax
from jax.experimental import pallas as pl
from jax.experimental.pallas import tpu as pltpu
from jax.sharding import PartitionSpec as P

HEAD_DIM = 64
TILE = 128
GROUP = 256


NORM_EPSILON = 1e-12
MASKED_SCORE = -1000000000.0
ROOT_HALF = 0.7071067811865476
INV_ROOT_TAU = 0.3989422804014327
LOW = jnp.bfloat16
FULL = jnp.float32
VMEM_LIMIT = 48 * 1024 * 1024


def contract(left, right, left_dim, right_dim):
    return lax.dot_general(
        left, right, (((left_dim,), (right_dim,)), ((), ())), preferred_element_type=jnp.float32
    )


def swap(values, mask):
    return lax.ppermute(values, "tensor", [(i, i ^ mask) for i in range(4)])


def after(values, *others):
    return lax.optimization_barrier((values, *others))[0]


def spread(stacked):
    return lax.all_to_all(stacked, "dp", 0, 0, tiled=True)


def plane_groups():
    count = lax.axis_size("dp") // 2
    return [list(range(count)), list(range(count, 2 * count))]


def plane(stacked):
    return lax.all_to_all(stacked, "dp", 0, 0, tiled=True, axis_index_groups=plane_groups())


def side(values):
    count = lax.axis_size("dp")
    pairs = [(i, (i + count // 2) % count) for i in range(count)]
    return lax.ppermute(values, "dp", pairs)


def halves(values):
    high = lax.reduce_precision(values, 8, 7)
    return (high.astype(LOW), (values - high).astype(LOW))


def far_sum(total):
    quarter = total.shape[0] // 2
    sent = total.astype(LOW)
    sent = jnp.concatenate([sent[quarter:], sent[:quarter]], axis=0)
    return swap(sent, 2)


def ordered_segments(segment_row, my_index):
    quarters = segment_row.reshape(4, -1)
    core = my_index % 2 == 1
    quarters = jnp.where(core, quarters[jnp.array([1, 0, 3, 2])], quarters)
    far = my_index // 2 == 1
    quarters = jnp.where(far, quarters[jnp.array([2, 3, 0, 1])], quarters)
    return jnp.concatenate([quarters[0], quarters[2], quarters[1], quarters[3]])


def call(body, out_shapes, *operands, smem=0, scratch=()):
    specs = [pl.BlockSpec(memory_space=pltpu.SMEM)] * smem
    specs += [pl.BlockSpec(memory_space=pltpu.VMEM)] * (len(operands) - smem)
    return pl.pallas_call(
        body,
        out_shape=[jax.ShapeDtypeStruct(shape, kind) for shape, kind in out_shapes],
        in_specs=specs,
        out_specs=[pl.BlockSpec(memory_space=pltpu.VMEM)] * len(out_shapes),
        scratch_shapes=list(scratch),
        compiler_params=pltpu.CompilerParams(vmem_limit_bytes=VMEM_LIMIT),
        cost_estimate=pl.CostEstimate(flops=1000, bytes_accessed=1000, transcendentals=0),
    )(*operands)


def lanes(shape, dim=1):
    return lax.broadcasted_iota(jnp.int32, shape, dim)


def head_tile(head):
    return head // 2


def head_mask(head, shape, dim=1):
    index = lanes(shape, dim)
    return index >= HEAD_DIM if head % 2 else index < HEAD_DIM


def only(values, mask):
    return jnp.where(mask, values, jnp.zeros_like(values))


def packed_out(weight_ref):
    rows = weight_ref.shape[0]
    parts = [
        weight_ref[:, GROUP * i + TILE : GROUP * (i + 1)].astype(FULL) for i in range(3)
    ]
    low = head_mask(0, (rows, TILE))
    first = jnp.where(low, pltpu.roll(parts[0], HEAD_DIM, 1), parts[1])
    second = jnp.where(low, pltpu.roll(parts[2], HEAD_DIM, 1), 0.0)
    return jnp.concatenate([first, second], axis=1).astype(LOW)


def lined_heads(rows):
    first, second = rows[:, :TILE], rows[:, TILE:]
    return [pltpu.roll(first, HEAD_DIM, 1), first, pltpu.roll(second, HEAD_DIM, 1)]


def transposed(values):
    return jnp.transpose(values.astype(FULL))


def expand_matrix(count):
    shape = (count, 4 * count)
    return jnp.where(lanes(shape) // 4 == lanes(shape, 0), 1.0, 0.0).astype(LOW)


def forward_kernel(
    index_ref,
    near_ref,
    other_ref,
    weight_ref,
    segment_ref,
    qkv_ref,
    mixed_ref,
    log_ref,
    send_ref,
    keep_ref,
    vector_ref,
    up_bias_ref,
):
    index = index_ref[0]
    half = near_ref.shape[0]
    columns = 3 * HEAD_DIM
    width = weight_ref.shape[0]
    held = weight_ref[:, 3 * GROUP :].astype(FULL)
    flat = jnp.transpose(held)
    vector_ref[...] = flat[:8] + flat[12:20]
    own = weight_ref[pl.ds(pl.multiple_of(index * columns, 64), columns), 3 * GROUP :].astype(FULL)
    own = jnp.concatenate([own, jnp.zeros((GROUP - columns, TILE), FULL)], axis=0)
    own = jnp.transpose(own)
    expand = expand_matrix(columns)
    wide = jnp.dot(own[:24, :].astype(LOW)[:, :GROUP], jnp.concatenate(
        [expand, jnp.zeros((GROUP - columns, 4 * columns), LOW)], axis=0
    ), preferred_element_type=FULL)
    up_bias = jnp.zeros((1, 4 * columns), FULL)
    place = lanes((1, 4 * columns)) % 4
    for step in range(4):
        row = wide[8 + step : 9 + step] + wide[20 + step : 21 + step]
        up_bias = jnp.where(place == step, row, up_bias)
    up_bias_ref[...] = up_bias
    bias = jnp.concatenate(
        [
            own[0:1] + own[12:13],
            jnp.zeros((1, GROUP), FULL),
            own[1:2] + own[13:14],
        ],
        axis=1,
    )
    keep = lanes((1, 3 * GROUP)) % GROUP < columns
    for at, rows_ref in ((0, near_ref), (half, other_ref)):
        got = jnp.dot(rows_ref[...], weight_ref[:, : 3 * GROUP], preferred_element_type=FULL)
        qkv_ref[at : at + half, :] = jnp.where(keep, got + bias, 0.0).astype(LOW)

    length = 2 * half
    row_segments = segment_ref[...]
    column_segments = jnp.transpose(
        jnp.broadcast_to(row_segments.astype(FULL), (TILE, length))
    )[:, :1].astype(jnp.int32)
    same = column_segments == row_segments
    mixed_tiles = [None, None]
    for head in range(3):
        at = TILE * head_tile(head)
        mask = head_mask(head, (length, TILE))
        key = only(qkv_ref[:, GROUP + at : GROUP + at + TILE], mask) * jnp.asarray(0.125, LOW)
        scores = contract(key, qkv_ref[:, at : at + TILE], 1, 1)
        scores = jnp.where(same, scores, MASKED_SCORE)
        highest = jnp.max(scores, axis=0, keepdims=True)
        shifted = jnp.exp(scores - highest)
        total = jnp.sum(shifted, axis=0, keepdims=True)
        probs = (shifted * (1.0 / total)).astype(LOW)
        log_ref[head : head + 1, :] = highest + jnp.log(total)
        value = only(qkv_ref[:, 2 * GROUP + at : 2 * GROUP + at + TILE], mask)
        got = jnp.dot(transposed(value).astype(LOW), probs, preferred_element_type=FULL)
        tile = head_tile(head)
        mixed_tiles[tile] = got if mixed_tiles[tile] is None else mixed_tiles[tile] + got
    log_ref[3:, :] = jnp.zeros((5, length), FULL)
    for tile in range(2):
        mixed_ref[:, TILE * tile : TILE * (tile + 1)] = jnp.transpose(mixed_tiles[tile]).astype(LOW)
    out = packed_out(weight_ref)
    keep_ref[...] = contract(mixed_ref[:half, :], out, 1, 1)
    send_ref[...] = contract(mixed_ref[half:, :], out, 1, 1).astype(LOW)


def backward_kernel(
    index_ref,
    near_ref,
    other_ref,
    qkv_ref,
    log_ref,
    weight_ref,
    segment_ref,
    sums_ref,
    up_sum_ref,
    grad_ref,
    send_ref,
    keep_ref,
    vector_ref,
    mixed_grad,
    key_grad,
    value_grad,
    columns_held,
):
    index = index_ref[0]
    half = near_ref.shape[0]
    length = 2 * half
    columns = 3 * HEAD_DIM
    out = packed_out(weight_ref)
    mixed_grad[:half, :] = jnp.dot(near_ref[...], out, preferred_element_type=FULL).astype(LOW)
    mixed_grad[half:, :] = jnp.dot(other_ref[...], out, preferred_element_type=FULL).astype(LOW)
    row_segments = segment_ref[...]
    column_segments = jnp.transpose(
        jnp.broadcast_to(row_segments.astype(FULL), (TILE, length))
    )[:, :1].astype(jnp.int32)
    same = column_segments == row_segments
    sums = []
    for tile in range(2):
        at = TILE * tile
        query_grad = jnp.zeros((TILE, length), FULL)
        for head in (0, 1) if tile == 0 else (2,):
            mask = head_mask(head, (length, TILE))
            scale = jnp.asarray(0.125, LOW)
            key = only(qkv_ref[:, GROUP + at : GROUP + at + TILE], mask) * scale
            query = only(qkv_ref[:, at : at + TILE], mask)
            value = only(qkv_ref[:, 2 * GROUP + at : 2 * GROUP + at + TILE], mask)
            grad = only(mixed_grad[:, at : at + TILE], mask)
            scores = contract(key, query, 1, 1)
            probs = jnp.exp(
                jnp.where(same, scores, MASKED_SCORE) - log_ref[head : head + 1, :]
            )
            probs_grad = contract(value, grad, 1, 1)
            inner = jnp.sum(probs * probs_grad, axis=0, keepdims=True)
            scores_grad = (probs * (probs_grad - inner)).astype(LOW)
            got = jnp.dot(probs.astype(LOW), grad, preferred_element_type=FULL)
            got_key = jnp.dot(scores_grad, query * scale, preferred_element_type=FULL)
            if head % 2 == 0:
                value_grad[...] = got
                key_grad[...] = got_key
            else:
                value_grad[...] += got
                key_grad[...] += got_key
            query_grad += jnp.dot(
                transposed(key).astype(LOW), scores_grad, preferred_element_type=FULL
            )
        query_low = jnp.transpose(query_grad).astype(LOW)
        value_low = value_grad[...].astype(LOW)
        grad_ref[:, at : at + TILE] = query_low
        grad_ref[:, GROUP + at : GROUP + at + TILE] = key_grad[...].astype(LOW)
        grad_ref[:, 2 * GROUP + at : 2 * GROUP + at + TILE] = value_low
        sums.append(
            (
                jnp.sum(query_low.astype(FULL), axis=0, keepdims=True),
                jnp.sum(value_low.astype(FULL), axis=0, keepdims=True),
            )
        )
    wide = weight_ref[:, : 3 * GROUP]
    keep_ref[...] = contract(grad_ref[:half, :], wide, 1, 1)
    send_ref[...] = contract(grad_ref[half:, :], wide, 1, 1).astype(LOW)

    up_row = up_sum_ref[...]
    place = lanes((8, 4 * columns))
    spaced = jnp.where(place % 4 == lanes((8, 4 * columns), 0), up_row, 0.0)
    high = spaced.astype(LOW)
    low = (spaced - high.astype(FULL)).astype(LOW)
    expand = expand_matrix(columns)
    up_rows = contract(high, expand, 1, 1) + contract(low, expand, 1, 1)
    up_rows = jnp.concatenate([up_rows, jnp.zeros((8, GROUP - columns), FULL)], axis=1)
    query_sum = jnp.concatenate([sums[0][0], sums[1][0]], axis=1)
    value_sum = jnp.concatenate([sums[0][1], sums[1][1]], axis=1)
    at_row = lanes((8, GROUP), 0)
    late = jnp.where(at_row == 6, query_sum, jnp.where(at_row == 7, value_sum, 0.0))
    stacked = jnp.concatenate([late, up_rows, jnp.zeros((TILE - 16, GROUP), FULL)], axis=0)
    columns_held[...] = jnp.zeros_like(columns_held)
    columns_held[pl.ds(pl.multiple_of(index * columns, 64), columns), :] = jnp.transpose(stacked)[
        :columns
    ]
    placed = jnp.transpose(columns_held[...])[:16]
    given = sums_ref[...]
    vector_ref[:8, :] = placed[:8] + given
    vector_ref[8:, :] = placed[8:]


def weights_kernel(tokens_near, tokens_other, near_ref, other_ref, grad_ref, mixed_ref, out_ref):
    half = near_ref.shape[0]
    width = near_ref.shape[1]
    got = contract(tokens_near[...], grad_ref[:half, :], 0, 0) + contract(
        tokens_other[...], grad_ref[half:, :], 0, 0
    )
    out_grad = contract(near_ref[...], mixed_ref[:half, :], 0, 0) + contract(
        other_ref[...], mixed_ref[half:, :], 0, 0
    )
    high = head_mask(1, (width, TILE))
    for part, lined in enumerate(lined_heads(out_grad)):
        at = GROUP * part
        out_ref[:, at : at + TILE] = got[:, at : at + TILE].astype(LOW)
        out_ref[:, at + TILE : at + GROUP] = jnp.where(
            high, lined, got[:, at + TILE : at + GROUP]
        ).astype(LOW)
    out_ref[:, 3 * GROUP :] = jnp.zeros((width, TILE), LOW)


def place_of(vector_rows, shape, dim):
    place = lanes(shape, dim)
    many = 8 * vector_rows
    row = jnp.where(place < many, place % vector_rows, (place - many) // 4)
    column = jnp.where(place < many, place // vector_rows, 8 + (place - many) % 4)
    return (row, jnp.where(place < many + 4 * vector_rows, column, 1000))


def first_block_kernel(
    index_ref, own_ref, core_ref, far_ref, both_ref, q_ref, k_ref, v_ref, out_ref, block_ref
):
    index = index_ref[0]
    rows = q_ref.shape[0]
    vector_rows = rows // 4
    shape = (rows, own_ref.shape[1])
    row_at = lanes(shape, 0)
    near = [own_ref[...], core_ref[...], far_ref[...], both_ref[...]]
    spread_rows = jnp.zeros(shape, FULL)
    for at in range(4):
        row = near[3]
        for mask in (2, 1, 0):
            row = jnp.where((index ^ mask) == at, near[mask], row)
        spread_rows = jnp.where(row_at // vector_rows == at, row, spread_rows)
    place_row, _ = place_of(vector_rows, shape, 1)
    spread_rows = jnp.where(place_row == row_at % vector_rows, spread_rows, 0.0)
    high = spread_rows.astype(LOW)
    low = (spread_rows - high.astype(FULL)).astype(LOW)
    shape = (shape[1], TILE)
    _, place_column = place_of(vector_rows, shape, 0)
    columns = lanes(shape)
    first = jnp.where(place_column == columns, 1.0, 0.0).astype(LOW)
    second = jnp.where(place_column + 12 == columns, 1.0, 0.0).astype(LOW)
    packed = jnp.dot(high, first, preferred_element_type=FULL) + jnp.dot(
        low, second, preferred_element_type=FULL
    )
    out = out_ref[...].astype(FULL)
    block = jnp.concatenate(
        [
            q_ref[...].astype(FULL),
            out[:, :HEAD_DIM],
            k_ref[...].astype(FULL),
            out[:, HEAD_DIM : 2 * HEAD_DIM],
            v_ref[...].astype(FULL),
            out[:, 2 * HEAD_DIM :],
            packed,
        ],
        axis=1,
    ).astype(LOW)
    for at in range(block_ref.shape[0]):
        block_ref[at] = block


def second_block_kernel(index_ref, own_ref, other_ref, block_ref):
    lower = index_ref[0] == 0
    own = own_ref[...].astype(FULL)
    other = other_ref[...].astype(FULL)
    block = jnp.concatenate(
        [jnp.where(lower, own, other), jnp.where(lower, other, own)], axis=0
    ).astype(LOW)
    for at in range(block_ref.shape[0]):
        block_ref[at] = block


def moments(values, gain, shift):
    center = values - jnp.mean(values, axis=-1, keepdims=True)
    scale_inv = lax.rsqrt(jnp.mean(center * center, axis=-1, keepdims=True) + NORM_EPSILON)
    normed = center * scale_inv
    return (normed * gain + shift, normed, scale_inv)


def norm_backward(upstream, normed, scale_inv, gain):
    scaled = upstream * gain
    return scale_inv * (
        scaled
        - jnp.mean(scaled, axis=-1, keepdims=True)
        - normed * jnp.mean(scaled * normed, axis=-1, keepdims=True)
    )


def blocks_of(rows, size=64):
    return [(at, at + size) for at in range(0, rows, size)]


def first_norm_kernel(
    tokens_ref, chip_ref, far_ref, rows_ref, first_ref, low_ref, normed_ref, scale_ref
):
    for at, to in blocks_of(tokens_ref.shape[0]):
        values = (
            tokens_ref[at:to].astype(FULL)
            + (chip_ref[at:to] + far_ref[at:to].astype(FULL))
            + rows_ref[2:3]
        )
        first, normed, scale_inv = moments(values, rows_ref[4:5], rows_ref[5:6])
        first_ref[at:to] = first
        low_ref[at:to] = first.astype(LOW)
        normed_ref[at:to] = normed
        scale_ref[at:to] = jnp.broadcast_to(scale_inv, (to - at, TILE))


def feed_kernel(
    near_ref,
    other_ref,
    blocks_ref,
    bias_ref,
    active_ref,
    slope_ref,
    keep_ref,
    send_ref,
    up_ref,
    down_ref,
):
    count, rows, wide = blocks_ref.shape
    rows = rows // 2
    hidden = wide // 2
    group = 1 if rows % 16 == 0 else 2
    for lower in range(2):
        for at in range(0, count, group):
            got = jnp.concatenate(
                [
                    blocks_ref[at + i].astype(FULL)[rows * lower : rows * (lower + 1)]
                    for i in range(group)
                ],
                axis=0,
            ).astype(LOW)
            to = (lower * count + at) * rows
            up_ref[to : to + group * rows] = got[:, :hidden]
            down_ref[to : to + group * rows] = got[:, hidden:]
    half = near_ref.shape[0]
    size = half // 2
    for base, rows_ref in ((half, other_ref), (0, near_ref)):
        for at, to in blocks_of(half, size):
            upward = (
                jnp.dot(rows_ref[at:to], up_ref[...], preferred_element_type=FULL) + bias_ref[...]
            )
            for low, high in blocks_of(size, 32):
                part = upward[low:high]
                gate = 0.5 * (1.0 + lax.erf(part * ROOT_HALF))
                active_ref[base + at + low : base + at + high] = (part * gate).astype(LOW)
                slope_ref[base + at + low : base + at + high] = (
                    gate + part * jnp.exp(-0.5 * part * part) * INV_ROOT_TAU
                )
            got = contract(active_ref[base + at : base + to], down_ref[...], 1, 1)
            if base:
                send_ref[at:to] = got.astype(LOW)
            else:
                keep_ref[at:to] = got


def second_norm_kernel(
    first_ref,
    chip_ref,
    far_ref,
    rows_ref,
    cotangent_ref,
    cotangent_far_ref,
    output_ref,
    grad_ref,
    low_ref,
    sums_ref,
):
    own = output_ref.shape[0]
    sums = [jnp.zeros((1, first_ref.shape[1]), FULL) for _ in range(3)]
    for at, to in blocks_of(first_ref.shape[0]):
        values = first_ref[at:to] + (chip_ref[at:to] + far_ref[at:to].astype(FULL)) + rows_ref[3:4]
        output, normed, scale_inv = moments(values, rows_ref[6:7], rows_ref[7:8])
        if to <= own:
            upstream = cotangent_ref[at:to].astype(FULL)
            output_ref[at:to] = output.astype(LOW)
        else:
            upstream = cotangent_far_ref[at - own : to - own].astype(FULL)
        grad = norm_backward(upstream, normed, scale_inv, rows_ref[6:7])
        grad_ref[at:to] = grad
        low = grad.astype(LOW)
        low_ref[at:to] = low
        if to <= own:
            for i, part in enumerate((low.astype(FULL), upstream * normed, upstream)):
                sums[i] += jnp.sum(part, axis=0, keepdims=True)
    sums_ref[...] = jnp.concatenate(sums + [jnp.zeros((5, sums[0].shape[1]), FULL)], axis=0)


def feed_backward_kernel(
    near_ref, other_ref, up_ref, down_ref, slope_ref, grad_ref, keep_ref, send_ref, sum_ref
):
    half = near_ref.shape[0]
    size = half // 2
    total = jnp.zeros((1, up_ref.shape[1]), FULL)
    for base, rows_ref in ((half, other_ref), (0, near_ref)):
        for at, to in blocks_of(half, size):
            grad = jnp.dot(rows_ref[at:to], down_ref[...], preferred_element_type=FULL)
            for low, high in blocks_of(size, 32):
                place = slice(base + at + low, base + at + high)
                part = (grad[low:high] * slope_ref[place]).astype(LOW)
                grad_ref[place] = part
                total += jnp.sum(part.astype(FULL), axis=0, keepdims=True)
            got = contract(grad_ref[base + at : base + to], up_ref[...], 1, 1)
            if base:
                send_ref[at:to] = got.astype(LOW)
            else:
                keep_ref[at:to] = got
    sum_ref[...] = total


def feed_weights_kernel(
    hidden_near, hidden_other, branch_near, branch_other, active_ref, grad_ref, out_ref
):
    half = hidden_near.shape[0]
    count, rows, wide = out_ref.shape
    rows = rows // 2
    hidden = wide // 2
    for place, near, other, right in (
        (0, hidden_near, hidden_other, grad_ref),
        (hidden, branch_near, branch_other, active_ref),
    ):
        got = contract(near[...], right[:half], 0, 0) + contract(other[...], right[half:], 0, 0)
        for at in range(count):
            out_ref[at, :, place : place + hidden] = jnp.concatenate(
                [got[at * rows : (at + 1) * rows], got[(count + at) * rows :][:rows]], axis=0
            ).astype(LOW)


def first_norm_backward_kernel(
    second_ref,
    chip_ref,
    far_ref,
    normed_ref,
    scale_ref,
    rows_ref,
    second_sums_ref,
    grad_ref,
    low_ref,
    sums_ref,
):
    own = grad_ref.shape[0]
    sums = [jnp.zeros((1, second_ref.shape[1]), FULL) for _ in range(3)]
    for at, to in blocks_of(second_ref.shape[0]):
        upstream = second_ref[at:to] + (chip_ref[at:to] + far_ref[at:to].astype(FULL))
        normed = normed_ref[at:to]
        grad = norm_backward(upstream, normed, scale_ref[at:to, :1], rows_ref[4:5])
        low = grad.astype(LOW)
        low_ref[at:to] = low
        if to <= own:
            grad_ref[at:to] = grad
            for i, part in enumerate((low.astype(FULL), upstream * normed, upstream)):
                sums[i] += jnp.sum(part, axis=0, keepdims=True)
    given = second_sums_ref[...]
    sums_ref[...] = jnp.concatenate(
        [
            sums[0],
            given[0:1],
            sums[1],
            sums[2],
            given[1:3],
            jnp.zeros((2, sums[0].shape[1]), FULL),
        ],
        axis=0,
    )


def plane_sum_kernel(index_ref, blocks_ref, keep_ref, send_ref):
    rows = keep_ref.shape[0]
    total = blocks_ref[0].astype(FULL)
    for at in range(1, blocks_ref.shape[0]):
        total += blocks_ref[at].astype(FULL)
    lower = index_ref[0] == 0
    keep_ref[...] = jnp.where(lower, total[:rows], total[rows:])
    send_ref[...] = jnp.where(lower, total[rows:], total[:rows])


def last_sum_kernel(index_ref, blocks_ref, q_ref, k_ref, v_ref, out_ref, vector_ref):
    index = index_ref[0]
    rows = q_ref.shape[0]
    vector_rows = rows // 4
    columns = q_ref.shape[1]
    total = blocks_ref[0].astype(FULL)
    for at in range(1, blocks_ref.shape[0]):
        total += blocks_ref[at].astype(FULL)
    q_ref[...] = total[:, :columns]
    k_ref[...] = total[:, GROUP : GROUP + columns]
    v_ref[...] = total[:, 2 * GROUP : 2 * GROUP + columns]
    out_ref[...] = jnp.concatenate(
        [total[:, GROUP * i + columns : GROUP * (i + 1)] for i in range(3)], axis=1
    )
    packed = total[:, 3 * GROUP :]
    packed = packed + pltpu.roll(packed, TILE - 12, 1)
    wide = vector_ref.shape[1]
    _, place_column = place_of(vector_rows, (TILE, wide), 1)
    select = jnp.where(place_column == lanes((TILE, wide), 0), 1.0, 0.0).astype(LOW)
    line = jnp.zeros((rows, wide), FULL)
    left = packed
    for _ in range(3):
        part = left.astype(LOW)
        left = left - part.astype(FULL)
        line += jnp.dot(part, select, preferred_element_type=FULL)
    place_row, _ = place_of(vector_rows, (rows, wide), 1)
    keep = place_row + index * vector_rows == lanes((rows, wide), 0)
    vector_ref[...] = jnp.sum(jnp.where(keep, line, 0.0), axis=0, keepdims=True)


def shards(
    tokens,
    segments,
    q_weight,
    k_weight,
    v_weight,
    up_weight,
    out_weight,
    down_weight,
    q_bias,
    v_bias,
    out_bias,
    up_bias,
    down_bias,
    norm1_gain,
    norm1_shift,
    norm2_gain,
    norm2_shift,
    cotangent,
):
    my_index = lax.axis_index("tensor")
    dp_count = lax.axis_size("dp")
    local_len, width = tokens.shape[1:]
    half = 2 * local_len
    length = 4 * local_len
    shard_rows, head_cols = q_weight.shape
    hidden_cols = up_weight.shape[1]
    tokens = tokens[0]
    cotangent = cotangent[0]
    index = my_index.reshape(1)
    side_index = (lax.axis_index("dp") // (dp_count // 2)).reshape(1)

    vector_rows = q_bias.shape[0]
    line_size = -(-12 * vector_rows // TILE) * TILE
    line = jnp.concatenate(
        [
            q_bias,
            v_bias,
            out_bias,
            down_bias,
            norm1_gain,
            norm1_shift,
            norm2_gain,
            norm2_shift,
            up_bias,
            jnp.zeros((line_size - 12 * vector_rows,), FULL),
        ]
    )[None]
    lines = [line] + [swap(line, mask) for mask in (1, 2, 3)]
    tokens_far = swap(tokens, 2)
    second_own = jnp.concatenate([up_weight, down_weight], axis=1)
    second_side = side(second_own)
    (first_block,) = call(
        first_block_kernel,
        [((dp_count, shard_rows, 3 * GROUP + TILE), LOW)],
        index,
        *lines,
        q_weight,
        k_weight,
        v_weight,
        out_weight,
        smem=1,
    )
    first_full = spread(first_block).reshape(width, -1)
    tokens_pair = jnp.concatenate([tokens, tokens_far], axis=0)
    tokens_core = swap(tokens_pair, 1)
    cotangent_far = swap(after(cotangent, tokens_far), 2)
    segment_row = ordered_segments(segments[0], my_index)[None]
    (second_block,) = call(
        second_block_kernel,
        [((dp_count // 2, 2 * shard_rows, 2 * hidden_cols), LOW)],
        side_index,
        second_own,
        second_side,
        smem=1,
    )
    first_full, second_block, tokens_core, cotangent_far, segment_row = lax.optimization_barrier(
        (first_full, second_block, tokens_core, cotangent_far, segment_row)
    )
    second_full = plane(second_block)

    qkv_rows, mixed_rows, log_totals, attn_send, attn_keep, rows, bias_up = call(
        forward_kernel,
        [
            ((length, 3 * GROUP), LOW),
            ((length, GROUP), LOW),
            ((8, length), FULL),
            ((half, width), LOW),
            ((half, width), FULL),
            ((8, width), FULL),
            ((1, hidden_cols), FULL),
        ],
        index,
        tokens_pair,
        tokens_core,
        first_full,
        segment_row,
        smem=1,
    )
    attn_chip = attn_keep + swap(attn_send, 1).astype(FULL)
    first, hidden_low, normed_first, inv_first = call(
        first_norm_kernel,
        [((half, width), FULL), ((half, width), LOW), ((half, width), FULL), ((half, TILE), FULL)],
        tokens_pair,
        attn_chip,
        far_sum(attn_chip),
        rows,
    )
    hidden_core = swap(hidden_low, 1)
    active, slope, branch_keep, branch_send, up_full, down_full = call(
        feed_kernel,
        [
            ((length, hidden_cols), LOW),
            ((length, hidden_cols), FULL),
            ((half, width), FULL),
            ((half, width), LOW),
            ((width, hidden_cols), LOW),
            ((width, hidden_cols), LOW),
        ],
        hidden_low,
        hidden_core,
        second_full,
        bias_up,
    )
    branch_chip = branch_keep + swap(branch_send, 1).astype(FULL)
    layer_output, second_grad, branch_low, second_sums = call(
        second_norm_kernel,
        [((local_len, width), LOW), ((half, width), FULL), ((half, width), LOW), ((8, width), FULL)],
        first,
        branch_chip,
        far_sum(branch_chip),
        rows,
        cotangent,
        cotangent_far,
    )
    branch_core = swap(branch_low, 1)
    upward_grad, hidden_keep, hidden_send, up_sum = call(
        feed_backward_kernel,
        [
            ((length, hidden_cols), LOW),
            ((half, width), FULL),
            ((half, width), LOW),
            ((1, hidden_cols), FULL),
        ],
        branch_low,
        branch_core,
        up_full,
        down_full,
        slope,
    )
    hidden_chip = hidden_keep + swap(hidden_send, 1).astype(FULL)
    hidden_far = far_sum(hidden_chip)
    (pair_block,) = call(
        feed_weights_kernel,
        [((dp_count // 2, 2 * shard_rows, 2 * hidden_cols), LOW)],
        hidden_low,
        hidden_core,
        branch_low,
        branch_core,
        active,
        upward_grad,
    )
    pair_blocks = plane(after(pair_block, hidden_chip))
    resid_grad, attended_low, given = call(
        first_norm_backward_kernel,
        [((local_len, width), FULL), ((half, width), LOW), ((8, width), FULL)],
        second_grad,
        hidden_chip,
        hidden_far,
        normed_first,
        inv_first,
        rows,
        second_sums,
    )
    attended_core = swap(attended_low, 1)
    qkv_grad, input_send, input_keep, vector_sums = call(
        backward_kernel,
        [
            ((length, 3 * GROUP), LOW),
            ((half, width), LOW),
            ((half, width), FULL),
            ((16, width), FULL),
        ],
        index,
        attended_low,
        attended_core,
        qkv_rows,
        log_totals,
        first_full,
        segment_row,
        given,
        up_sum,
        smem=1,
        scratch=[
            pltpu.VMEM((length, GROUP), LOW),
            pltpu.VMEM((length, TILE), FULL),
            pltpu.VMEM((length, TILE), FULL),
            pltpu.VMEM((width, TILE), FULL),
        ],
    )
    vector_near = [swap(vector_sums, mask) for mask in (1, 2, 3)]
    input_got = swap(input_send, 1)
    (last_block,) = call(
        weights_kernel,
        [((width, 3 * GROUP + TILE), LOW)],
        tokens_pair,
        tokens_core,
        attended_low,
        attended_core,
        qkv_grad,
        mixed_rows,
    )
    vector_sums = vector_sums + vector_near[0] + vector_near[1] + vector_near[2]
    high, low = halves(vector_sums[:12].T)
    last_block = lax.dynamic_update_slice(
        last_block, jnp.concatenate([high, low], axis=1), (0, 3 * GROUP)
    )
    input_chip = input_keep + input_got.astype(FULL)
    input_far = swap(input_chip[local_len:].astype(LOW), 2)
    last_blocks = spread(
        after(last_block, input_chip).reshape(dp_count, shard_rows, 3 * GROUP + TILE)
    )
    input_grad = resid_grad + (input_chip[:local_len] + input_far.astype(FULL))

    pair_keep, pair_send = call(
        plane_sum_kernel,
        [((shard_rows, 2 * hidden_cols), FULL)] * 2,
        side_index,
        pair_blocks,
        smem=1,
    )
    pair_sum = pair_keep + side(pair_send)
    q_grad, k_grad, v_grad, out_grad, line = call(
        last_sum_kernel,
        [((shard_rows, head_cols), FULL)] * 4 + [((1, line_size), FULL)],
        index,
        last_blocks,
        smem=1,
    )
    line = line[0]
    vectors = [line[vector_rows * i : vector_rows * (i + 1)] for i in range(8)]
    return (
        layer_output[None],
        input_grad[None],
        q_grad,
        k_grad,
        v_grad,
        pair_sum[:, :hidden_cols],
        out_grad,
        pair_sum[:, hidden_cols:],
        vectors[6],
        vectors[7],
        vectors[0],
        line[8 * vector_rows : 12 * vector_rows],
        vectors[1],
        vectors[2],
        vectors[3],
        vectors[4],
        vectors[5],
    )


def solution(mesh):
    matrix = P("dp", "tensor")
    vector = P(("dp", "tensor"))
    rows = P("dp", "tensor", None)
    return jax.shard_map(
        shards,
        mesh=mesh,
        in_specs=(rows, P("dp", None)) + (matrix,) * 6 + (vector,) * 9 + (rows,),
        out_specs=(rows, rows) + (matrix,) * 6 + (vector,) * 9,
        check_vma=False,
    )
```

```python
import functools

import jax
import jax.numpy as jnp
from jax import lax
from jax.experimental import pallas as pl
from jax.experimental.pallas import tpu as pltpu
from jax.sharding import PartitionSpec as P

HEAD_DIM = 64
TILE = 128
GROUP = 256


NORM_EPSILON = 1e-12
MASKED_SCORE = -1000000000.0
ROOT_HALF = 0.7071067811865476
INV_ROOT_TAU = 0.3989422804014327
LOW = jnp.bfloat16
FULL = jnp.float32
VMEM_LIMIT = 48 * 1024 * 1024


def contract(left, right, left_dim, right_dim):
    return lax.dot_general(
        left, right, (((left_dim,), (right_dim,)), ((), ())), preferred_element_type=jnp.float32
    )


def swap(values, mask):
    return lax.ppermute(values, "tensor", [(i, i ^ mask) for i in range(4)])


def after(values, *others):
    return lax.optimization_barrier((values, *others))[0]


def spread(stacked):
    return lax.all_to_all(stacked, "dp", 0, 0, tiled=True)


def plane_groups():
    count = lax.axis_size("dp") // 2
    return [list(range(count)), list(range(count, 2 * count))]


def plane(stacked):
    return lax.all_to_all(stacked, "dp", 0, 0, tiled=True, axis_index_groups=plane_groups())


def side(values):
    count = lax.axis_size("dp")
    pairs = [(i, (i + count // 2) % count) for i in range(count)]
    return lax.ppermute(values, "dp", pairs)


def halves(values):
    high = lax.reduce_precision(values, 8, 7)
    return (high.astype(LOW), (values - high).astype(LOW))


def far_pack(total):
    quarter = total.shape[0] // 2
    sent = total.astype(LOW)
    return jnp.concatenate([sent[quarter:], sent[:quarter]], axis=0)


def ordered_segments(segment_row, my_index):
    quarters = segment_row.reshape(4, -1)
    core = my_index % 2 == 1
    quarters = jnp.where(core, quarters[jnp.array([1, 0, 3, 2])], quarters)
    far = my_index // 2 == 1
    quarters = jnp.where(far, quarters[jnp.array([2, 3, 0, 1])], quarters)
    return jnp.concatenate([quarters[0], quarters[2], quarters[1], quarters[3]])


def call(body, out_shapes, *operands, smem=0, scratch=(), away=(), far=(), aliases=None):
    specs = [pl.BlockSpec(memory_space=pltpu.SMEM)] * smem
    specs += [
        pl.BlockSpec(memory_space=pltpu.HBM if i in far else pltpu.VMEM)
        for i in range(smem, len(operands))
    ]
    return pl.pallas_call(
        body,
        out_shape=[
            pltpu.HBM(shape, kind) if i in away else jax.ShapeDtypeStruct(shape, kind)
            for i, (shape, kind) in enumerate(out_shapes)
        ],
        in_specs=specs,
        out_specs=[
            pl.BlockSpec(memory_space=pltpu.HBM if i in away else pltpu.VMEM)
            for i in range(len(out_shapes))
        ],
        input_output_aliases=aliases or {},
        scratch_shapes=list(scratch),
        compiler_params=pltpu.CompilerParams(vmem_limit_bytes=VMEM_LIMIT),
        cost_estimate=pl.CostEstimate(flops=1000, bytes_accessed=1000, transcendentals=0),
    )(*operands)


def lanes(shape, dim=1):
    return lax.broadcasted_iota(jnp.int32, shape, dim)


def head_tile(head):
    return head // 2


def head_mask(head, shape, dim=1):
    index = lanes(shape, dim)
    return index >= HEAD_DIM if head % 2 else index < HEAD_DIM


def only(values, mask):
    return jnp.where(mask, values, jnp.zeros_like(values))


def packed_out(weight_ref):
    rows = weight_ref.shape[0]
    parts = [
        weight_ref[:, GROUP * i + TILE : GROUP * (i + 1)].astype(FULL) for i in range(3)
    ]
    low = head_mask(0, (rows, TILE))
    first = jnp.where(low, pltpu.roll(parts[0], HEAD_DIM, 1), parts[1])
    second = jnp.where(low, pltpu.roll(parts[2], HEAD_DIM, 1), 0.0)
    return jnp.concatenate([first, second], axis=1).astype(LOW)


def lined_heads(rows):
    first, second = rows[:, :TILE], rows[:, TILE:]
    return [pltpu.roll(first, HEAD_DIM, 1), first, pltpu.roll(second, HEAD_DIM, 1)]


def transposed(values):
    return jnp.transpose(values.astype(FULL))


def expand_matrix(count):
    shape = (count, 4 * count)
    return jnp.where(lanes(shape) // 4 == lanes(shape, 0), 1.0, 0.0).astype(LOW)


def forward_kernel(
    index_ref,
    near_ref,
    other_ref,
    weight_ref,
    segment_ref,
    qkv_out,
    mixed_ref,
    log_ref,
    send_ref,
    keep_ref,
    vector_ref,
    up_bias_ref,
    qkv_ref,
    qkv_sem,
):
    index = index_ref[0]
    half = near_ref.shape[0]
    columns = 3 * HEAD_DIM
    width = weight_ref.shape[0]
    held = weight_ref[:, 3 * GROUP :].astype(FULL)
    flat = jnp.transpose(held)
    vector_ref[...] = flat[:8] + flat[12:20]
    own = weight_ref[pl.ds(pl.multiple_of(index * columns, 64), columns), 3 * GROUP :].astype(FULL)
    own = jnp.concatenate([own, jnp.zeros((GROUP - columns, TILE), FULL)], axis=0)
    own = jnp.transpose(own)
    expand = expand_matrix(columns)
    wide = jnp.dot(own[:24, :].astype(LOW)[:, :GROUP], jnp.concatenate(
        [expand, jnp.zeros((GROUP - columns, 4 * columns), LOW)], axis=0
    ), preferred_element_type=FULL)
    up_bias = jnp.zeros((1, 4 * columns), FULL)
    place = lanes((1, 4 * columns)) % 4
    for step in range(4):
        row = wide[8 + step : 9 + step] + wide[20 + step : 21 + step]
        up_bias = jnp.where(place == step, row, up_bias)
    up_bias_ref[...] = up_bias
    bias = jnp.concatenate(
        [
            own[0:1] + own[12:13],
            jnp.zeros((1, GROUP), FULL),
            own[1:2] + own[13:14],
        ],
        axis=1,
    )
    keep = lanes((1, 3 * GROUP)) % GROUP < columns
    for at, rows_ref in ((0, near_ref), (half, other_ref)):
        got = jnp.dot(rows_ref[...], weight_ref[:, : 3 * GROUP], preferred_element_type=FULL)
        qkv_ref[at : at + half, :] = jnp.where(keep, got + bias, 0.0).astype(LOW)
    qkv_copy = pltpu.make_async_copy(qkv_ref, qkv_out, qkv_sem)
    qkv_copy.start()

    length = 2 * half
    row_segments = segment_ref[...]
    column_segments = jnp.transpose(
        jnp.broadcast_to(row_segments.astype(FULL), (TILE, length))
    )[:, :1].astype(jnp.int32)
    same = column_segments == row_segments
    mixed_tiles = [None, None]
    for head in range(3):
        at = TILE * head_tile(head)
        mask = head_mask(head, (length, TILE))
        key = only(qkv_ref[:, GROUP + at : GROUP + at + TILE], mask) * jnp.asarray(0.125, LOW)
        scores = contract(key, qkv_ref[:, at : at + TILE], 1, 1)
        scores = jnp.where(same, scores, MASKED_SCORE)
        highest = jnp.max(scores, axis=0, keepdims=True)
        shifted = jnp.exp(scores - highest)
        total = jnp.sum(shifted, axis=0, keepdims=True)
        probs = (shifted * (1.0 / total)).astype(LOW)
        log_ref[head : head + 1, :] = highest + jnp.log(total)
        value = only(qkv_ref[:, 2 * GROUP + at : 2 * GROUP + at + TILE], mask)
        got = jnp.dot(transposed(value).astype(LOW), probs, preferred_element_type=FULL)
        tile = head_tile(head)
        mixed_tiles[tile] = got if mixed_tiles[tile] is None else mixed_tiles[tile] + got
    log_ref[3:, :] = jnp.zeros((5, length), FULL)
    for tile in range(2):
        mixed_ref[:, TILE * tile : TILE * (tile + 1)] = jnp.transpose(mixed_tiles[tile]).astype(LOW)
    out = packed_out(weight_ref)
    keep_ref[...] = contract(mixed_ref[:half, :], out, 1, 1)
    send_ref[...] = contract(mixed_ref[half:, :], out, 1, 1).astype(LOW)
    qkv_copy.wait()


def backward_kernel(
    index_ref,
    near_ref,
    other_ref,
    qkv_ref,
    log_ref,
    weight_ref,
    segment_ref,
    sums_ref,
    up_sum_ref,
    up_sum_other_ref,
    grad_ref,
    send_ref,
    keep_ref,
    vector_ref,
    mixed_grad,
    key_grad,
    value_grad,
    columns_held,
):
    index = index_ref[0]
    half = near_ref.shape[0]
    length = 2 * half
    columns = 3 * HEAD_DIM
    out = packed_out(weight_ref)
    mixed_grad[:half, :] = jnp.dot(near_ref[...], out, preferred_element_type=FULL).astype(LOW)
    mixed_grad[half:, :] = jnp.dot(other_ref[...], out, preferred_element_type=FULL).astype(LOW)
    row_segments = segment_ref[...]
    column_segments = jnp.transpose(
        jnp.broadcast_to(row_segments.astype(FULL), (TILE, length))
    )[:, :1].astype(jnp.int32)
    same = column_segments == row_segments
    sums = []
    for tile in range(2):
        at = TILE * tile
        query_grad = jnp.zeros((TILE, length), FULL)
        for head in (0, 1) if tile == 0 else (2,):
            mask = head_mask(head, (length, TILE))
            scale = jnp.asarray(0.125, LOW)
            key = only(qkv_ref[:, GROUP + at : GROUP + at + TILE], mask) * scale
            query = only(qkv_ref[:, at : at + TILE], mask)
            value = only(qkv_ref[:, 2 * GROUP + at : 2 * GROUP + at + TILE], mask)
            grad = only(mixed_grad[:, at : at + TILE], mask)
            scores = contract(key, query, 1, 1)
            probs = jnp.exp(
                jnp.where(same, scores, MASKED_SCORE) - log_ref[head : head + 1, :]
            )
            probs_grad = contract(value, grad, 1, 1)
            inner = jnp.sum(probs * probs_grad, axis=0, keepdims=True)
            scores_grad = (probs * (probs_grad - inner)).astype(LOW)
            got = jnp.dot(probs.astype(LOW), grad, preferred_element_type=FULL)
            got_key = jnp.dot(scores_grad, query * scale, preferred_element_type=FULL)
            if head % 2 == 0:
                value_grad[...] = got
                key_grad[...] = got_key
            else:
                value_grad[...] += got
                key_grad[...] += got_key
            query_grad += jnp.dot(
                transposed(key).astype(LOW), scores_grad, preferred_element_type=FULL
            )
        query_low = jnp.transpose(query_grad).astype(LOW)
        value_low = value_grad[...].astype(LOW)
        grad_ref[:, at : at + TILE] = query_low
        grad_ref[:, GROUP + at : GROUP + at + TILE] = key_grad[...].astype(LOW)
        grad_ref[:, 2 * GROUP + at : 2 * GROUP + at + TILE] = value_low
        sums.append(
            (
                jnp.sum(query_low.astype(FULL), axis=0, keepdims=True),
                jnp.sum(value_low.astype(FULL), axis=0, keepdims=True),
            )
        )
    wide = weight_ref[:, : 3 * GROUP]
    keep_ref[...] = contract(grad_ref[:half, :], wide, 1, 1)
    send_ref[...] = contract(grad_ref[half:, :], wide, 1, 1).astype(LOW)

    up_row = up_sum_ref[...] + up_sum_other_ref[...]
    place = lanes((8, 4 * columns))
    spaced = jnp.where(place % 4 == lanes((8, 4 * columns), 0), up_row, 0.0)
    high = spaced.astype(LOW)
    low = (spaced - high.astype(FULL)).astype(LOW)
    expand = expand_matrix(columns)
    up_rows = contract(high, expand, 1, 1) + contract(low, expand, 1, 1)
    up_rows = jnp.concatenate([up_rows, jnp.zeros((8, GROUP - columns), FULL)], axis=1)
    query_sum = jnp.concatenate([sums[0][0], sums[1][0]], axis=1)
    value_sum = jnp.concatenate([sums[0][1], sums[1][1]], axis=1)
    at_row = lanes((8, GROUP), 0)
    late = jnp.where(at_row == 6, query_sum, jnp.where(at_row == 7, value_sum, 0.0))
    stacked = jnp.concatenate([late, up_rows, jnp.zeros((TILE - 16, GROUP), FULL)], axis=0)
    columns_held[...] = jnp.zeros_like(columns_held)
    columns_held[pl.ds(pl.multiple_of(index * columns, 64), columns), :] = jnp.transpose(stacked)[
        :columns
    ]
    placed = jnp.transpose(columns_held[...])[:16]
    given = sums_ref[...]
    vector_ref[:8, :] = placed[:8] + given
    vector_ref[8:, :] = placed[8:]


def weights_kernel(
    tokens_near, tokens_other, near_ref, other_ref, grad_ref, mixed_ref, out, out_ref, sem
):
    half = near_ref.shape[0]
    width = near_ref.shape[1]
    got = contract(tokens_near[...], grad_ref[:half, :], 0, 0) + contract(
        tokens_other[...], grad_ref[half:, :], 0, 0
    )
    out_grad = contract(near_ref[...], mixed_ref[:half, :], 0, 0) + contract(
        other_ref[...], mixed_ref[half:, :], 0, 0
    )
    high = head_mask(1, (width, TILE))
    for part, lined in enumerate(lined_heads(out_grad)):
        at = GROUP * part
        out_ref[:, at : at + TILE] = got[:, at : at + TILE].astype(LOW)
        out_ref[:, at + TILE : at + GROUP] = jnp.where(
            high, lined, got[:, at + TILE : at + GROUP]
        ).astype(LOW)
    copy = pltpu.make_async_copy(out_ref, out.at[:, : 3 * GROUP], sem)
    copy.start()
    copy.wait()


def vectors_kernel(block_ref, own_ref, core_ref, far_ref, both_ref, out_ref, held, sem):
    total = own_ref[...] + core_ref[...] + (far_ref[...] + both_ref[...])
    total = total[:12]
    high = total.astype(LOW).astype(FULL)
    rows = jnp.concatenate(
        [high, total - high, jnp.zeros((TILE - 24, total.shape[1]), FULL)], axis=0
    )
    held[...] = jnp.transpose(rows).astype(LOW)
    copy = pltpu.make_async_copy(held, out_ref.at[:, 3 * GROUP :], sem)
    copy.start()
    copy.wait()


def place_of(vector_rows, shape, dim):
    place = lanes(shape, dim)
    many = 8 * vector_rows
    row = jnp.where(place < many, place % vector_rows, (place - many) // 4)
    column = jnp.where(place < many, place // vector_rows, 8 + (place - many) % 4)
    return (row, jnp.where(place < many + 4 * vector_rows, column, 1000))


def first_block_kernel(
    index_ref, own_ref, core_ref, far_ref, both_ref, weight_ref, block_ref
):
    index = index_ref[0]
    rows = weight_ref.shape[0]
    columns_each = weight_ref.shape[1] // 4
    vector_rows = rows // 4
    shape = (rows, own_ref.shape[1])
    row_at = lanes(shape, 0)
    near = [own_ref[...], core_ref[...], far_ref[...], both_ref[...]]
    spread_rows = jnp.zeros(shape, FULL)
    for at in range(4):
        row = near[3]
        for mask in (2, 1, 0):
            row = jnp.where((index ^ mask) == at, near[mask], row)
        spread_rows = jnp.where(row_at // vector_rows == at, row, spread_rows)
    place_row, _ = place_of(vector_rows, shape, 1)
    spread_rows = jnp.where(place_row == row_at % vector_rows, spread_rows, 0.0)
    high = spread_rows.astype(LOW)
    low = (spread_rows - high.astype(FULL)).astype(LOW)
    shape = (shape[1], TILE)
    _, place_column = place_of(vector_rows, shape, 0)
    columns = lanes(shape)
    first = jnp.where(place_column == columns, 1.0, 0.0).astype(LOW)
    second = jnp.where(place_column + 12 == columns, 1.0, 0.0).astype(LOW)
    packed = jnp.dot(high, first, preferred_element_type=FULL) + jnp.dot(
        low, second, preferred_element_type=FULL
    )
    weight = weight_ref[...].astype(FULL)
    q_part, k_part, v_part, out = [
        weight[:, columns_each * i : columns_each * (i + 1)] for i in range(4)
    ]
    block = jnp.concatenate(
        [
            q_part,
            out[:, :HEAD_DIM],
            k_part,
            out[:, HEAD_DIM : 2 * HEAD_DIM],
            v_part,
            out[:, 2 * HEAD_DIM :],
            packed,
        ],
        axis=1,
    ).astype(LOW)
    for at in range(block_ref.shape[0]):
        block_ref[at] = block


def second_block_kernel(index_ref, own_ref, other_ref, block_ref):
    lower = index_ref[0] == 0
    own = own_ref[...].astype(FULL)
    other = other_ref[...].astype(FULL)
    block = jnp.concatenate(
        [jnp.where(lower, own, other), jnp.where(lower, other, own)], axis=0
    ).astype(LOW)
    for at in range(block_ref.shape[0]):
        block_ref[at] = block


def moments(values, gain, shift):
    center = values - jnp.mean(values, axis=-1, keepdims=True)
    scale_inv = lax.rsqrt(jnp.mean(center * center, axis=-1, keepdims=True) + NORM_EPSILON)
    normed = center * scale_inv
    return (normed * gain + shift, normed, scale_inv)


def norm_backward(upstream, normed, scale_inv, gain):
    scaled = upstream * gain
    return scale_inv * (
        scaled
        - jnp.mean(scaled, axis=-1, keepdims=True)
        - normed * jnp.mean(scaled * normed, axis=-1, keepdims=True)
    )


def blocks_of(rows, size=64):
    return [(at, at + size) for at in range(0, rows, size)]


def first_norm_kernel(tokens_ref, chip_ref, far_ref, rows_ref, low_ref, scale_ref):
    for at, to in blocks_of(tokens_ref.shape[0], TILE):
        values = (
            tokens_ref[at:to].astype(FULL)
            + (chip_ref[at:to] + far_ref[at:to].astype(FULL))
            + rows_ref[2:3]
        )
        first, _, scale_inv = moments(values, rows_ref[4:5], rows_ref[5:6])
        low_ref[at:to] = first.astype(LOW)
        scale_ref[:, at:to] = jnp.transpose(jnp.broadcast_to(scale_inv, (TILE, TILE)))[:8]


def feed_rows(rows_ref, up, down, bias_ref, active_ref, slope_ref, part_ref):
    size = rows_ref.shape[0] // 2
    for at, to in blocks_of(rows_ref.shape[0], size):
        upward = jnp.dot(rows_ref[at:to], up[...], preferred_element_type=FULL) + bias_ref[...]
        for low, high in blocks_of(size, 32):
            part = upward[low:high]
            gate = 0.5 * (1.0 + lax.erf(part * ROOT_HALF))
            active_ref[at + low : at + high] = (part * gate).astype(LOW)
            slope_ref[at + low : at + high] = (
                gate + part * jnp.exp(-0.5 * part * part) * INV_ROOT_TAU
            )
        got = contract(active_ref[at:to], down[...], 1, 1)
        part_ref[at:to] = got.astype(part_ref.dtype)


def feed_other_kernel(
    rows_ref, blocks_ref, bias_ref, active_ref, slope_ref, part_ref, up_ref, down_ref
):
    count, rows, wide = blocks_ref.shape
    rows = rows // 2
    hidden = wide // 2
    group = 1 if rows % 16 == 0 else 2
    for lower in range(2):
        for at in range(0, count, group):
            got = jnp.concatenate(
                [
                    blocks_ref[at + i].astype(FULL)[rows * lower : rows * (lower + 1)]
                    for i in range(group)
                ],
                axis=0,
            ).astype(LOW)
            to = (lower * count + at) * rows
            up_ref[to : to + group * rows] = got[:, :hidden]
            down_ref[to : to + group * rows] = got[:, hidden:]
    feed_rows(rows_ref, up_ref, down_ref, bias_ref, active_ref, slope_ref, part_ref)


def feed_near_kernel(rows_ref, up_ref, down_ref, bias_ref, active_ref, slope_ref, part_ref):
    feed_rows(rows_ref, up_ref, down_ref, bias_ref, active_ref, slope_ref, part_ref)


def second_norm_kernel(
    first_ref,
    chip_ref,
    far_ref,
    rows_ref,
    cotangent_ref,
    cotangent_far_ref,
    output_ref,
    low_ref,
    sums_ref,
):
    own = output_ref.shape[0]
    sums = [jnp.zeros((1, first_ref.shape[1]), FULL) for _ in range(3)]
    for at, to in blocks_of(first_ref.shape[0]):
        values = first_ref[at:to].astype(FULL) + (chip_ref[at:to] + far_ref[at:to].astype(FULL)) + rows_ref[3:4]
        output, normed, scale_inv = moments(values, rows_ref[6:7], rows_ref[7:8])
        if to <= own:
            upstream = cotangent_ref[at:to].astype(FULL)
            output_ref[at:to] = output.astype(LOW)
        else:
            upstream = cotangent_far_ref[at - own : to - own].astype(FULL)
        grad = norm_backward(upstream, normed, scale_inv, rows_ref[6:7])
        low = grad.astype(LOW)
        low_ref[at:to] = low
        if to <= own:
            for i, part in enumerate((low.astype(FULL), upstream * normed, upstream)):
                sums[i] += jnp.sum(part, axis=0, keepdims=True)
    sums_ref[...] = jnp.concatenate(sums + [jnp.zeros((5, sums[0].shape[1]), FULL)], axis=0)


def feed_backward_kernel(rows_ref, up_ref, down_ref, slope_ref, grad_ref, part_ref, sum_ref):
    size = rows_ref.shape[0] // 2
    total = jnp.zeros((1, up_ref.shape[1]), FULL)
    for at, to in blocks_of(rows_ref.shape[0], size):
        grad = jnp.dot(rows_ref[at:to], down_ref[...], preferred_element_type=FULL)
        for low, high in blocks_of(size, 32):
            place = slice(at + low, at + high)
            part = (grad[low:high] * slope_ref[place]).astype(LOW)
            grad_ref[place] = part
            total += jnp.sum(part.astype(FULL), axis=0, keepdims=True)
        got = contract(grad_ref[at:to], up_ref[...], 1, 1)
        part_ref[at:to] = got.astype(part_ref.dtype)
    sum_ref[...] = total


def feed_weights_kernel(
    hidden_near,
    hidden_other,
    branch_near,
    branch_other,
    active_near,
    active_other,
    grad_near,
    grad_other,
    out,
    out_ref,
    sems,
):
    count, rows, wide = out_ref.shape
    rows = rows // 2
    hidden = wide // 2
    copies = []
    for place, near, other, right_near, right_other in (
        (0, hidden_near, hidden_other, grad_near, grad_other),
        (hidden, branch_near, branch_other, active_near, active_other),
    ):
        got = contract(near[...], right_near[...], 0, 0) + contract(
            other[...], right_other[...], 0, 0
        )
        for at in range(count):
            out_ref[at, :, place : place + hidden] = jnp.concatenate(
                [got[at * rows : (at + 1) * rows], got[(count + at) * rows :][:rows]], axis=0
            ).astype(LOW)
        half = pl.ds(place, hidden)
        copy = pltpu.make_async_copy(
            out_ref.at[:, :, half], out.at[:, :, half], sems.at[place // hidden]
        )
        copy.start()
        copies.append(copy)
    for copy in copies:
        copy.wait()


def first_norm_backward_kernel(
    second_ref,
    chip_ref,
    far_ref,
    first_ref,
    scale_ref,
    rows_ref,
    second_sums_ref,
    grad_ref,
    low_ref,
    sums_ref,
):
    own = grad_ref.shape[0]
    sums = [jnp.zeros((1, second_ref.shape[1]), FULL) for _ in range(3)]
    inverse = 1.0 / rows_ref[4:5]
    for at, to in blocks_of(second_ref.shape[0], TILE):
        upstream = second_ref[at:to].astype(FULL) + (
            chip_ref[at:to] + far_ref[at:to].astype(FULL)
        )
        normed = (first_ref[at:to].astype(FULL) - rows_ref[5:6]) * inverse
        scale_inv = jnp.transpose(jnp.broadcast_to(scale_ref[:1, at:to], (TILE, TILE)))[:, :1]
        grad = norm_backward(upstream, normed, scale_inv, rows_ref[4:5])
        low = grad.astype(LOW)
        low_ref[at:to] = low
        if to <= own:
            grad_ref[at:to] = grad
            for i, part in enumerate((low.astype(FULL), upstream * normed, upstream)):
                sums[i] += jnp.sum(part, axis=0, keepdims=True)
    given = second_sums_ref[...]
    sums_ref[...] = jnp.concatenate(
        [
            sums[0],
            given[0:1],
            sums[1],
            sums[2],
            given[1:3],
            jnp.zeros((2, sums[0].shape[1]), FULL),
        ],
        axis=0,
    )


def plane_sum_kernel(index_ref, blocks_ref, keep_ref, send_ref):
    rows = keep_ref.shape[0]
    total = blocks_ref[0].astype(FULL)
    for at in range(1, blocks_ref.shape[0]):
        total += blocks_ref[at].astype(FULL)
    lower = index_ref[0] == 0
    keep_ref[...] = jnp.where(lower, total[:rows], total[rows:])
    send_ref[...] = jnp.where(lower, total[rows:], total[:rows]).astype(send_ref.dtype)


def last_sum_kernel(index_ref, blocks_ref, q_ref, k_ref, v_ref, out_ref, vector_ref):
    index = index_ref[0]
    rows = q_ref.shape[0]
    vector_rows = rows // 4
    columns = q_ref.shape[1]
    total = blocks_ref[0].astype(FULL)
    for at in range(1, blocks_ref.shape[0]):
        total += blocks_ref[at].astype(FULL)
    q_ref[...] = total[:, :columns]
    k_ref[...] = total[:, GROUP : GROUP + columns]
    v_ref[...] = total[:, 2 * GROUP : 2 * GROUP + columns]
    out_ref[...] = jnp.concatenate(
        [total[:, GROUP * i + columns : GROUP * (i + 1)] for i in range(3)], axis=1
    )
    packed = total[:, 3 * GROUP :]
    packed = packed + pltpu.roll(packed, TILE - 12, 1)
    wide = vector_ref.shape[1]
    _, place_column = place_of(vector_rows, (TILE, wide), 1)
    select = jnp.where(place_column == lanes((TILE, wide), 0), 1.0, 0.0).astype(LOW)
    line = jnp.zeros((rows, wide), FULL)
    left = packed
    for _ in range(3):
        part = left.astype(LOW)
        left = left - part.astype(FULL)
        line += jnp.dot(part, select, preferred_element_type=FULL)
    place_row, _ = place_of(vector_rows, (rows, wide), 1)
    keep = place_row + index * vector_rows == lanes((rows, wide), 0)
    vector_ref[...] = jnp.sum(jnp.where(keep, line, 0.0), axis=0, keepdims=True)


def shards(
    tokens,
    segments,
    q_weight,
    k_weight,
    v_weight,
    up_weight,
    out_weight,
    down_weight,
    q_bias,
    v_bias,
    out_bias,
    up_bias,
    down_bias,
    norm1_gain,
    norm1_shift,
    norm2_gain,
    norm2_shift,
    cotangent,
):
    my_index = lax.axis_index("tensor")
    dp_count = lax.axis_size("dp")
    local_len, width = tokens.shape[1:]
    half = 2 * local_len
    length = 4 * local_len
    shard_rows, head_cols = q_weight.shape
    hidden_cols = up_weight.shape[1]
    tokens = tokens[0]
    cotangent = cotangent[0]
    index = my_index.reshape(1)
    side_index = (lax.axis_index("dp") // (dp_count // 2)).reshape(1)

    vector_rows = q_bias.shape[0]
    line_size = -(-12 * vector_rows // TILE) * TILE
    first_own = jnp.concatenate([q_weight, k_weight, v_weight, out_weight], axis=1)
    second_own = jnp.concatenate([up_weight, down_weight], axis=1)
    line = jnp.concatenate(
        [
            after(q_bias, first_own, second_own),
            v_bias,
            out_bias,
            down_bias,
            norm1_gain,
            norm1_shift,
            norm2_gain,
            norm2_shift,
            up_bias,
            jnp.zeros((line_size - 12 * vector_rows,), FULL),
        ]
    )[None]
    lines = [line] + [swap(line, mask) for mask in (1, 2, 3)]
    tokens_far = swap(tokens, 2)
    second_side = side(second_own)
    first_own, tokens_far, second_side = lax.optimization_barrier(
        (first_own, tokens_far, second_side)
    )
    (first_block,) = call(
        first_block_kernel,
        [((dp_count, shard_rows, 3 * GROUP + TILE), LOW)],
        index,
        *lines,
        first_own,
        smem=1,
    )
    first_full = spread(first_block).reshape(width, -1)
    tokens_pair = jnp.concatenate([tokens, tokens_far], axis=0)
    tokens_core = swap(tokens_pair, 1)
    segment_row = ordered_segments(segments[0], my_index)[None]
    (second_block,) = call(
        second_block_kernel,
        [((dp_count // 2, 2 * shard_rows, 2 * hidden_cols), LOW)],
        side_index,
        second_own,
        second_side,
        smem=1,
    )
    first_full, second_block, tokens_core, segment_row = lax.optimization_barrier(
        (first_full, second_block, tokens_core, segment_row)
    )
    second_full = plane(second_block)

    qkv_rows, mixed_rows, log_totals, attn_send, attn_keep, rows, bias_up = call(
        forward_kernel,
        [
            ((length, 3 * GROUP), LOW),
            ((length, GROUP), LOW),
            ((8, length), FULL),
            ((half, width), LOW),
            ((half, width), FULL),
            ((8, width), FULL),
            ((1, hidden_cols), FULL),
        ],
        index,
        tokens_pair,
        tokens_core,
        first_full,
        segment_row,
        smem=1,
        scratch=[pltpu.VMEM((length, 3 * GROUP), LOW), pltpu.SemaphoreType.DMA],
        away=(0,),
    )
    attn_chip = attn_keep + swap(attn_send, 1).astype(FULL)
    attn_far = swap(far_pack(attn_chip), 2)
    cotangent_far = swap(after(cotangent, attn_far), 2)
    hidden_low, inv_first = call(
        first_norm_kernel,
        [((half, width), LOW), ((8, half), FULL)],
        tokens_pair,
        attn_chip,
        attn_far,
        rows,
    )
    hidden_core = after(swap(hidden_low, 1), cotangent_far)
    active_other, slope_other, branch_send, up_full, down_full = call(
        feed_other_kernel,
        [
            ((half, hidden_cols), LOW),
            ((half, hidden_cols), FULL),
            ((half, width), LOW),
            ((width, hidden_cols), LOW),
            ((width, hidden_cols), LOW),
        ],
        hidden_core,
        second_full,
        bias_up,
    )
    branch_got = swap(branch_send, 1)
    active_near, slope_near, branch_keep = call(
        feed_near_kernel,
        [((half, hidden_cols), LOW), ((half, hidden_cols), FULL), ((half, width), FULL)],
        hidden_low,
        up_full,
        down_full,
        bias_up,
    )
    branch_chip = branch_keep + branch_got.astype(FULL)
    layer_output, branch_low, second_sums = call(
        second_norm_kernel,
        [((local_len, width), LOW), ((half, width), LOW), ((8, width), FULL)],
        hidden_low,
        branch_chip,
        swap(far_pack(branch_chip), 2),
        rows,
        cotangent,
        cotangent_far,
    )
    branch_core = swap(branch_low, 1)
    grad_shapes = [((half, hidden_cols), LOW), ((half, width), LOW), ((1, hidden_cols), FULL)]
    upward_other, hidden_send, up_sum_other = call(
        feed_backward_kernel, grad_shapes, branch_core, up_full, down_full, slope_other
    )
    hidden_got = swap(hidden_send, 1)
    grad_shapes[1] = ((half, width), FULL)
    upward_near, hidden_keep, up_sum_near = call(
        feed_backward_kernel, grad_shapes, branch_low, up_full, down_full, slope_near
    )
    hidden_chip = hidden_keep + hidden_got.astype(FULL)
    hidden_sent = far_pack(hidden_chip)
    hidden_far = swap(hidden_sent, 2)
    (pair_block,) = call(
        feed_weights_kernel,
        [((dp_count // 2, 2 * shard_rows, 2 * hidden_cols), LOW)],
        hidden_low,
        hidden_core,
        branch_low,
        branch_core,
        active_near,
        active_other,
        upward_near,
        upward_other,
        scratch=[
            pltpu.VMEM((dp_count // 2, 2 * shard_rows, 2 * hidden_cols), LOW),
            pltpu.SemaphoreType.DMA((2,)),
        ],
        away=(0,),
    )
    pair_blocks = plane(pair_block)
    resid_grad, attended_low, given = call(
        first_norm_backward_kernel,
        [((local_len, width), FULL), ((half, width), LOW), ((8, width), FULL)],
        branch_low,
        hidden_chip,
        hidden_far,
        hidden_low,
        inv_first,
        rows,
        second_sums,
    )
    attended_core = swap(attended_low, 1)
    qkv_grad, input_send, input_keep, vector_sums = call(
        backward_kernel,
        [
            ((length, 3 * GROUP), LOW),
            ((half, width), LOW),
            ((half, width), FULL),
            ((16, width), FULL),
        ],
        index,
        attended_low,
        attended_core,
        qkv_rows,
        log_totals,
        first_full,
        segment_row,
        given,
        up_sum_near,
        up_sum_other,
        smem=1,
        scratch=[
            pltpu.VMEM((length, GROUP), LOW),
            pltpu.VMEM((length, TILE), FULL),
            pltpu.VMEM((length, TILE), FULL),
            pltpu.VMEM((width, TILE), FULL),
        ],
    )
    input_chip = input_keep + swap(input_send, 1).astype(FULL)
    input_sent = input_chip[local_len:].astype(LOW)
    input_far = swap(input_sent, 2)
    vector_near = [swap(vector_sums, mask) for mask in (1, 2, 3)]
    (last_block,) = call(
        weights_kernel,
        [((width, 3 * GROUP + TILE), LOW)],
        tokens_pair,
        tokens_core,
        attended_low,
        attended_core,
        qkv_grad,
        mixed_rows,
        scratch=[pltpu.VMEM((width, 3 * GROUP), LOW), pltpu.SemaphoreType.DMA],
        away=(0,),
    )
    (last_block,) = call(
        vectors_kernel,
        [((width, 3 * GROUP + TILE), LOW)],
        last_block,
        vector_sums,
        *vector_near,
        scratch=[pltpu.VMEM((width, TILE), LOW), pltpu.SemaphoreType.DMA],
        away=(0,),
        far=(0,),
        aliases={0: 0},
    )
    last_block = after(last_block, input_far)
    last_blocks = spread(last_block.reshape(dp_count, shard_rows, 3 * GROUP + TILE))
    input_grad = resid_grad + (input_chip[:local_len] + input_far.astype(FULL))

    pair_keep, pair_send = call(
        plane_sum_kernel,
        [((shard_rows, 2 * hidden_cols), FULL), ((shard_rows, 2 * hidden_cols), LOW)],
        side_index,
        pair_blocks,
        smem=1,
    )
    pair_sum = pair_keep + side(pair_send).astype(FULL)
    q_grad, k_grad, v_grad, out_grad, line = call(
        last_sum_kernel,
        [((shard_rows, head_cols), FULL)] * 4 + [((1, line_size), FULL)],
        index,
        last_blocks,
        smem=1,
    )
    line = line[0]
    vectors = [line[vector_rows * i : vector_rows * (i + 1)] for i in range(8)]
    return (
        layer_output[None],
        input_grad[None],
        q_grad,
        k_grad,
        v_grad,
        pair_sum[:, :hidden_cols],
        out_grad,
        pair_sum[:, hidden_cols:],
        vectors[6],
        vectors[7],
        vectors[0],
        line[8 * vector_rows : 12 * vector_rows],
        vectors[1],
        vectors[2],
        vectors[3],
        vectors[4],
        vectors[5],
    )


def solution(mesh):
    matrix = P("dp", "tensor")
    vector = P(("dp", "tensor"))
    rows = P("dp", "tensor", None)
    return jax.shard_map(
        shards,
        mesh=mesh,
        in_specs=(rows, P("dp", None)) + (matrix,) * 6 + (vector,) * 9 + (rows,),
        out_specs=(rows, rows) + (matrix,) * 6 + (vector,) * 9,
        check_vma=False,
    )
```

```python
import functools

import jax
import jax.numpy as jnp
from jax import lax
from jax.experimental import pallas as pl
from jax.experimental.pallas import tpu as pltpu
from jax.sharding import PartitionSpec as P

HEAD_DIM = 64
TILE = 128
GROUP = 256


NORM_EPSILON = 1e-12
MASKED_SCORE = -1000000000.0
ROOT_HALF = 0.7071067811865476
INV_ROOT_TAU = 0.3989422804014327
LOW = jnp.bfloat16
FULL = jnp.float32
VMEM_LIMIT = 48 * 1024 * 1024


def contract(left, right, left_dim, right_dim):
    return lax.dot_general(
        left, right, (((left_dim,), (right_dim,)), ((), ())), preferred_element_type=jnp.float32
    )


def swap(values, mask):
    return lax.ppermute(values, "tensor", [(i, i ^ mask) for i in range(4)])


def after(values, *others):
    return lax.optimization_barrier((values, *others))[0]


def spread(stacked):
    return lax.all_to_all(stacked, "dp", 0, 0, tiled=True)


def plane_groups():
    count = lax.axis_size("dp") // 2
    return [list(range(count)), list(range(count, 2 * count))]


def plane(stacked):
    return lax.all_to_all(stacked, "dp", 0, 0, tiled=True, axis_index_groups=plane_groups())


def side(values):
    count = lax.axis_size("dp")
    pairs = [(i, (i + count // 2) % count) for i in range(count)]
    return lax.ppermute(values, "dp", pairs)


def halves(values):
    high = lax.reduce_precision(values, 8, 7)
    return (high.astype(LOW), (values - high).astype(LOW))


def far_pack(total):
    quarter = total.shape[0] // 2
    sent = total.astype(LOW)
    return jnp.concatenate([sent[quarter:], sent[:quarter]], axis=0)


def ordered_segments(segment_row, my_index):
    quarters = segment_row.reshape(4, -1)
    core = my_index % 2 == 1
    quarters = jnp.where(core, quarters[jnp.array([1, 0, 3, 2])], quarters)
    far = my_index // 2 == 1
    quarters = jnp.where(far, quarters[jnp.array([2, 3, 0, 1])], quarters)
    return jnp.concatenate([quarters[0], quarters[2], quarters[1], quarters[3]])


def call(body, out_shapes, *operands, smem=0, scratch=(), away=(), far=(), aliases=None):
    specs = [pl.BlockSpec(memory_space=pltpu.SMEM)] * smem
    specs += [
        pl.BlockSpec(memory_space=pltpu.HBM if i in far else pltpu.VMEM)
        for i in range(smem, len(operands))
    ]
    return pl.pallas_call(
        body,
        out_shape=[
            pltpu.HBM(shape, kind) if i in away else jax.ShapeDtypeStruct(shape, kind)
            for i, (shape, kind) in enumerate(out_shapes)
        ],
        in_specs=specs,
        out_specs=[
            pl.BlockSpec(memory_space=pltpu.HBM if i in away else pltpu.VMEM)
            for i in range(len(out_shapes))
        ],
        input_output_aliases=aliases or {},
        scratch_shapes=list(scratch),
        compiler_params=pltpu.CompilerParams(vmem_limit_bytes=VMEM_LIMIT),
        cost_estimate=pl.CostEstimate(flops=1000, bytes_accessed=1000, transcendentals=0),
    )(*operands)


def lanes(shape, dim=1):
    return lax.broadcasted_iota(jnp.int32, shape, dim)


def head_tile(head):
    return head // 2


def head_mask(head, shape, dim=1):
    index = lanes(shape, dim)
    return index >= HEAD_DIM if head % 2 else index < HEAD_DIM


def only(values, mask):
    return jnp.where(mask, values, jnp.zeros_like(values))


def packed_out(weight_ref):
    rows = weight_ref.shape[0]
    parts = [
        weight_ref[:, GROUP * i + TILE : GROUP * (i + 1)].astype(FULL) for i in range(3)
    ]
    low = head_mask(0, (rows, TILE))
    first = jnp.where(low, pltpu.roll(parts[0], HEAD_DIM, 1), parts[1])
    second = jnp.where(low, pltpu.roll(parts[2], HEAD_DIM, 1), 0.0)
    return jnp.concatenate([first, second], axis=1).astype(LOW)


def lined_heads(rows):
    first, second = rows[:, :TILE], rows[:, TILE:]
    return [pltpu.roll(first, HEAD_DIM, 1), first, pltpu.roll(second, HEAD_DIM, 1)]


def transposed(values):
    return jnp.transpose(values.astype(FULL))


def expand_matrix(count):
    shape = (count, 4 * count)
    return jnp.where(lanes(shape) // 4 == lanes(shape, 0), 1.0, 0.0).astype(LOW)


def unpack_lines(index, line_refs, vector_ref, columns, width):
    devices, size = line_refs[0].shape[1:]
    each = width // (4 * devices)
    flipped = []
    for part in range(2):
        near = [ref[part].astype(FULL) for ref in line_refs]
        ordered = []
        for at in range(4):
            row = near[3]
            for mask in (2, 1, 0):
                row = jnp.where((index ^ mask) == at, near[mask], row)
            ordered.append(row)
        flipped.append(jnp.transpose(jnp.concatenate(ordered, axis=0)).astype(LOW))

    def spread_lines(place, valid):
        shape = (4 * devices, place.shape[1])
        row = lanes(shape, 0)
        select = (row % devices == place // (4 * each)) & (
            row // devices == place % (4 * each) // each
        )
        select = jnp.where(select & valid, 1.0, 0.0).astype(LOW)
        return [jnp.dot(part, select, preferred_element_type=FULL) for part in flipped]

    def vectors_at(place, valid):
        line_at = lanes((size, place.shape[1]), 0)
        keep = (line_at < 8 * each) & (line_at % each == place % each)
        row = lanes((8, size), 0)
        gather = jnp.where(lanes((8, size)) // each == row, 1.0, 0.0).astype(LOW)
        total = jnp.zeros((8, place.shape[1]), FULL)
        for part in spread_lines(place, valid):
            part = jnp.where(keep, part, 0.0).astype(LOW)
            total += jnp.dot(gather, part, preferred_element_type=FULL)
        return total

    place = lanes((1, width))
    vector_ref[...] = vectors_at(place, place >= 0)
    place = lanes((1, GROUP))
    own = vectors_at(place + index * columns, place < columns)
    bias = jnp.concatenate([own[0:1], jnp.zeros((1, GROUP), FULL), own[1:2]], axis=1)
    place = lanes((1, 4 * columns)) + index * (4 * columns)
    line_at = lanes((size, 4 * columns), 0)
    keep = line_at == 8 * each + place % (4 * each)
    up_bias = jnp.zeros((1, 4 * columns), FULL)
    for part in spread_lines(place // 4, place >= 0):
        up_bias += jnp.sum(jnp.where(keep, part, 0.0), axis=0, keepdims=True)
    return (bias, up_bias)


def forward_kernel(
    index_ref,
    near_ref,
    other_ref,
    weight_ref,
    segment_ref,
    line_ref,
    line_core_ref,
    line_far_ref,
    line_both_ref,
    qkv_out,
    mixed_ref,
    log_ref,
    send_ref,
    keep_ref,
    vector_ref,
    up_bias_ref,
    qkv_ref,
    qkv_sem,
):
    index = index_ref[0]
    half = near_ref.shape[0]
    columns = 3 * HEAD_DIM
    line_refs = (line_ref, line_core_ref, line_far_ref, line_both_ref)
    width = weight_ref.shape[0]
    width = weight_ref.shape[0]
    bias, up_bias = unpack_lines(index, line_refs, vector_ref, columns, width)
    up_bias_ref[...] = up_bias
    keep = lanes((1, 3 * GROUP)) % GROUP < columns
    for at, rows_ref in ((0, near_ref), (half, other_ref)):
        got = jnp.dot(rows_ref[...], weight_ref[:, : 3 * GROUP], preferred_element_type=FULL)
        qkv_ref[at : at + half, :] = jnp.where(keep, got + bias, 0.0).astype(LOW)
    qkv_copy = pltpu.make_async_copy(qkv_ref, qkv_out, qkv_sem)
    qkv_copy.start()

    length = 2 * half
    row_segments = segment_ref[...]
    column_segments = jnp.transpose(
        jnp.broadcast_to(row_segments.astype(FULL), (TILE, length))
    )[:, :1].astype(jnp.int32)
    same = column_segments == row_segments
    mixed_tiles = [None, None]
    for head in range(3):
        at = TILE * head_tile(head)
        mask = head_mask(head, (length, TILE))
        key = only(qkv_ref[:, GROUP + at : GROUP + at + TILE], mask) * jnp.asarray(0.125, LOW)
        scores = contract(key, qkv_ref[:, at : at + TILE], 1, 1)
        scores = jnp.where(same, scores, MASKED_SCORE)
        highest = jnp.max(scores, axis=0, keepdims=True)
        shifted = jnp.exp(scores - highest)
        total = jnp.sum(shifted, axis=0, keepdims=True)
        probs = (shifted * (1.0 / total)).astype(LOW)
        log_ref[head : head + 1, :] = highest + jnp.log(total)
        value = only(qkv_ref[:, 2 * GROUP + at : 2 * GROUP + at + TILE], mask)
        got = jnp.dot(transposed(value).astype(LOW), probs, preferred_element_type=FULL)
        tile = head_tile(head)
        mixed_tiles[tile] = got if mixed_tiles[tile] is None else mixed_tiles[tile] + got
    log_ref[3:, :] = jnp.zeros((5, length), FULL)
    for tile in range(2):
        mixed_ref[:, TILE * tile : TILE * (tile + 1)] = jnp.transpose(mixed_tiles[tile]).astype(LOW)
    out = packed_out(weight_ref)
    keep_ref[...] = contract(mixed_ref[:half, :], out, 1, 1)
    send_ref[...] = contract(mixed_ref[half:, :], out, 1, 1).astype(LOW)
    qkv_copy.wait()


def backward_kernel(
    index_ref,
    near_ref,
    other_ref,
    qkv_ref,
    log_ref,
    weight_ref,
    segment_ref,
    sums_ref,
    up_sum_ref,
    up_sum_other_ref,
    grad_ref,
    send_ref,
    keep_ref,
    vector_ref,
    mixed_grad,
    key_grad,
    value_grad,
    columns_held,
):
    index = index_ref[0]
    half = near_ref.shape[0]
    length = 2 * half
    columns = 3 * HEAD_DIM
    out = packed_out(weight_ref)
    mixed_grad[:half, :] = jnp.dot(near_ref[...], out, preferred_element_type=FULL).astype(LOW)
    mixed_grad[half:, :] = jnp.dot(other_ref[...], out, preferred_element_type=FULL).astype(LOW)
    row_segments = segment_ref[...]
    column_segments = jnp.transpose(
        jnp.broadcast_to(row_segments.astype(FULL), (TILE, length))
    )[:, :1].astype(jnp.int32)
    same = column_segments == row_segments
    sums = []
    for tile in range(2):
        at = TILE * tile
        query_grad = jnp.zeros((TILE, length), FULL)
        for head in (0, 1) if tile == 0 else (2,):
            mask = head_mask(head, (length, TILE))
            scale = jnp.asarray(0.125, LOW)
            key = only(qkv_ref[:, GROUP + at : GROUP + at + TILE], mask) * scale
            query = only(qkv_ref[:, at : at + TILE], mask)
            value = only(qkv_ref[:, 2 * GROUP + at : 2 * GROUP + at + TILE], mask)
            grad = only(mixed_grad[:, at : at + TILE], mask)
            scores = contract(key, query, 1, 1)
            probs = jnp.exp(
                jnp.where(same, scores, MASKED_SCORE) - log_ref[head : head + 1, :]
            )
            probs_grad = contract(value, grad, 1, 1)
            inner = jnp.sum(probs * probs_grad, axis=0, keepdims=True)
            scores_grad = (probs * (probs_grad - inner)).astype(LOW)
            got = jnp.dot(probs.astype(LOW), grad, preferred_element_type=FULL)
            got_key = jnp.dot(scores_grad, query * scale, preferred_element_type=FULL)
            if head % 2 == 0:
                value_grad[...] = got
                key_grad[...] = got_key
            else:
                value_grad[...] += got
                key_grad[...] += got_key
            query_grad += jnp.dot(
                transposed(key).astype(LOW), scores_grad, preferred_element_type=FULL
            )
        query_low = jnp.transpose(query_grad).astype(LOW)
        value_low = value_grad[...].astype(LOW)
        grad_ref[:, at : at + TILE] = query_low
        grad_ref[:, GROUP + at : GROUP + at + TILE] = key_grad[...].astype(LOW)
        grad_ref[:, 2 * GROUP + at : 2 * GROUP + at + TILE] = value_low
        sums.append(
            (
                jnp.sum(query_low.astype(FULL), axis=0, keepdims=True),
                jnp.sum(value_low.astype(FULL), axis=0, keepdims=True),
            )
        )
    wide = weight_ref[:, : 3 * GROUP]
    keep_ref[...] = contract(grad_ref[:half, :], wide, 1, 1)
    send_ref[...] = contract(grad_ref[half:, :], wide, 1, 1).astype(LOW)

    up_row = up_sum_ref[...] + up_sum_other_ref[...]
    place = lanes((8, 4 * columns))
    spaced = jnp.where(place % 4 == lanes((8, 4 * columns), 0), up_row, 0.0)
    high = spaced.astype(LOW)
    low = (spaced - high.astype(FULL)).astype(LOW)
    expand = expand_matrix(columns)
    up_rows = contract(high, expand, 1, 1) + contract(low, expand, 1, 1)
    up_rows = jnp.concatenate([up_rows, jnp.zeros((8, GROUP - columns), FULL)], axis=1)
    query_sum = jnp.concatenate([sums[0][0], sums[1][0]], axis=1)
    value_sum = jnp.concatenate([sums[0][1], sums[1][1]], axis=1)
    at_row = lanes((8, GROUP), 0)
    late = jnp.where(at_row == 6, query_sum, jnp.where(at_row == 7, value_sum, 0.0))
    stacked = jnp.concatenate([late, up_rows, jnp.zeros((TILE - 16, GROUP), FULL)], axis=0)
    columns_held[...] = jnp.zeros_like(columns_held)
    columns_held[pl.ds(pl.multiple_of(index * columns, 64), columns), :] = jnp.transpose(stacked)[
        :columns
    ]
    placed = jnp.transpose(columns_held[...])[:16]
    given = sums_ref[...]
    vector_ref[:8, :] = placed[:8] + given
    vector_ref[8:, :] = placed[8:]


def weights_kernel(
    tokens_near, tokens_other, near_ref, other_ref, grad_ref, mixed_ref, out, out_ref, sem
):
    half = near_ref.shape[0]
    width = near_ref.shape[1]
    got = contract(tokens_near[...], grad_ref[:half, :], 0, 0) + contract(
        tokens_other[...], grad_ref[half:, :], 0, 0
    )
    out_grad = contract(near_ref[...], mixed_ref[:half, :], 0, 0) + contract(
        other_ref[...], mixed_ref[half:, :], 0, 0
    )
    high = head_mask(1, (width, TILE))
    for part, lined in enumerate(lined_heads(out_grad)):
        at = GROUP * part
        out_ref[:, at : at + TILE] = got[:, at : at + TILE].astype(LOW)
        out_ref[:, at + TILE : at + GROUP] = jnp.where(
            high, lined, got[:, at + TILE : at + GROUP]
        ).astype(LOW)
    copy = pltpu.make_async_copy(out_ref, out.at[:, : 3 * GROUP], sem)
    copy.start()
    copy.wait()


def vectors_kernel(block_ref, own_ref, core_ref, far_ref, both_ref, out_ref, held, sem):
    total = own_ref[...] + core_ref[...] + (far_ref[...] + both_ref[...])
    total = total[:12]
    high = total.astype(LOW).astype(FULL)
    rows = jnp.concatenate(
        [high, total - high, jnp.zeros((TILE - 24, total.shape[1]), FULL)], axis=0
    )
    held[...] = jnp.transpose(rows).astype(LOW)
    copy = pltpu.make_async_copy(held, out_ref.at[:, 3 * GROUP :], sem)
    copy.start()
    copy.wait()


def place_of(vector_rows, shape, dim):
    place = lanes(shape, dim)
    many = 8 * vector_rows
    row = jnp.where(place < many, place % vector_rows, (place - many) // 4)
    column = jnp.where(place < many, place // vector_rows, 8 + (place - many) % 4)
    return (row, jnp.where(place < many + 4 * vector_rows, column, 1000))


def first_block_kernel(line_ref, weight_ref, block_ref):
    rows = weight_ref.shape[0]
    columns_each = weight_ref.shape[1] // 4
    count = line_ref.shape[0]
    row_at = lanes((rows, TILE), 0)
    packed = jnp.zeros((rows, TILE), FULL)
    for at in range(count):
        line = line_ref[at : at + 1]
        high = line.astype(LOW).astype(FULL)
        packed = jnp.where(row_at == at, high, packed)
        packed = jnp.where(row_at == count + at, line - high, packed)
    weight = weight_ref[...].astype(FULL)
    q_part, k_part, v_part, out = [
        weight[:, columns_each * i : columns_each * (i + 1)] for i in range(4)
    ]
    block = jnp.concatenate(
        [
            q_part,
            out[:, :HEAD_DIM],
            k_part,
            out[:, HEAD_DIM : 2 * HEAD_DIM],
            v_part,
            out[:, 2 * HEAD_DIM :],
            packed,
        ],
        axis=1,
    ).astype(LOW)
    for at in range(block_ref.shape[0]):
        block_ref[at] = block


def second_block_kernel(index_ref, own_ref, other_ref, block_ref):
    lower = index_ref[0] == 0
    own = own_ref[...].astype(FULL)
    other = other_ref[...].astype(FULL)
    block = jnp.concatenate(
        [jnp.where(lower, own, other), jnp.where(lower, other, own)], axis=0
    ).astype(LOW)
    for at in range(block_ref.shape[0]):
        block_ref[at] = block


def moments(values, gain, shift):
    center = values - jnp.mean(values, axis=-1, keepdims=True)
    scale_inv = lax.rsqrt(jnp.mean(center * center, axis=-1, keepdims=True) + NORM_EPSILON)
    normed = center * scale_inv
    return (normed * gain + shift, normed, scale_inv)


def norm_backward(upstream, normed, scale_inv, gain):
    scaled = upstream * gain
    return scale_inv * (
        scaled
        - jnp.mean(scaled, axis=-1, keepdims=True)
        - normed * jnp.mean(scaled * normed, axis=-1, keepdims=True)
    )


def blocks_of(rows, size=64):
    return [(at, at + size) for at in range(0, rows, size)]


def first_norm_kernel(tokens_ref, chip_ref, far_ref, rows_ref, low_ref, scale_ref):
    for at, to in blocks_of(tokens_ref.shape[0], TILE):
        values = (
            tokens_ref[at:to].astype(FULL)
            + (chip_ref[at:to] + far_ref[at:to].astype(FULL))
            + rows_ref[2:3]
        )
        first, _, scale_inv = moments(values, rows_ref[4:5], rows_ref[5:6])
        low_ref[at:to] = first.astype(LOW)
        scale_ref[:, at:to] = jnp.transpose(jnp.broadcast_to(scale_inv, (TILE, TILE)))[:8]


def feed_rows(rows_ref, up, down, bias_ref, active_ref, slope_ref, part_ref):
    size = rows_ref.shape[0] // 2
    for at, to in blocks_of(rows_ref.shape[0], size):
        upward = jnp.dot(rows_ref[at:to], up[...], preferred_element_type=FULL) + bias_ref[...]
        for low, high in blocks_of(size, 32):
            part = upward[low:high]
            gate = 0.5 * (1.0 + lax.erf(part * ROOT_HALF))
            active_ref[at + low : at + high] = (part * gate).astype(LOW)
            slope_ref[at + low : at + high] = (
                gate + part * jnp.exp(-0.5 * part * part) * INV_ROOT_TAU
            ).astype(LOW)
        got = contract(active_ref[at:to], down[...], 1, 1)
        part_ref[at:to] = got.astype(part_ref.dtype)


def feed_other_kernel(
    rows_ref, blocks_ref, bias_ref, active_ref, slope_ref, part_ref, up_ref, down_ref
):
    count, rows, wide = blocks_ref.shape
    rows = rows // 2
    hidden = wide // 2
    group = 1 if rows % 16 == 0 else 2
    for lower in range(2):
        for at in range(0, count, group):
            got = jnp.concatenate(
                [
                    blocks_ref[at + i].astype(FULL)[rows * lower : rows * (lower + 1)]
                    for i in range(group)
                ],
                axis=0,
            ).astype(LOW)
            to = (lower * count + at) * rows
            up_ref[to : to + group * rows] = got[:, :hidden]
            down_ref[to : to + group * rows] = got[:, hidden:]
    feed_rows(rows_ref, up_ref, down_ref, bias_ref, active_ref, slope_ref, part_ref)


def feed_near_kernel(rows_ref, up_ref, down_ref, bias_ref, active_ref, slope_ref, part_ref):
    feed_rows(rows_ref, up_ref, down_ref, bias_ref, active_ref, slope_ref, part_ref)


def second_norm_kernel(
    first_ref,
    chip_ref,
    far_ref,
    rows_ref,
    cotangent_ref,
    cotangent_far_ref,
    output_ref,
    low_ref,
    sums_ref,
):
    own = output_ref.shape[0]
    sums = [jnp.zeros((1, first_ref.shape[1]), FULL) for _ in range(3)]
    for at, to in blocks_of(first_ref.shape[0]):
        values = first_ref[at:to].astype(FULL) + (chip_ref[at:to] + far_ref[at:to].astype(FULL)) + rows_ref[3:4]
        output, normed, scale_inv = moments(values, rows_ref[6:7], rows_ref[7:8])
        if to <= own:
            upstream = cotangent_ref[at:to].astype(FULL)
            output_ref[at:to] = output.astype(LOW)
        else:
            upstream = cotangent_far_ref[at - own : to - own].astype(FULL)
        grad = norm_backward(upstream, normed, scale_inv, rows_ref[6:7])
        low = grad.astype(LOW)
        low_ref[at:to] = low
        if to <= own:
            for i, part in enumerate((low.astype(FULL), upstream * normed, upstream)):
                sums[i] += jnp.sum(part, axis=0, keepdims=True)
    sums_ref[...] = jnp.concatenate(sums + [jnp.zeros((5, sums[0].shape[1]), FULL)], axis=0)


def feed_backward_kernel(rows_ref, up_ref, down_ref, slope_ref, grad_ref, part_ref, sum_ref):
    size = rows_ref.shape[0] // 2
    total = jnp.zeros((1, up_ref.shape[1]), FULL)
    for at, to in blocks_of(rows_ref.shape[0], size):
        grad = jnp.dot(rows_ref[at:to], down_ref[...], preferred_element_type=FULL)
        for low, high in blocks_of(size, 32):
            place = slice(at + low, at + high)
            part = (grad[low:high] * slope_ref[place].astype(FULL)).astype(LOW)
            grad_ref[place] = part
            total += jnp.sum(part.astype(FULL), axis=0, keepdims=True)
        got = contract(grad_ref[at:to], up_ref[...], 1, 1)
        part_ref[at:to] = got.astype(part_ref.dtype)
    sum_ref[...] = total


def feed_weights_kernel(
    hidden_near,
    hidden_other,
    branch_near,
    branch_other,
    active_near,
    active_other,
    grad_near,
    grad_other,
    out,
    out_ref,
    sems,
):
    count, rows, wide = out_ref.shape
    rows = rows // 2
    hidden = wide // 2
    copies = []
    for place, near, other, right_near, right_other in (
        (0, hidden_near, hidden_other, grad_near, grad_other),
        (hidden, branch_near, branch_other, active_near, active_other),
    ):
        got = contract(near[...], right_near[...], 0, 0) + contract(
            other[...], right_other[...], 0, 0
        )
        for at in range(count):
            out_ref[at, :, place : place + hidden] = jnp.concatenate(
                [got[at * rows : (at + 1) * rows], got[(count + at) * rows :][:rows]], axis=0
            ).astype(LOW)
        half = pl.ds(place, hidden)
        copy = pltpu.make_async_copy(
            out_ref.at[:, :, half], out.at[:, :, half], sems.at[place // hidden]
        )
        copy.start()
        copies.append(copy)
    for copy in copies:
        copy.wait()


def first_norm_backward_kernel(
    second_ref,
    chip_ref,
    far_ref,
    first_ref,
    scale_ref,
    rows_ref,
    second_sums_ref,
    grad_ref,
    low_ref,
    sums_ref,
):
    own = grad_ref.shape[0]
    sums = [jnp.zeros((1, second_ref.shape[1]), FULL) for _ in range(3)]
    inverse = 1.0 / rows_ref[4:5]
    for at, to in blocks_of(second_ref.shape[0], TILE):
        upstream = second_ref[at:to].astype(FULL) + (
            chip_ref[at:to] + far_ref[at:to].astype(FULL)
        )
        normed = (first_ref[at:to].astype(FULL) - rows_ref[5:6]) * inverse
        scale_inv = jnp.transpose(jnp.broadcast_to(scale_ref[:1, at:to], (TILE, TILE)))[:, :1]
        grad = norm_backward(upstream, normed, scale_inv, rows_ref[4:5])
        low = grad.astype(LOW)
        low_ref[at:to] = low
        if to <= own:
            grad_ref[at:to] = grad
            for i, part in enumerate((low.astype(FULL), upstream * normed, upstream)):
                sums[i] += jnp.sum(part, axis=0, keepdims=True)
    given = second_sums_ref[...]
    sums_ref[...] = jnp.concatenate(
        [
            sums[0],
            given[0:1],
            sums[1],
            sums[2],
            given[1:3],
            jnp.zeros((2, sums[0].shape[1]), FULL),
        ],
        axis=0,
    )


def plane_sum_kernel(index_ref, blocks_ref, keep_ref, send_ref):
    rows = keep_ref.shape[0]
    total = blocks_ref[0].astype(FULL)
    for at in range(1, blocks_ref.shape[0]):
        total += blocks_ref[at].astype(FULL)
    lower = index_ref[0] == 0
    keep_ref[...] = jnp.where(lower, total[:rows], total[rows:])
    send_ref[...] = jnp.where(lower, total[rows:], total[:rows]).astype(send_ref.dtype)


def last_sum_kernel(index_ref, blocks_ref, q_ref, k_ref, v_ref, out_ref, *vector_refs):
    index = index_ref[0]
    rows = q_ref.shape[0]
    vector_rows = rows // 4
    columns = q_ref.shape[1]
    total = blocks_ref[0].astype(FULL)
    for at in range(1, blocks_ref.shape[0]):
        total += blocks_ref[at].astype(FULL)
    q_ref[...] = total[:, :columns]
    k_ref[...] = total[:, GROUP : GROUP + columns]
    v_ref[...] = total[:, 2 * GROUP : 2 * GROUP + columns]
    out_ref[...] = jnp.concatenate(
        [total[:, GROUP * i + columns : GROUP * (i + 1)] for i in range(3)], axis=1
    )
    packed = total[:, 3 * GROUP :]
    packed = packed + pltpu.roll(packed, TILE - 12, 1)
    wide = -(-12 * vector_rows // TILE) * TILE
    _, place_column = place_of(vector_rows, (TILE, wide), 1)
    select = jnp.where(place_column == lanes((TILE, wide), 0), 1.0, 0.0).astype(LOW)
    line = jnp.zeros((rows, wide), FULL)
    left = packed
    for _ in range(3):
        part = left.astype(LOW)
        left = left - part.astype(FULL)
        line += jnp.dot(part, select, preferred_element_type=FULL)
    place_row, _ = place_of(vector_rows, (rows, wide), 1)
    keep = place_row + index * vector_rows == lanes((rows, wide), 0)
    line = jnp.sum(jnp.where(keep, line, 0.0), axis=0, keepdims=True)
    for at, ref in enumerate(vector_refs):
        size = ref.shape[1]
        place = at * vector_rows
        ref[...] = pltpu.roll(line, wide - place, 1)[:, :size] if place else line[:, :size]


def shards(
    tokens,
    segments,
    q_weight,
    k_weight,
    v_weight,
    up_weight,
    out_weight,
    down_weight,
    q_bias,
    v_bias,
    out_bias,
    up_bias,
    down_bias,
    norm1_gain,
    norm1_shift,
    norm2_gain,
    norm2_shift,
    cotangent,
):
    my_index = lax.axis_index("tensor")
    dp_count = lax.axis_size("dp")
    local_len, width = tokens.shape[1:]
    half = 2 * local_len
    length = 4 * local_len
    shard_rows, head_cols = q_weight.shape
    hidden_cols = up_weight.shape[1]
    tokens = tokens[0]
    cotangent = cotangent[0]
    index = my_index.reshape(1)
    side_index = (lax.axis_index("dp") // (dp_count // 2)).reshape(1)

    vector_rows = q_bias.shape[0]
    line_size = -(-12 * vector_rows // TILE) * TILE
    line_count = line_size // TILE
    line = jnp.concatenate(
        [
            q_bias,
            v_bias,
            out_bias,
            down_bias,
            norm1_gain,
            norm1_shift,
            norm2_gain,
            norm2_shift,
            up_bias,
            jnp.zeros((line_size - 12 * vector_rows,), FULL),
        ]
    ).reshape(line_count, TILE)
    first_own = jnp.concatenate([q_weight, k_weight, v_weight, out_weight], axis=1)
    (first_block,) = call(
        first_block_kernel,
        [((dp_count, shard_rows, 3 * GROUP + TILE), LOW)],
        line,
        first_own,
    )
    first_blocks = spread(first_block)
    tokens_far = swap(tokens, 2)
    second_own = jnp.concatenate([up_weight, down_weight], axis=1)
    second_side = side(second_own)
    tokens_pair = jnp.concatenate([tokens, tokens_far], axis=0)
    tokens_core = swap(tokens_pair, 1)
    segment_row = ordered_segments(segments[0], my_index)[None]
    (second_block,) = call(
        second_block_kernel,
        [((dp_count // 2, 2 * shard_rows, 2 * hidden_cols), LOW)],
        side_index,
        second_own,
        second_side,
        smem=1,
    )
    first_blocks, second_block = lax.optimization_barrier((first_blocks, second_block))
    first_full = first_blocks.reshape(width, -1)
    lines = first_blocks[:, : 2 * line_count, 3 * GROUP :]
    lines = lines.reshape(dp_count, 2, line_size).transpose(1, 0, 2)
    lines = [lines] + [swap(lines, mask) for mask in (1, 2, 3)]
    second_full = plane(second_block)

    qkv_rows, mixed_rows, log_totals, attn_send, attn_keep, rows, bias_up = call(
        forward_kernel,
        [
            ((length, 3 * GROUP), LOW),
            ((length, GROUP), LOW),
            ((8, length), FULL),
            ((half, width), LOW),
            ((half, width), FULL),
            ((8, width), FULL),
            ((1, hidden_cols), FULL),
        ],
        index,
        tokens_pair,
        tokens_core,
        first_full,
        segment_row,
        *lines,
        smem=1,
        scratch=[pltpu.VMEM((length, 3 * GROUP), LOW), pltpu.SemaphoreType.DMA],
        away=(0,),
    )
    attn_chip = attn_keep + swap(attn_send, 1).astype(FULL)
    attn_far = swap(far_pack(attn_chip), 2)
    cotangent_far = swap(after(cotangent, attn_send), 2)
    hidden_low, inv_first = call(
        first_norm_kernel,
        [((half, width), LOW), ((8, half), FULL)],
        tokens_pair,
        attn_chip,
        after(attn_far, cotangent_far),
        rows,
    )
    hidden_core = after(swap(hidden_low, 1), cotangent_far)
    active_other, slope_other, branch_send, up_full, down_full = call(
        feed_other_kernel,
        [
            ((half, hidden_cols), LOW),
            ((half, hidden_cols), LOW),
            ((half, width), LOW),
            ((width, hidden_cols), LOW),
            ((width, hidden_cols), LOW),
        ],
        hidden_core,
        second_full,
        bias_up,
    )
    branch_got = swap(branch_send, 1)
    active_near, slope_near, branch_keep = call(
        feed_near_kernel,
        [((half, hidden_cols), LOW), ((half, hidden_cols), LOW), ((half, width), FULL)],
        hidden_low,
        up_full,
        down_full,
        bias_up,
    )
    branch_chip = branch_keep + branch_got.astype(FULL)
    layer_output, branch_low, second_sums = call(
        second_norm_kernel,
        [((local_len, width), LOW), ((half, width), LOW), ((8, width), FULL)],
        hidden_low,
        branch_chip,
        swap(far_pack(branch_chip), 2),
        rows,
        cotangent,
        cotangent_far,
    )
    branch_core = swap(branch_low, 1)
    near_shapes = [((half, hidden_cols), LOW), ((half, width), FULL), ((1, hidden_cols), FULL)]
    upward_near, hidden_keep, up_sum_near = call(
        feed_backward_kernel, near_shapes, branch_low, up_full, down_full, slope_near
    )
    other_shapes = [near_shapes[0], ((half, width), LOW), near_shapes[2]]
    upward_other, hidden_send, up_sum_other = call(
        feed_backward_kernel,
        other_shapes,
        after(branch_core, upward_near),
        up_full,
        down_full,
        slope_other,
    )
    hidden_got = swap(hidden_send, 1)
    hidden_chip = hidden_keep + hidden_got.astype(FULL)
    hidden_sent = far_pack(hidden_chip)
    hidden_far = swap(hidden_sent, 2)
    (pair_block,) = call(
        feed_weights_kernel,
        [((dp_count // 2, 2 * shard_rows, 2 * hidden_cols), LOW)],
        hidden_low,
        hidden_core,
        branch_low,
        branch_core,
        active_near,
        active_other,
        upward_near,
        upward_other,
        scratch=[
            pltpu.VMEM((dp_count // 2, 2 * shard_rows, 2 * hidden_cols), LOW),
            pltpu.SemaphoreType.DMA((2,)),
        ],
        away=(0,),
    )
    pair_blocks = plane(pair_block)
    resid_grad, attended_low, given = call(
        first_norm_backward_kernel,
        [((local_len, width), FULL), ((half, width), LOW), ((8, width), FULL)],
        branch_low,
        hidden_chip,
        hidden_far,
        hidden_low,
        inv_first,
        rows,
        second_sums,
    )
    attended_core = swap(attended_low, 1)
    qkv_grad, input_send, input_keep, vector_sums = call(
        backward_kernel,
        [
            ((length, 3 * GROUP), LOW),
            ((half, width), LOW),
            ((half, width), FULL),
            ((16, width), FULL),
        ],
        index,
        attended_low,
        attended_core,
        qkv_rows,
        log_totals,
        first_full,
        segment_row,
        given,
        up_sum_near,
        up_sum_other,
        smem=1,
        scratch=[
            pltpu.VMEM((length, GROUP), LOW),
            pltpu.VMEM((length, TILE), FULL),
            pltpu.VMEM((length, TILE), FULL),
            pltpu.VMEM((width, TILE), FULL),
        ],
    )
    input_chip = input_keep + swap(input_send, 1).astype(FULL)
    input_sent = input_chip[local_len:].astype(LOW)
    input_far = swap(input_sent, 2)
    vector_near = [swap(vector_sums, mask) for mask in (1, 2, 3)]
    (last_block,) = call(
        weights_kernel,
        [((width, 3 * GROUP + TILE), LOW)],
        tokens_pair,
        tokens_core,
        attended_low,
        attended_core,
        qkv_grad,
        mixed_rows,
        scratch=[pltpu.VMEM((width, 3 * GROUP), LOW), pltpu.SemaphoreType.DMA],
        away=(0,),
    )
    (last_block,) = call(
        vectors_kernel,
        [((width, 3 * GROUP + TILE), LOW)],
        last_block,
        vector_sums,
        *vector_near,
        scratch=[pltpu.VMEM((width, TILE), LOW), pltpu.SemaphoreType.DMA],
        away=(0,),
        far=(0,),
        aliases={0: 0},
    )
    last_block = after(last_block, input_far)
    last_blocks = spread(last_block.reshape(dp_count, shard_rows, 3 * GROUP + TILE))
    input_grad = resid_grad + (input_chip[:local_len] + input_far.astype(FULL))

    pair_keep, pair_send = call(
        plane_sum_kernel,
        [((shard_rows, 2 * hidden_cols), FULL), ((shard_rows, 2 * hidden_cols), LOW)],
        side_index,
        pair_blocks,
        smem=1,
    )
    pair_sum = pair_keep + side(pair_send).astype(FULL)
    q_grad, k_grad, v_grad, out_grad, *vectors = call(
        last_sum_kernel,
        [((shard_rows, head_cols), FULL)] * 4
        + [((1, vector_rows), FULL)] * 8
        + [((1, 4 * vector_rows), FULL)],
        index,
        last_blocks,
        smem=1,
    )
    vectors = [vector.reshape(-1) for vector in vectors]
    return (
        layer_output[None],
        input_grad[None],
        q_grad,
        k_grad,
        v_grad,
        pair_sum[:, :hidden_cols],
        out_grad,
        pair_sum[:, hidden_cols:],
        vectors[6],
        vectors[7],
        vectors[0],
        vectors[8],
        vectors[1],
        vectors[2],
        vectors[3],
        vectors[4],
        vectors[5],
    )


def solution(mesh):
    matrix = P("dp", "tensor")
    vector = P(("dp", "tensor"))
    rows = P("dp", "tensor", None)
    return jax.shard_map(
        shards,
        mesh=mesh,
        in_specs=(rows, P("dp", None)) + (matrix,) * 6 + (vector,) * 9 + (rows,),
        out_specs=(rows, rows) + (matrix,) * 6 + (vector,) * 9,
        check_vma=False,
    )
```

```python
import functools

import jax
import jax.numpy as jnp
from jax import lax
from jax.experimental import pallas as pl
from jax.experimental.pallas import tpu as pltpu
from jax.sharding import PartitionSpec as P

HEAD_DIM = 64
TILE = 128
GROUP = 256


NORM_EPSILON = 1e-12
MASKED_SCORE = -1000000000.0
ROOT_HALF = 0.7071067811865476
INV_ROOT_TAU = 0.3989422804014327
LOW = jnp.bfloat16
FULL = jnp.float32
VMEM_LIMIT = 48 * 1024 * 1024


def contract(left, right, left_dim, right_dim):
    return lax.dot_general(
        left, right, (((left_dim,), (right_dim,)), ((), ())), preferred_element_type=jnp.float32
    )


def swap(values, mask):
    return lax.ppermute(values, "tensor", [(i, i ^ mask) for i in range(4)])


def after(values, *others):
    return lax.optimization_barrier((values, *others))[0]


def spread(stacked):
    return lax.all_to_all(stacked, "dp", 0, 0, tiled=True)


def plane_groups():
    count = lax.axis_size("dp") // 2
    return [list(range(count)), list(range(count, 2 * count))]


def plane(stacked):
    return lax.all_to_all(stacked, "dp", 0, 0, tiled=True, axis_index_groups=plane_groups())


def side(values, mask=0):
    count = lax.axis_size("dp")
    pairs = [
        (4 * i + j, 4 * ((i + count // 2) % count) + (j ^ mask))
        for i in range(count)
        for j in range(4)
    ]
    return lax.ppermute(values, ("dp", "tensor"), pairs)


def halves(values):
    high = lax.reduce_precision(values, 8, 7)
    return (high.astype(LOW), (values - high).astype(LOW))


def far_pack(total):
    quarter = total.shape[0] // 2
    sent = total.astype(LOW)
    return jnp.concatenate([sent[quarter:], sent[:quarter]], axis=0)


def ordered_segments(segment_row, my_index):
    quarters = segment_row.reshape(4, -1)
    core = my_index % 2 == 1
    quarters = jnp.where(core, quarters[jnp.array([1, 0, 3, 2])], quarters)
    far = my_index // 2 == 1
    quarters = jnp.where(far, quarters[jnp.array([2, 3, 0, 1])], quarters)
    return jnp.concatenate([quarters[0], quarters[2], quarters[1], quarters[3]])


def call(body, out_shapes, *operands, smem=0, scratch=(), away=(), far=(), aliases=None):
    specs = [pl.BlockSpec(memory_space=pltpu.SMEM)] * smem
    specs += [
        pl.BlockSpec(memory_space=pltpu.HBM if i in far else pltpu.VMEM)
        for i in range(smem, len(operands))
    ]
    return pl.pallas_call(
        body,
        out_shape=[
            pltpu.HBM(shape, kind) if i in away else jax.ShapeDtypeStruct(shape, kind)
            for i, (shape, kind) in enumerate(out_shapes)
        ],
        in_specs=specs,
        out_specs=[
            pl.BlockSpec(memory_space=pltpu.HBM if i in away else pltpu.VMEM)
            for i in range(len(out_shapes))
        ],
        input_output_aliases=aliases or {},
        scratch_shapes=list(scratch),
        compiler_params=pltpu.CompilerParams(vmem_limit_bytes=VMEM_LIMIT),
        cost_estimate=pl.CostEstimate(flops=1000, bytes_accessed=1000, transcendentals=0),
    )(*operands)


def lanes(shape, dim=1):
    return lax.broadcasted_iota(jnp.int32, shape, dim)


def head_tile(head):
    return head // 2


def head_mask(head, shape, dim=1):
    index = lanes(shape, dim)
    return index >= HEAD_DIM if head % 2 else index < HEAD_DIM


def only(values, mask):
    return jnp.where(mask, values, jnp.zeros_like(values))


def packed_out(weight_ref):
    rows = weight_ref.shape[0]
    parts = [
        weight_ref[:, GROUP * i + TILE : GROUP * (i + 1)].astype(FULL) for i in range(3)
    ]
    low = head_mask(0, (rows, TILE))
    first = jnp.where(low, pltpu.roll(parts[0], HEAD_DIM, 1), parts[1])
    second = jnp.where(low, pltpu.roll(parts[2], HEAD_DIM, 1), 0.0)
    return jnp.concatenate([first, second], axis=1).astype(LOW)


def lined_heads(rows):
    first, second = rows[:, :TILE], rows[:, TILE:]
    return [pltpu.roll(first, HEAD_DIM, 1), first, pltpu.roll(second, HEAD_DIM, 1)]


def transposed(values):
    return jnp.transpose(values.astype(FULL))


def expand_matrix(count):
    shape = (count, 4 * count)
    return jnp.where(lanes(shape) // 4 == lanes(shape, 0), 1.0, 0.0).astype(LOW)


def unpack_lines(index, lower, line_refs, vector_ref, columns, width):
    devices, size = line_refs[0].shape[1:]
    devices = 2 * devices
    each = width // (4 * devices)
    flipped = []
    for part in range(2):
        near = [ref[part].astype(FULL) for ref in line_refs]
        ordered = []
        for at in range(8):
            row = near[7]
            for mask in range(7):
                row = jnp.where((2 * index + lower) ^ (mask % 4 * 2 + mask // 4) == at, near[mask], row)
            ordered.append(row)
        flipped.append(jnp.transpose(jnp.concatenate(ordered, axis=0)).astype(LOW))

    def spread_lines(place, valid):
        shape = (4 * devices, place.shape[1])
        row = lanes(shape, 0)
        select = (row % devices == place // (4 * each)) & (
            row // devices == place % (4 * each) // each
        )
        select = jnp.where(select & valid, 1.0, 0.0).astype(LOW)
        return [jnp.dot(part, select, preferred_element_type=FULL) for part in flipped]

    def vectors_at(place, valid):
        line_at = lanes((size, place.shape[1]), 0)
        keep = (line_at < 8 * each) & (line_at % each == place % each)
        row = lanes((8, size), 0)
        gather = jnp.where(lanes((8, size)) // each == row, 1.0, 0.0).astype(LOW)
        total = jnp.zeros((8, place.shape[1]), FULL)
        for part in spread_lines(place, valid):
            part = jnp.where(keep, part, 0.0).astype(LOW)
            total += jnp.dot(gather, part, preferred_element_type=FULL)
        return total

    place = lanes((1, width))
    vector_ref[...] = vectors_at(place, place >= 0)
    place = lanes((1, GROUP))
    own = vectors_at(place + index * columns, place < columns)
    bias = jnp.concatenate([own[0:1], jnp.zeros((1, GROUP), FULL), own[1:2]], axis=1)
    place = lanes((1, 4 * columns)) + index * (4 * columns)
    line_at = lanes((size, 4 * columns), 0)
    keep = line_at == 8 * each + place % (4 * each)
    up_bias = jnp.zeros((1, 4 * columns), FULL)
    for part in spread_lines(place // 4, place >= 0):
        up_bias += jnp.sum(jnp.where(keep, part, 0.0), axis=0, keepdims=True)
    return (bias, up_bias)


def forward_kernel(
    index_ref,
    near_ref,
    other_ref,
    half_ref,
    half_other_ref,
    segment_ref,
    *refs,
):
    line_refs = refs[:8]
    (
        qkv_out,
        mixed_ref,
        log_ref,
        send_ref,
        keep_ref,
        vector_ref,
        up_bias_ref,
        weight_ref,
        qkv_ref,
        qkv_sem,
    ) = refs[8:]
    index, lower = index_ref[0], index_ref[1]
    half = near_ref.shape[0]
    columns = 3 * HEAD_DIM
    width = weight_ref.shape[0]
    part = width // 2
    weight_ref[pl.ds(pl.multiple_of(lower * part, 16), part), :] = half_ref[:, : 3 * GROUP]
    weight_ref[pl.ds(pl.multiple_of((1 - lower) * part, 16), part), :] = half_other_ref[
        :, : 3 * GROUP
    ]
    bias, up_bias = unpack_lines(index, lower, line_refs, vector_ref, columns, width)
    up_bias_ref[...] = up_bias
    keep = lanes((1, 3 * GROUP)) % GROUP < columns
    for at, rows_ref in ((0, near_ref), (half, other_ref)):
        got = jnp.dot(rows_ref[...], weight_ref[:, : 3 * GROUP], preferred_element_type=FULL)
        qkv_ref[at : at + half, :] = jnp.where(keep, got + bias, 0.0).astype(LOW)
    qkv_copy = pltpu.make_async_copy(qkv_ref, qkv_out, qkv_sem)
    qkv_copy.start()

    length = 2 * half
    row_segments = segment_ref[...]
    column_segments = jnp.transpose(
        jnp.broadcast_to(row_segments.astype(FULL), (TILE, length))
    )[:, :1].astype(jnp.int32)
    same = column_segments == row_segments
    mixed_tiles = [None, None]
    for head in range(3):
        at = TILE * head_tile(head)
        mask = head_mask(head, (length, TILE))
        key = only(qkv_ref[:, GROUP + at : GROUP + at + TILE], mask) * jnp.asarray(0.125, LOW)
        scores = contract(key, qkv_ref[:, at : at + TILE], 1, 1)
        scores = jnp.where(same, scores, MASKED_SCORE)
        highest = jnp.max(scores, axis=0, keepdims=True)
        shifted = jnp.exp(scores - highest)
        total = jnp.sum(shifted, axis=0, keepdims=True)
        probs = (shifted * (1.0 / total)).astype(LOW)
        log_ref[head : head + 1, :] = highest + jnp.log(total)
        value = only(qkv_ref[:, 2 * GROUP + at : 2 * GROUP + at + TILE], mask)
        got = jnp.dot(transposed(value).astype(LOW), probs, preferred_element_type=FULL)
        tile = head_tile(head)
        mixed_tiles[tile] = got if mixed_tiles[tile] is None else mixed_tiles[tile] + got
    log_ref[3:, :] = jnp.zeros((5, length), FULL)
    for tile in range(2):
        mixed_ref[:, TILE * tile : TILE * (tile + 1)] = jnp.transpose(mixed_tiles[tile]).astype(LOW)
    out = packed_out(weight_ref)
    keep_ref[...] = contract(mixed_ref[:half, :], out, 1, 1)
    send_ref[...] = contract(mixed_ref[half:, :], out, 1, 1).astype(LOW)
    qkv_copy.wait()


def backward_kernel(
    index_ref,
    near_ref,
    other_ref,
    qkv_ref,
    log_ref,
    weight_ref,
    segment_ref,
    sums_ref,
    up_sum_ref,
    up_sum_other_ref,
    grad_ref,
    send_ref,
    keep_ref,
    vector_ref,
    mixed_grad,
    key_grad,
    value_grad,
    columns_held,
):
    index = index_ref[0]
    half = near_ref.shape[0]
    length = 2 * half
    columns = 3 * HEAD_DIM
    out = packed_out(weight_ref)
    mixed_grad[:half, :] = jnp.dot(near_ref[...], out, preferred_element_type=FULL).astype(LOW)
    mixed_grad[half:, :] = jnp.dot(other_ref[...], out, preferred_element_type=FULL).astype(LOW)
    row_segments = segment_ref[...]
    column_segments = jnp.transpose(
        jnp.broadcast_to(row_segments.astype(FULL), (TILE, length))
    )[:, :1].astype(jnp.int32)
    same = column_segments == row_segments
    sums = []
    for tile in range(2):
        at = TILE * tile
        query_grad = jnp.zeros((TILE, length), FULL)
        for head in (0, 1) if tile == 0 else (2,):
            mask = head_mask(head, (length, TILE))
            scale = jnp.asarray(0.125, LOW)
            key = only(qkv_ref[:, GROUP + at : GROUP + at + TILE], mask) * scale
            query = only(qkv_ref[:, at : at + TILE], mask)
            value = only(qkv_ref[:, 2 * GROUP + at : 2 * GROUP + at + TILE], mask)
            grad = only(mixed_grad[:, at : at + TILE], mask)
            scores = contract(key, query, 1, 1)
            probs = jnp.exp(
                jnp.where(same, scores, MASKED_SCORE) - log_ref[head : head + 1, :]
            )
            probs_grad = contract(value, grad, 1, 1)
            inner = jnp.sum(probs * probs_grad, axis=0, keepdims=True)
            scores_grad = (probs * (probs_grad - inner)).astype(LOW)
            got = jnp.dot(probs.astype(LOW), grad, preferred_element_type=FULL)
            got_key = jnp.dot(scores_grad, query * scale, preferred_element_type=FULL)
            if head % 2 == 0:
                value_grad[...] = got
                key_grad[...] = got_key
            else:
                value_grad[...] += got
                key_grad[...] += got_key
            query_grad += jnp.dot(
                transposed(key).astype(LOW), scores_grad, preferred_element_type=FULL
            )
        query_low = jnp.transpose(query_grad).astype(LOW)
        value_low = value_grad[...].astype(LOW)
        grad_ref[:, at : at + TILE] = query_low
        grad_ref[:, GROUP + at : GROUP + at + TILE] = key_grad[...].astype(LOW)
        grad_ref[:, 2 * GROUP + at : 2 * GROUP + at + TILE] = value_low
        sums.append(
            (
                jnp.sum(query_low.astype(FULL), axis=0, keepdims=True),
                jnp.sum(value_low.astype(FULL), axis=0, keepdims=True),
            )
        )
    wide = weight_ref[:, : 3 * GROUP]
    keep_ref[...] = contract(grad_ref[:half, :], wide, 1, 1)
    send_ref[...] = contract(grad_ref[half:, :], wide, 1, 1).astype(LOW)

    up_row = up_sum_ref[...] + up_sum_other_ref[...]
    place = lanes((8, 4 * columns))
    spaced = jnp.where(place % 4 == lanes((8, 4 * columns), 0), up_row, 0.0)
    high = spaced.astype(LOW)
    low = (spaced - high.astype(FULL)).astype(LOW)
    expand = expand_matrix(columns)
    up_rows = contract(high, expand, 1, 1) + contract(low, expand, 1, 1)
    up_rows = jnp.concatenate([up_rows, jnp.zeros((8, GROUP - columns), FULL)], axis=1)
    query_sum = jnp.concatenate([sums[0][0], sums[1][0]], axis=1)
    value_sum = jnp.concatenate([sums[0][1], sums[1][1]], axis=1)
    at_row = lanes((8, GROUP), 0)
    late = jnp.where(at_row == 6, query_sum, jnp.where(at_row == 7, value_sum, 0.0))
    stacked = jnp.concatenate([late, up_rows, jnp.zeros((TILE - 16, GROUP), FULL)], axis=0)
    columns_held[...] = jnp.zeros_like(columns_held)
    columns_held[pl.ds(pl.multiple_of(index * columns, 64), columns), :] = jnp.transpose(stacked)[
        :columns
    ]
    placed = jnp.transpose(columns_held[...])[:16]
    given = sums_ref[...]
    vector_ref[:8, :] = placed[:8] + given
    vector_ref[8:, :] = placed[8:]


def weights_kernel(
    tokens_near, tokens_other, near_ref, other_ref, grad_ref, mixed_ref, out, out_ref, sem
):
    half = near_ref.shape[0]
    width = near_ref.shape[1]
    got = contract(tokens_near[...], grad_ref[:half, :], 0, 0) + contract(
        tokens_other[...], grad_ref[half:, :], 0, 0
    )
    out_grad = contract(near_ref[...], mixed_ref[:half, :], 0, 0) + contract(
        other_ref[...], mixed_ref[half:, :], 0, 0
    )
    high = head_mask(1, (width, TILE))
    for part, lined in enumerate(lined_heads(out_grad)):
        at = GROUP * part
        out_ref[:, at : at + TILE] = got[:, at : at + TILE].astype(LOW)
        out_ref[:, at + TILE : at + GROUP] = jnp.where(
            high, lined, got[:, at + TILE : at + GROUP]
        ).astype(LOW)
    copy = pltpu.make_async_copy(out_ref, out.at[:, : 3 * GROUP], sem)
    copy.start()
    copy.wait()


def vectors_kernel(block_ref, own_ref, core_ref, far_ref, both_ref, out_ref, held, sem):
    total = own_ref[...]
    for ref in (core_ref, far_ref, both_ref):
        total += ref[...].astype(FULL)
    total = total[:12]
    high = total.astype(LOW).astype(FULL)
    rows = jnp.concatenate(
        [high, total - high, jnp.zeros((TILE - 24, total.shape[1]), FULL)], axis=0
    )
    held[...] = jnp.transpose(rows).astype(LOW)
    copy = pltpu.make_async_copy(held, out_ref.at[:, 3 * GROUP :], sem)
    copy.start()
    copy.wait()


def place_of(vector_rows, shape, dim):
    place = lanes(shape, dim)
    many = 8 * vector_rows
    row = jnp.where(place < many, place % vector_rows, (place - many) // 4)
    column = jnp.where(place < many, place // vector_rows, 8 + (place - many) % 4)
    return (row, jnp.where(place < many + 4 * vector_rows, column, 1000))


def first_block_kernel(line_ref, weight_ref, block_ref):
    rows = weight_ref.shape[0]
    columns_each = weight_ref.shape[1] // 4
    count = line_ref.shape[0]
    row_at = lanes((rows, TILE), 0)
    packed = jnp.zeros((rows, TILE), FULL)
    for at in range(count):
        line = line_ref[at : at + 1]
        high = line.astype(LOW).astype(FULL)
        packed = jnp.where(row_at == at, high, packed)
        packed = jnp.where(row_at == count + at, line - high, packed)
    weight = weight_ref[...].astype(FULL)
    q_part, k_part, v_part, out = [
        weight[:, columns_each * i : columns_each * (i + 1)] for i in range(4)
    ]
    block = jnp.concatenate(
        [
            q_part,
            out[:, :HEAD_DIM],
            k_part,
            out[:, HEAD_DIM : 2 * HEAD_DIM],
            v_part,
            out[:, 2 * HEAD_DIM :],
            packed,
        ],
        axis=1,
    ).astype(LOW)
    for at in range(block_ref.shape[0]):
        block_ref[at] = block


def second_block_kernel(index_ref, own_ref, other_ref, block_ref):
    lower = index_ref[0] == 0
    own = own_ref[...].astype(FULL)
    other = other_ref[...].astype(FULL)
    block = jnp.concatenate(
        [jnp.where(lower, own, other), jnp.where(lower, other, own)], axis=0
    ).astype(LOW)
    for at in range(block_ref.shape[0]):
        block_ref[at] = block


def moments(values, gain, shift):
    center = values - jnp.mean(values, axis=-1, keepdims=True)
    scale_inv = lax.rsqrt(jnp.mean(center * center, axis=-1, keepdims=True) + NORM_EPSILON)
    normed = center * scale_inv
    return (normed * gain + shift, normed, scale_inv)


def norm_backward(upstream, normed, scale_inv, gain):
    scaled = upstream * gain
    return scale_inv * (
        scaled
        - jnp.mean(scaled, axis=-1, keepdims=True)
        - normed * jnp.mean(scaled * normed, axis=-1, keepdims=True)
    )


def blocks_of(rows, size=64):
    return [(at, at + size) for at in range(0, rows, size)]


def first_norm_kernel(tokens_ref, chip_ref, far_ref, rows_ref, low_ref, scale_ref):
    for at, to in blocks_of(tokens_ref.shape[0], TILE):
        values = (
            tokens_ref[at:to].astype(FULL)
            + (chip_ref[at:to] + far_ref[at:to].astype(FULL))
            + rows_ref[2:3]
        )
        first, _, scale_inv = moments(values, rows_ref[4:5], rows_ref[5:6])
        low_ref[at:to] = first.astype(LOW)
        scale_ref[:, at:to] = jnp.transpose(jnp.broadcast_to(scale_inv, (TILE, TILE)))[:8]


def feed_rows(rows_ref, up, down, bias_ref, active_ref, slope_ref, part_ref):
    size = rows_ref.shape[0] // 2
    for at, to in blocks_of(rows_ref.shape[0], size):
        upward = jnp.dot(rows_ref[at:to], up[...], preferred_element_type=FULL) + bias_ref[...]
        for low, high in blocks_of(size, 32):
            part = upward[low:high]
            gate = 0.5 * (1.0 + lax.erf(part * ROOT_HALF))
            active_ref[at + low : at + high] = (part * gate).astype(LOW)
            slope_ref[at + low : at + high] = (
                gate + part * jnp.exp(-0.5 * part * part) * INV_ROOT_TAU
            ).astype(LOW)
        got = contract(active_ref[at:to], down[...], 1, 1)
        part_ref[at:to] = got.astype(part_ref.dtype)


def feed_other_kernel(
    rows_ref, blocks_ref, bias_ref, active_ref, slope_ref, part_ref, up_ref, down_ref
):
    count, rows, wide = blocks_ref.shape
    rows = rows // 2
    hidden = wide // 2
    group = 1 if rows % 16 == 0 else 2
    for lower in range(2):
        for at in range(0, count, group):
            got = jnp.concatenate(
                [
                    blocks_ref[at + i].astype(FULL)[rows * lower : rows * (lower + 1)]
                    for i in range(group)
                ],
                axis=0,
            ).astype(LOW)
            to = (lower * count + at) * rows
            up_ref[to : to + group * rows] = got[:, :hidden]
            down_ref[to : to + group * rows] = got[:, hidden:]
    feed_rows(rows_ref, up_ref, down_ref, bias_ref, active_ref, slope_ref, part_ref)


def feed_near_kernel(rows_ref, up_ref, down_ref, bias_ref, active_ref, slope_ref, part_ref):
    feed_rows(rows_ref, up_ref, down_ref, bias_ref, active_ref, slope_ref, part_ref)


def second_norm_kernel(
    first_ref,
    chip_ref,
    far_ref,
    rows_ref,
    cotangent_ref,
    cotangent_far_ref,
    output_ref,
    low_ref,
    sums_ref,
):
    own = output_ref.shape[0]
    sums = [jnp.zeros((1, first_ref.shape[1]), FULL) for _ in range(3)]
    for at, to in blocks_of(first_ref.shape[0]):
        values = first_ref[at:to].astype(FULL) + (chip_ref[at:to] + far_ref[at:to].astype(FULL)) + rows_ref[3:4]
        output, normed, scale_inv = moments(values, rows_ref[6:7], rows_ref[7:8])
        if to <= own:
            upstream = cotangent_ref[at:to].astype(FULL)
            output_ref[at:to] = output.astype(LOW)
        else:
            upstream = cotangent_far_ref[at - own : to - own].astype(FULL)
        grad = norm_backward(upstream, normed, scale_inv, rows_ref[6:7])
        low = grad.astype(LOW)
        low_ref[at:to] = low
        if to <= own:
            for i, part in enumerate((low.astype(FULL), upstream * normed, upstream)):
                sums[i] += jnp.sum(part, axis=0, keepdims=True)
    sums_ref[...] = jnp.concatenate(sums + [jnp.zeros((5, sums[0].shape[1]), FULL)], axis=0)


def feed_backward_kernel(rows_ref, up_ref, down_ref, slope_ref, grad_ref, part_ref, sum_ref):
    size = rows_ref.shape[0] // 2
    total = jnp.zeros((1, up_ref.shape[1]), FULL)
    for at, to in blocks_of(rows_ref.shape[0], size):
        grad = jnp.dot(rows_ref[at:to], down_ref[...], preferred_element_type=FULL)
        for low, high in blocks_of(size, 32):
            place = slice(at + low, at + high)
            part = (grad[low:high] * slope_ref[place].astype(FULL)).astype(LOW)
            grad_ref[place] = part
            total += jnp.sum(part.astype(FULL), axis=0, keepdims=True)
        got = contract(grad_ref[at:to], up_ref[...], 1, 1)
        part_ref[at:to] = got.astype(part_ref.dtype)
    sum_ref[...] = total


def feed_weights_kernel(
    hidden_near,
    hidden_other,
    branch_near,
    branch_other,
    active_near,
    active_other,
    grad_near,
    grad_other,
    out,
    out_ref,
    sems,
):
    count, rows, wide = out_ref.shape
    rows = rows // 2
    hidden = wide // 2
    copies = []
    for place, near, other, right_near, right_other in (
        (0, hidden_near, hidden_other, grad_near, grad_other),
        (hidden, branch_near, branch_other, active_near, active_other),
    ):
        got = contract(near[...], right_near[...], 0, 0) + contract(
            other[...], right_other[...], 0, 0
        )
        for at in range(count):
            out_ref[at, :, place : place + hidden] = jnp.concatenate(
                [got[at * rows : (at + 1) * rows], got[(count + at) * rows :][:rows]], axis=0
            ).astype(LOW)
        half = pl.ds(place, hidden)
        copy = pltpu.make_async_copy(
            out_ref.at[:, :, half], out.at[:, :, half], sems.at[place // hidden]
        )
        copy.start()
        copies.append(copy)
    for copy in copies:
        copy.wait()


def first_norm_backward_kernel(
    second_ref,
    chip_ref,
    far_ref,
    first_ref,
    scale_ref,
    rows_ref,
    second_sums_ref,
    grad_ref,
    low_ref,
    sums_ref,
):
    own = grad_ref.shape[0]
    sums = [jnp.zeros((1, second_ref.shape[1]), FULL) for _ in range(3)]
    inverse = 1.0 / rows_ref[4:5]
    for at, to in blocks_of(second_ref.shape[0], TILE):
        upstream = second_ref[at:to].astype(FULL) + (
            chip_ref[at:to] + far_ref[at:to].astype(FULL)
        )
        normed = (first_ref[at:to].astype(FULL) - rows_ref[5:6]) * inverse
        scale_inv = jnp.transpose(jnp.broadcast_to(scale_ref[:1, at:to], (TILE, TILE)))[:, :1]
        grad = norm_backward(upstream, normed, scale_inv, rows_ref[4:5])
        low = grad.astype(LOW)
        low_ref[at:to] = low
        if to <= own:
            grad_ref[at:to] = grad
            for i, part in enumerate((low.astype(FULL), upstream * normed, upstream)):
                sums[i] += jnp.sum(part, axis=0, keepdims=True)
    given = second_sums_ref[...]
    sums_ref[...] = jnp.concatenate(
        [
            sums[0],
            given[0:1],
            sums[1],
            sums[2],
            given[1:3],
            jnp.zeros((2, sums[0].shape[1]), FULL),
        ],
        axis=0,
    )


def plane_sum_kernel(index_ref, blocks_ref, keep_ref, send_ref):
    rows = keep_ref.shape[0]
    total = blocks_ref[0].astype(FULL)
    for at in range(1, blocks_ref.shape[0]):
        total += blocks_ref[at].astype(FULL)
    lower = index_ref[0] == 0
    keep_ref[...] = jnp.where(lower, total[:rows], total[rows:])
    send_ref[...] = jnp.where(lower, total[rows:], total[:rows]).astype(send_ref.dtype)


def last_sum_kernel(index_ref, blocks_ref, q_ref, k_ref, v_ref, out_ref, *vector_refs):
    index = index_ref[0]
    rows = q_ref.shape[0]
    vector_rows = rows // 4
    columns = q_ref.shape[1]
    total = blocks_ref[0].astype(FULL)
    for at in range(1, blocks_ref.shape[0]):
        total += blocks_ref[at].astype(FULL)
    q_ref[...] = total[:, :columns]
    k_ref[...] = total[:, GROUP : GROUP + columns]
    v_ref[...] = total[:, 2 * GROUP : 2 * GROUP + columns]
    out_ref[...] = jnp.concatenate(
        [total[:, GROUP * i + columns : GROUP * (i + 1)] for i in range(3)], axis=1
    )
    packed = total[:, 3 * GROUP :]
    packed = packed + pltpu.roll(packed, TILE - 12, 1)
    wide = -(-12 * vector_rows // TILE) * TILE
    _, place_column = place_of(vector_rows, (TILE, wide), 1)
    select = jnp.where(place_column == lanes((TILE, wide), 0), 1.0, 0.0).astype(LOW)
    line = jnp.zeros((rows, wide), FULL)
    left = packed
    for _ in range(3):
        part = left.astype(LOW)
        left = left - part.astype(FULL)
        line += jnp.dot(part, select, preferred_element_type=FULL)
    place_row, _ = place_of(vector_rows, (rows, wide), 1)
    keep = place_row + index * vector_rows == lanes((rows, wide), 0)
    line = jnp.sum(jnp.where(keep, line, 0.0), axis=0, keepdims=True)
    for at, ref in enumerate(vector_refs):
        size = ref.shape[1]
        place = at * vector_rows
        ref[...] = pltpu.roll(line, wide - place, 1)[:, :size] if place else line[:, :size]


def shards(
    tokens,
    segments,
    q_weight,
    k_weight,
    v_weight,
    up_weight,
    out_weight,
    down_weight,
    q_bias,
    v_bias,
    out_bias,
    up_bias,
    down_bias,
    norm1_gain,
    norm1_shift,
    norm2_gain,
    norm2_shift,
    cotangent,
):
    my_index = lax.axis_index("tensor")
    dp_count = lax.axis_size("dp")
    local_len, width = tokens.shape[1:]
    half = 2 * local_len
    length = 4 * local_len
    shard_rows, head_cols = q_weight.shape
    hidden_cols = up_weight.shape[1]
    tokens = tokens[0]
    cotangent = cotangent[0]
    index = my_index.reshape(1)
    side_index = (lax.axis_index("dp") // (dp_count // 2)).reshape(1)

    vector_rows = q_bias.shape[0]
    line_size = -(-12 * vector_rows // TILE) * TILE
    line_count = line_size // TILE
    line = jnp.concatenate(
        [
            q_bias,
            v_bias,
            out_bias,
            down_bias,
            norm1_gain,
            norm1_shift,
            norm2_gain,
            norm2_shift,
            up_bias,
            jnp.zeros((line_size - 12 * vector_rows,), FULL),
        ]
    ).reshape(line_count, TILE)
    first_own = jnp.concatenate([q_weight, k_weight, v_weight, out_weight], axis=1)
    (first_block,) = call(
        first_block_kernel,
        [((dp_count // 2, shard_rows, 3 * GROUP + TILE), LOW)],
        line,
        first_own,
    )
    first_half = plane(first_block)
    tokens_far = swap(tokens, 2)
    second_own = jnp.concatenate([up_weight, down_weight], axis=1)
    second_side = side(second_own)
    tokens_pair = jnp.concatenate([tokens, tokens_far], axis=0)
    cotangent_far = swap(cotangent, 2)
    tokens_core = swap(after(tokens_pair, cotangent_far), 1)
    segment_row = ordered_segments(segments[0], my_index)[None]
    (second_block,) = call(
        second_block_kernel,
        [((dp_count // 2, 2 * shard_rows, 2 * hidden_cols), LOW)],
        side_index,
        second_own,
        second_side,
        smem=1,
    )
    first_half, second_block = lax.optimization_barrier((first_half, second_block))
    first_other = side(first_half)
    lines = first_half[:, : 2 * line_count, 3 * GROUP :]
    lines = lines.reshape(dp_count // 2, 2, line_size).transpose(1, 0, 2)
    lines = [lines] + [swap(lines, mask) for mask in (1, 2, 3)] + [side(lines, m) for m in range(4)]
    second_full = plane(second_block)

    qkv_rows, mixed_rows, log_totals, attn_send, attn_keep, rows, bias_up, first_full = call(
        forward_kernel,
        [
            ((length, 3 * GROUP), LOW),
            ((length, GROUP), LOW),
            ((8, length), FULL),
            ((half, width), LOW),
            ((half, width), FULL),
            ((8, width), FULL),
            ((1, hidden_cols), FULL),
            ((width, 3 * GROUP), LOW),
        ],
        jnp.concatenate([index, side_index]),
        tokens_pair,
        tokens_core,
        first_half.reshape(width // 2, -1),
        first_other.reshape(width // 2, -1),
        segment_row,
        *lines,
        smem=1,
        scratch=[pltpu.VMEM((length, 3 * GROUP), LOW), pltpu.SemaphoreType.DMA],
        away=(0,),
    )
    attn_chip = attn_keep + swap(attn_send, 1).astype(FULL)
    attn_far = swap(far_pack(attn_chip), 2)
    hidden_low, inv_first = call(
        first_norm_kernel,
        [((half, width), LOW), ((8, half), FULL)],
        tokens_pair,
        attn_chip,
        attn_far,
        rows,
    )
    hidden_core = swap(hidden_low, 1)
    active_other, slope_other, branch_send, up_full, down_full = call(
        feed_other_kernel,
        [
            ((half, hidden_cols), LOW),
            ((half, hidden_cols), LOW),
            ((half, width), LOW),
            ((width, hidden_cols), LOW),
            ((width, hidden_cols), LOW),
        ],
        hidden_core,
        second_full,
        bias_up,
    )
    branch_got = swap(branch_send, 1)
    active_near, slope_near, branch_keep = call(
        feed_near_kernel,
        [((half, hidden_cols), LOW), ((half, hidden_cols), LOW), ((half, width), FULL)],
        hidden_low,
        up_full,
        down_full,
        bias_up,
    )
    branch_chip = branch_keep + branch_got.astype(FULL)
    layer_output, branch_low, second_sums = call(
        second_norm_kernel,
        [((local_len, width), LOW), ((half, width), LOW), ((8, width), FULL)],
        hidden_low,
        branch_chip,
        swap(far_pack(branch_chip), 2),
        rows,
        cotangent,
        cotangent_far,
    )
    branch_core = swap(branch_low, 1)
    near_shapes = [((half, hidden_cols), LOW), ((half, width), FULL), ((1, hidden_cols), FULL)]
    upward_near, hidden_keep, up_sum_near = call(
        feed_backward_kernel, near_shapes, branch_low, up_full, down_full, slope_near
    )
    other_shapes = [near_shapes[0], ((half, width), LOW), near_shapes[2]]
    upward_other, hidden_send, up_sum_other = call(
        feed_backward_kernel,
        other_shapes,
        after(branch_core, upward_near),
        up_full,
        down_full,
        slope_other,
    )
    hidden_got = swap(hidden_send, 1)
    hidden_chip = hidden_keep + hidden_got.astype(FULL)
    hidden_sent = far_pack(hidden_chip)
    hidden_far = swap(hidden_sent, 2)
    (pair_block,) = call(
        feed_weights_kernel,
        [((dp_count // 2, 2 * shard_rows, 2 * hidden_cols), LOW)],
        hidden_low,
        hidden_core,
        branch_low,
        branch_core,
        active_near,
        active_other,
        upward_near,
        upward_other,
        scratch=[
            pltpu.VMEM((dp_count // 2, 2 * shard_rows, 2 * hidden_cols), LOW),
            pltpu.SemaphoreType.DMA((2,)),
        ],
        away=(0,),
    )
    pair_blocks = plane(pair_block)
    resid_grad, attended_low, given = call(
        first_norm_backward_kernel,
        [((local_len, width), FULL), ((half, width), LOW), ((8, width), FULL)],
        branch_low,
        hidden_chip,
        hidden_far,
        hidden_low,
        inv_first,
        rows,
        second_sums,
    )
    attended_core = swap(attended_low, 1)
    qkv_grad, input_send, input_keep, vector_sums = call(
        backward_kernel,
        [
            ((length, 3 * GROUP), LOW),
            ((half, width), LOW),
            ((half, width), FULL),
            ((16, width), FULL),
        ],
        index,
        attended_low,
        attended_core,
        qkv_rows,
        log_totals,
        first_full,
        segment_row,
        given,
        up_sum_near,
        up_sum_other,
        smem=1,
        scratch=[
            pltpu.VMEM((length, GROUP), LOW),
            pltpu.VMEM((length, TILE), FULL),
            pltpu.VMEM((length, TILE), FULL),
            pltpu.VMEM((width, TILE), FULL),
        ],
    )
    input_chip = input_keep + swap(input_send, 1).astype(FULL)
    input_sent = input_chip[local_len:].astype(LOW)
    input_far = swap(input_sent, 2)
    vector_near = [swap(vector_sums.astype(LOW), mask) for mask in (1, 2, 3)]
    (last_block,) = call(
        weights_kernel,
        [((width, 3 * GROUP + TILE), LOW)],
        tokens_pair,
        tokens_core,
        attended_low,
        attended_core,
        qkv_grad,
        mixed_rows,
        scratch=[pltpu.VMEM((width, 3 * GROUP), LOW), pltpu.SemaphoreType.DMA],
        away=(0,),
    )
    (last_block,) = call(
        vectors_kernel,
        [((width, 3 * GROUP + TILE), LOW)],
        last_block,
        vector_sums,
        *vector_near,
        scratch=[pltpu.VMEM((width, TILE), LOW), pltpu.SemaphoreType.DMA],
        away=(0,),
        far=(0,),
        aliases={0: 0},
    )
    last_block = after(last_block, input_far)
    last_blocks = spread(last_block.reshape(dp_count, shard_rows, 3 * GROUP + TILE))
    input_grad = resid_grad + (input_chip[:local_len] + input_far.astype(FULL))

    pair_keep, pair_send = call(
        plane_sum_kernel,
        [((shard_rows, 2 * hidden_cols), FULL), ((shard_rows, 2 * hidden_cols), LOW)],
        side_index,
        pair_blocks,
        smem=1,
    )
    pair_sum = pair_keep + side(pair_send).astype(FULL)
    q_grad, k_grad, v_grad, out_grad, *vectors = call(
        last_sum_kernel,
        [((shard_rows, head_cols), FULL)] * 4
        + [((1, vector_rows), FULL)] * 8
        + [((1, 4 * vector_rows), FULL)],
        index,
        last_blocks,
        smem=1,
    )
    vectors = [vector.reshape(-1) for vector in vectors]
    return (
        layer_output[None],
        input_grad[None],
        q_grad,
        k_grad,
        v_grad,
        pair_sum[:, :hidden_cols],
        out_grad,
        pair_sum[:, hidden_cols:],
        vectors[6],
        vectors[7],
        vectors[0],
        vectors[8],
        vectors[1],
        vectors[2],
        vectors[3],
        vectors[4],
        vectors[5],
    )


def solution(mesh):
    matrix = P("dp", "tensor")
    vector = P(("dp", "tensor"))
    rows = P("dp", "tensor", None)
    return jax.shard_map(
        shards,
        mesh=mesh,
        in_specs=(rows, P("dp", None)) + (matrix,) * 6 + (vector,) * 9 + (rows,),
        out_specs=(rows, rows) + (matrix,) * 6 + (vector,) * 9,
        check_vma=False,
    )
```

```python
import functools

import jax
import jax.numpy as jnp
from jax import lax
from jax.experimental import pallas as pl
from jax.experimental.pallas import tpu as pltpu
from jax.sharding import PartitionSpec as P

HEAD_DIM = 64
TILE = 128
GROUP = 256


NORM_EPSILON = 1e-12
MASKED_SCORE = -1000000000.0
ROOT_HALF = 0.7071067811865476
INV_ROOT_TAU = 0.3989422804014327
LOW = jnp.bfloat16
FULL = jnp.float32
VMEM_LIMIT = 48 * 1024 * 1024


def contract(left, right, left_dim, right_dim):
    return lax.dot_general(
        left, right, (((left_dim,), (right_dim,)), ((), ())), preferred_element_type=jnp.float32
    )


def swap(values, mask):
    return lax.ppermute(values, "tensor", [(i, i ^ mask) for i in range(4)])


def after(values, *others):
    return lax.optimization_barrier((values, *others))[0]


def spread(stacked):
    return lax.all_to_all(stacked, "dp", 0, 0, tiled=True)


def plane_groups():
    count = lax.axis_size("dp") // 2
    return [list(range(count)), list(range(count, 2 * count))]


def plane(stacked):
    return lax.all_to_all(stacked, "dp", 0, 0, tiled=True, axis_index_groups=plane_groups())


def side(values, mask=0):
    count = lax.axis_size("dp")
    pairs = [
        (4 * i + j, 4 * ((i + count // 2) % count) + (j ^ mask))
        for i in range(count)
        for j in range(4)
    ]
    return lax.ppermute(values, ("dp", "tensor"), pairs)


def halves(values):
    high = lax.reduce_precision(values, 8, 7)
    return (high.astype(LOW), (values - high).astype(LOW))


def far_pack(total):
    quarter = total.shape[0] // 2
    sent = total.astype(LOW)
    return jnp.concatenate([sent[quarter:], sent[:quarter]], axis=0)


def ordered_segments(segment_row, my_index):
    quarters = segment_row.reshape(4, -1)
    core = my_index % 2 == 1
    quarters = jnp.where(core, quarters[jnp.array([1, 0, 3, 2])], quarters)
    far = my_index // 2 == 1
    quarters = jnp.where(far, quarters[jnp.array([2, 3, 0, 1])], quarters)
    return jnp.concatenate([quarters[0], quarters[2], quarters[1], quarters[3]])


def call(body, out_shapes, *operands, smem=0, scratch=(), away=(), far=(), aliases=None):
    specs = [pl.BlockSpec(memory_space=pltpu.SMEM)] * smem
    specs += [
        pl.BlockSpec(memory_space=pltpu.HBM if i in far else pltpu.VMEM)
        for i in range(smem, len(operands))
    ]
    return pl.pallas_call(
        body,
        out_shape=[
            pltpu.HBM(shape, kind) if i in away else jax.ShapeDtypeStruct(shape, kind)
            for i, (shape, kind) in enumerate(out_shapes)
        ],
        in_specs=specs,
        out_specs=[
            pl.BlockSpec(memory_space=pltpu.HBM if i in away else pltpu.VMEM)
            for i in range(len(out_shapes))
        ],
        input_output_aliases=aliases or {},
        scratch_shapes=list(scratch),
        compiler_params=pltpu.CompilerParams(vmem_limit_bytes=VMEM_LIMIT),
        cost_estimate=pl.CostEstimate(flops=1000, bytes_accessed=1000, transcendentals=0),
    )(*operands)


def lanes(shape, dim=1):
    return lax.broadcasted_iota(jnp.int32, shape, dim)


def head_tile(head):
    return head // 2


def head_mask(head, shape, dim=1):
    index = lanes(shape, dim)
    return index >= HEAD_DIM if head % 2 else index < HEAD_DIM


def only(values, mask):
    return jnp.where(mask, values, jnp.zeros_like(values))


def packed_out(weight_ref):
    rows = weight_ref.shape[0]
    parts = [
        weight_ref[:, GROUP * i + TILE : GROUP * (i + 1)].astype(FULL) for i in range(3)
    ]
    low = head_mask(0, (rows, TILE))
    first = jnp.where(low, pltpu.roll(parts[0], HEAD_DIM, 1), parts[1])
    second = jnp.where(low, pltpu.roll(parts[2], HEAD_DIM, 1), 0.0)
    return jnp.concatenate([first, second], axis=1).astype(LOW)


def lined_heads(rows):
    first, second = rows[:, :TILE], rows[:, TILE:]
    return [pltpu.roll(first, HEAD_DIM, 1), first, pltpu.roll(second, HEAD_DIM, 1)]


def transposed(values):
    return jnp.transpose(values.astype(FULL))


def expand_matrix(count):
    shape = (count, 4 * count)
    return jnp.where(lanes(shape) // 4 == lanes(shape, 0), 1.0, 0.0).astype(LOW)


def unpack_lines(index, lower, line_refs, vector_ref, columns, width):
    devices, size = line_refs[0].shape[2:]
    devices = 2 * devices
    each = width // (4 * devices)
    flipped = []
    for part in range(2):
        near = [ref[far, part].astype(FULL) for far in range(2) for ref in line_refs]
        ordered = []
        for at in range(8):
            row = near[7]
            for mask in range(7):
                row = jnp.where((2 * index + lower) ^ (mask % 4 * 2 + mask // 4) == at, near[mask], row)
            ordered.append(row)
        flipped.append(jnp.transpose(jnp.concatenate(ordered, axis=0)).astype(LOW))

    def spread_lines(place, valid):
        shape = (4 * devices, place.shape[1])
        row = lanes(shape, 0)
        select = (row % devices == place // (4 * each)) & (
            row // devices == place % (4 * each) // each
        )
        select = jnp.where(select & valid, 1.0, 0.0).astype(LOW)
        return [jnp.dot(part, select, preferred_element_type=FULL) for part in flipped]

    def vectors_at(place, valid):
        line_at = lanes((size, place.shape[1]), 0)
        keep = (line_at < 8 * each) & (line_at % each == place % each)
        row = lanes((8, size), 0)
        gather = jnp.where(lanes((8, size)) // each == row, 1.0, 0.0).astype(LOW)
        total = jnp.zeros((8, place.shape[1]), FULL)
        for part in spread_lines(place, valid):
            part = jnp.where(keep, part, 0.0).astype(LOW)
            total += jnp.dot(gather, part, preferred_element_type=FULL)
        return total

    place = lanes((1, width))
    vector_ref[...] = vectors_at(place, place >= 0)
    place = lanes((1, GROUP))
    own = vectors_at(place + index * columns, place < columns)
    bias = jnp.concatenate([own[0:1], jnp.zeros((1, GROUP), FULL), own[1:2]], axis=1)
    place = lanes((1, 4 * columns)) + index * (4 * columns)
    line_at = lanes((size, 4 * columns), 0)
    keep = line_at == 8 * each + place % (4 * each)
    up_bias = jnp.zeros((1, 4 * columns), FULL)
    for part in spread_lines(place // 4, place >= 0):
        up_bias += jnp.sum(jnp.where(keep, part, 0.0), axis=0, keepdims=True)
    return (bias, up_bias)


def forward_kernel(
    index_ref,
    near_ref,
    other_ref,
    half_ref,
    half_other_ref,
    segment_ref,
    *refs,
):
    line_refs = refs[:4]
    (
        qkv_out,
        mixed_ref,
        log_ref,
        send_ref,
        keep_ref,
        vector_ref,
        up_bias_ref,
        weight_ref,
        qkv_ref,
        qkv_sem,
    ) = refs[4:]
    index, lower = index_ref[0], index_ref[1]
    half = near_ref.shape[0]
    columns = 3 * HEAD_DIM
    width = weight_ref.shape[0]
    part = width // 2
    weight_ref[pl.ds(pl.multiple_of(lower * part, 16), part), :] = half_ref[:, : 3 * GROUP]
    weight_ref[pl.ds(pl.multiple_of((1 - lower) * part, 16), part), :] = half_other_ref[
        :, : 3 * GROUP
    ]
    bias, up_bias = unpack_lines(index, lower, line_refs, vector_ref, columns, width)
    up_bias_ref[...] = up_bias
    keep = lanes((1, 3 * GROUP)) % GROUP < columns
    for at, rows_ref in ((0, near_ref), (half, other_ref)):
        got = jnp.dot(rows_ref[...], weight_ref[:, : 3 * GROUP], preferred_element_type=FULL)
        qkv_ref[at : at + half, :] = jnp.where(keep, got + bias, 0.0).astype(LOW)
    qkv_copy = pltpu.make_async_copy(qkv_ref, qkv_out, qkv_sem)
    qkv_copy.start()

    length = 2 * half
    row_segments = segment_ref[...]
    column_segments = jnp.transpose(
        jnp.broadcast_to(row_segments.astype(FULL), (TILE, length))
    )[:, :1].astype(jnp.int32)
    same = column_segments == row_segments
    mixed_tiles = [None, None]
    for head in range(3):
        at = TILE * head_tile(head)
        mask = head_mask(head, (length, TILE))
        key = only(qkv_ref[:, GROUP + at : GROUP + at + TILE], mask) * jnp.asarray(0.125, LOW)
        scores = contract(key, qkv_ref[:, at : at + TILE], 1, 1)
        scores = jnp.where(same, scores, MASKED_SCORE)
        highest = jnp.max(scores, axis=0, keepdims=True)
        shifted = jnp.exp(scores - highest)
        total = jnp.sum(shifted, axis=0, keepdims=True)
        probs = (shifted * (1.0 / total)).astype(LOW)
        log_ref[head : head + 1, :] = highest + jnp.log(total)
        value = only(qkv_ref[:, 2 * GROUP + at : 2 * GROUP + at + TILE], mask)
        got = jnp.dot(transposed(value).astype(LOW), probs, preferred_element_type=FULL)
        tile = head_tile(head)
        mixed_tiles[tile] = got if mixed_tiles[tile] is None else mixed_tiles[tile] + got
    log_ref[3:, :] = jnp.zeros((5, length), FULL)
    for tile in range(2):
        mixed_ref[:, TILE * tile : TILE * (tile + 1)] = jnp.transpose(mixed_tiles[tile]).astype(LOW)
    out = packed_out(weight_ref)
    keep_ref[...] = contract(mixed_ref[:half, :], out, 1, 1)
    send_ref[...] = contract(mixed_ref[half:, :], out, 1, 1).astype(LOW)
    qkv_copy.wait()


def backward_kernel(
    index_ref,
    near_ref,
    other_ref,
    qkv_ref,
    log_ref,
    weight_ref,
    segment_ref,
    sums_ref,
    up_sum_ref,
    up_sum_other_ref,
    grad_ref,
    send_ref,
    keep_ref,
    vector_ref,
    mixed_grad,
    key_grad,
    value_grad,
    columns_held,
):
    index = index_ref[0]
    half = near_ref.shape[0]
    length = 2 * half
    columns = 3 * HEAD_DIM
    out = packed_out(weight_ref)
    mixed_grad[:half, :] = jnp.dot(near_ref[...], out, preferred_element_type=FULL).astype(LOW)
    mixed_grad[half:, :] = jnp.dot(other_ref[...], out, preferred_element_type=FULL).astype(LOW)
    row_segments = segment_ref[...]
    column_segments = jnp.transpose(
        jnp.broadcast_to(row_segments.astype(FULL), (TILE, length))
    )[:, :1].astype(jnp.int32)
    same = column_segments == row_segments
    sums = []
    for tile in range(2):
        at = TILE * tile
        query_grad = jnp.zeros((TILE, length), FULL)
        for head in (0, 1) if tile == 0 else (2,):
            mask = head_mask(head, (length, TILE))
            scale = jnp.asarray(0.125, LOW)
            key = only(qkv_ref[:, GROUP + at : GROUP + at + TILE], mask) * scale
            query = only(qkv_ref[:, at : at + TILE], mask)
            value = only(qkv_ref[:, 2 * GROUP + at : 2 * GROUP + at + TILE], mask)
            grad = only(mixed_grad[:, at : at + TILE], mask)
            scores = contract(key, query, 1, 1)
            probs = jnp.exp(
                jnp.where(same, scores, MASKED_SCORE) - log_ref[head : head + 1, :]
            )
            probs_grad = contract(value, grad, 1, 1)
            inner = jnp.sum(probs * probs_grad, axis=0, keepdims=True)
            scores_grad = (probs * (probs_grad - inner)).astype(LOW)
            got = jnp.dot(probs.astype(LOW), grad, preferred_element_type=FULL)
            got_key = jnp.dot(scores_grad, query * scale, preferred_element_type=FULL)
            if head % 2 == 0:
                value_grad[...] = got
                key_grad[...] = got_key
            else:
                value_grad[...] += got
                key_grad[...] += got_key
            query_grad += jnp.dot(
                transposed(key).astype(LOW), scores_grad, preferred_element_type=FULL
            )
        query_low = jnp.transpose(query_grad).astype(LOW)
        value_low = value_grad[...].astype(LOW)
        grad_ref[:, at : at + TILE] = query_low
        grad_ref[:, GROUP + at : GROUP + at + TILE] = key_grad[...].astype(LOW)
        grad_ref[:, 2 * GROUP + at : 2 * GROUP + at + TILE] = value_low
        sums.append(
            (
                jnp.sum(query_low.astype(FULL), axis=0, keepdims=True),
                jnp.sum(value_low.astype(FULL), axis=0, keepdims=True),
            )
        )
    wide = weight_ref[:, : 3 * GROUP]
    keep_ref[...] = contract(grad_ref[:half, :], wide, 1, 1)
    send_ref[...] = contract(grad_ref[half:, :], wide, 1, 1).astype(LOW)

    up_row = up_sum_ref[...] + up_sum_other_ref[...]
    place = lanes((8, 4 * columns))
    spaced = jnp.where(place % 4 == lanes((8, 4 * columns), 0), up_row, 0.0)
    high = spaced.astype(LOW)
    low = (spaced - high.astype(FULL)).astype(LOW)
    expand = expand_matrix(columns)
    up_rows = contract(high, expand, 1, 1) + contract(low, expand, 1, 1)
    up_rows = jnp.concatenate([up_rows, jnp.zeros((8, GROUP - columns), FULL)], axis=1)
    query_sum = jnp.concatenate([sums[0][0], sums[1][0]], axis=1)
    value_sum = jnp.concatenate([sums[0][1], sums[1][1]], axis=1)
    at_row = lanes((8, GROUP), 0)
    late = jnp.where(at_row == 6, query_sum, jnp.where(at_row == 7, value_sum, 0.0))
    stacked = jnp.concatenate([late, up_rows, jnp.zeros((TILE - 16, GROUP), FULL)], axis=0)
    columns_held[...] = jnp.zeros_like(columns_held)
    columns_held[pl.ds(pl.multiple_of(index * columns, 64), columns), :] = jnp.transpose(stacked)[
        :columns
    ]
    placed = jnp.transpose(columns_held[...])[:16]
    given = sums_ref[...]
    vector_ref[:8, :] = placed[:8] + given
    vector_ref[8:, :] = placed[8:]


def weights_kernel(
    tokens_near, tokens_other, near_ref, other_ref, grad_ref, mixed_ref, out, out_ref, sem
):
    half = near_ref.shape[0]
    width = near_ref.shape[1]
    got = contract(tokens_near[...], grad_ref[:half, :], 0, 0) + contract(
        tokens_other[...], grad_ref[half:, :], 0, 0
    )
    out_grad = contract(near_ref[...], mixed_ref[:half, :], 0, 0) + contract(
        other_ref[...], mixed_ref[half:, :], 0, 0
    )
    high = head_mask(1, (width, TILE))
    for part, lined in enumerate(lined_heads(out_grad)):
        at = GROUP * part
        out_ref[:, at : at + TILE] = got[:, at : at + TILE].astype(LOW)
        out_ref[:, at + TILE : at + GROUP] = jnp.where(
            high, lined, got[:, at + TILE : at + GROUP]
        ).astype(LOW)
    copy = pltpu.make_async_copy(out_ref, out.at[:, : 3 * GROUP], sem)
    copy.start()
    copy.wait()


def vectors_kernel(block_ref, own_ref, core_ref, far_ref, both_ref, out_ref, held, sem):
    total = own_ref[...]
    for ref in (core_ref, far_ref, both_ref):
        total += ref[...].astype(FULL)
    total = total[:12]
    high = total.astype(LOW).astype(FULL)
    rows = jnp.concatenate(
        [high, total - high, jnp.zeros((TILE - 24, total.shape[1]), FULL)], axis=0
    )
    held[...] = jnp.transpose(rows).astype(LOW)
    copy = pltpu.make_async_copy(held, out_ref.at[:, 3 * GROUP :], sem)
    copy.start()
    copy.wait()


def place_of(vector_rows, shape, dim):
    place = lanes(shape, dim)
    many = 8 * vector_rows
    row = jnp.where(place < many, place % vector_rows, (place - many) // 4)
    column = jnp.where(place < many, place // vector_rows, 8 + (place - many) % 4)
    return (row, jnp.where(place < many + 4 * vector_rows, column, 1000))


def first_block_kernel(line_ref, weight_ref, block_ref):
    rows = weight_ref.shape[0]
    columns_each = weight_ref.shape[1] // 4
    count = line_ref.shape[0]
    row_at = lanes((rows, TILE), 0)
    packed = jnp.zeros((rows, TILE), FULL)
    for at in range(count):
        line = line_ref[at : at + 1]
        high = line.astype(LOW).astype(FULL)
        packed = jnp.where(row_at == at, high, packed)
        packed = jnp.where(row_at == count + at, line - high, packed)
    weight = weight_ref[...].astype(FULL)
    q_part, k_part, v_part, out = [
        weight[:, columns_each * i : columns_each * (i + 1)] for i in range(4)
    ]
    block = jnp.concatenate(
        [
            q_part,
            out[:, :HEAD_DIM],
            k_part,
            out[:, HEAD_DIM : 2 * HEAD_DIM],
            v_part,
            out[:, 2 * HEAD_DIM :],
            packed,
        ],
        axis=1,
    ).astype(LOW)
    for at in range(block_ref.shape[0]):
        block_ref[at] = block


def second_block_kernel(index_ref, own_ref, other_ref, block_ref):
    lower = index_ref[0] == 0
    own = own_ref[...].astype(FULL)
    other = other_ref[...].astype(FULL)
    block = jnp.concatenate(
        [jnp.where(lower, own, other), jnp.where(lower, other, own)], axis=0
    ).astype(LOW)
    for at in range(block_ref.shape[0]):
        block_ref[at] = block


def moments(values, gain, shift):
    center = values - jnp.mean(values, axis=-1, keepdims=True)
    scale_inv = lax.rsqrt(jnp.mean(center * center, axis=-1, keepdims=True) + NORM_EPSILON)
    normed = center * scale_inv
    return (normed * gain + shift, normed, scale_inv)


def norm_backward(upstream, normed, scale_inv, gain):
    scaled = upstream * gain
    return scale_inv * (
        scaled
        - jnp.mean(scaled, axis=-1, keepdims=True)
        - normed * jnp.mean(scaled * normed, axis=-1, keepdims=True)
    )


def blocks_of(rows, size=64):
    return [(at, at + size) for at in range(0, rows, size)]


def first_norm_kernel(tokens_ref, chip_ref, far_ref, rows_ref, low_ref, scale_ref):
    for at, to in blocks_of(tokens_ref.shape[0], TILE):
        values = (
            tokens_ref[at:to].astype(FULL)
            + (chip_ref[at:to] + far_ref[at:to].astype(FULL))
            + rows_ref[2:3]
        )
        first, _, scale_inv = moments(values, rows_ref[4:5], rows_ref[5:6])
        low_ref[at:to] = first.astype(LOW)
        scale_ref[:, at:to] = jnp.transpose(jnp.broadcast_to(scale_inv, (TILE, TILE)))[:8]


def feed_rows(rows_ref, up, down, bias_ref, active_ref, slope_ref, part_ref):
    size = rows_ref.shape[0] // 2
    for at, to in blocks_of(rows_ref.shape[0], size):
        upward = jnp.dot(rows_ref[at:to], up[...], preferred_element_type=FULL) + bias_ref[...]
        for low, high in blocks_of(size, 32):
            part = upward[low:high]
            gate = 0.5 * (1.0 + lax.erf(part * ROOT_HALF))
            active_ref[at + low : at + high] = (part * gate).astype(LOW)
            slope_ref[at + low : at + high] = (
                gate + part * jnp.exp(-0.5 * part * part) * INV_ROOT_TAU
            ).astype(LOW)
        got = contract(active_ref[at:to], down[...], 1, 1)
        part_ref[at:to] = got.astype(part_ref.dtype)


def feed_other_kernel(
    rows_ref, blocks_ref, bias_ref, active_ref, slope_ref, part_ref, up_ref, down_ref
):
    count, rows, wide = blocks_ref.shape
    rows = rows // 2
    hidden = wide // 2
    group = 1 if rows % 16 == 0 else 2
    for lower in range(2):
        for at in range(0, count, group):
            got = jnp.concatenate(
                [
                    blocks_ref[at + i].astype(FULL)[rows * lower : rows * (lower + 1)]
                    for i in range(group)
                ],
                axis=0,
            ).astype(LOW)
            to = (lower * count + at) * rows
            up_ref[to : to + group * rows] = got[:, :hidden]
            down_ref[to : to + group * rows] = got[:, hidden:]
    feed_rows(rows_ref, up_ref, down_ref, bias_ref, active_ref, slope_ref, part_ref)


def feed_near_kernel(rows_ref, up_ref, down_ref, bias_ref, active_ref, slope_ref, part_ref):
    feed_rows(rows_ref, up_ref, down_ref, bias_ref, active_ref, slope_ref, part_ref)


def second_norm_kernel(
    first_ref,
    chip_ref,
    far_ref,
    rows_ref,
    cotangent_ref,
    cotangent_far_ref,
    output_ref,
    low_ref,
    sums_ref,
):
    own = output_ref.shape[0]
    sums = [jnp.zeros((1, first_ref.shape[1]), FULL) for _ in range(3)]
    for at, to in blocks_of(first_ref.shape[0]):
        values = first_ref[at:to].astype(FULL) + (chip_ref[at:to] + far_ref[at:to].astype(FULL)) + rows_ref[3:4]
        output, normed, scale_inv = moments(values, rows_ref[6:7], rows_ref[7:8])
        if to <= own:
            upstream = cotangent_ref[at:to].astype(FULL)
            output_ref[at:to] = output.astype(LOW)
        else:
            upstream = cotangent_far_ref[at - own : to - own].astype(FULL)
        grad = norm_backward(upstream, normed, scale_inv, rows_ref[6:7])
        low = grad.astype(LOW)
        low_ref[at:to] = low
        if to <= own:
            for i, part in enumerate((low.astype(FULL), upstream * normed, upstream)):
                sums[i] += jnp.sum(part, axis=0, keepdims=True)
    sums_ref[...] = jnp.concatenate(sums + [jnp.zeros((5, sums[0].shape[1]), FULL)], axis=0)


def feed_backward_kernel(rows_ref, up_ref, down_ref, slope_ref, grad_ref, part_ref, sum_ref):
    size = rows_ref.shape[0] // 2
    total = jnp.zeros((1, up_ref.shape[1]), FULL)
    for at, to in blocks_of(rows_ref.shape[0], size):
        grad = jnp.dot(rows_ref[at:to], down_ref[...], preferred_element_type=FULL)
        for low, high in blocks_of(size, 32):
            place = slice(at + low, at + high)
            part = (grad[low:high] * slope_ref[place].astype(FULL)).astype(LOW)
            grad_ref[place] = part
            total += jnp.sum(part.astype(FULL), axis=0, keepdims=True)
        got = contract(grad_ref[at:to], up_ref[...], 1, 1)
        part_ref[at:to] = got.astype(part_ref.dtype)
    sum_ref[...] = total


def feed_weights_kernel(
    hidden_near,
    hidden_other,
    branch_near,
    branch_other,
    active_near,
    active_other,
    grad_near,
    grad_other,
    out,
    out_ref,
    sems,
):
    count, rows, wide = out_ref.shape
    rows = rows // 2
    hidden = wide // 2
    copies = []
    for place, near, other, right_near, right_other in (
        (0, hidden_near, hidden_other, grad_near, grad_other),
        (hidden, branch_near, branch_other, active_near, active_other),
    ):
        got = contract(near[...], right_near[...], 0, 0) + contract(
            other[...], right_other[...], 0, 0
        )
        for at in range(count):
            out_ref[at, :, place : place + hidden] = jnp.concatenate(
                [got[at * rows : (at + 1) * rows], got[(count + at) * rows :][:rows]], axis=0
            ).astype(LOW)
        half = pl.ds(place, hidden)
        copy = pltpu.make_async_copy(
            out_ref.at[:, :, half], out.at[:, :, half], sems.at[place // hidden]
        )
        copy.start()
        copies.append(copy)
    for copy in copies:
        copy.wait()


def first_norm_backward_kernel(
    second_ref,
    chip_ref,
    far_ref,
    first_ref,
    scale_ref,
    rows_ref,
    second_sums_ref,
    grad_ref,
    low_ref,
    sums_ref,
):
    own = grad_ref.shape[0]
    sums = [jnp.zeros((1, second_ref.shape[1]), FULL) for _ in range(3)]
    inverse = 1.0 / rows_ref[4:5]
    for at, to in blocks_of(second_ref.shape[0], TILE):
        upstream = second_ref[at:to].astype(FULL) + (
            chip_ref[at:to] + far_ref[at:to].astype(FULL)
        )
        normed = (first_ref[at:to].astype(FULL) - rows_ref[5:6]) * inverse
        scale_inv = jnp.transpose(jnp.broadcast_to(scale_ref[:1, at:to], (TILE, TILE)))[:, :1]
        grad = norm_backward(upstream, normed, scale_inv, rows_ref[4:5])
        low = grad.astype(LOW)
        low_ref[at:to] = low
        if to <= own:
            grad_ref[at:to] = grad
            for i, part in enumerate((low.astype(FULL), upstream * normed, upstream)):
                sums[i] += jnp.sum(part, axis=0, keepdims=True)
    given = second_sums_ref[...]
    sums_ref[...] = jnp.concatenate(
        [
            sums[0],
            given[0:1],
            sums[1],
            sums[2],
            given[1:3],
            jnp.zeros((2, sums[0].shape[1]), FULL),
        ],
        axis=0,
    )


def plane_sum_kernel(index_ref, blocks_ref, keep_ref, send_ref):
    rows = keep_ref.shape[0]
    total = blocks_ref[0].astype(FULL)
    for at in range(1, blocks_ref.shape[0]):
        total += blocks_ref[at].astype(FULL)
    lower = index_ref[0] == 0
    keep_ref[...] = jnp.where(lower, total[:rows], total[rows:])
    send_ref[...] = jnp.where(lower, total[rows:], total[:rows]).astype(send_ref.dtype)


def last_sum_kernel(index_ref, blocks_ref, q_ref, k_ref, v_ref, out_ref, *vector_refs):
    index = index_ref[0]
    rows = q_ref.shape[0]
    vector_rows = rows // 4
    columns = q_ref.shape[1]
    total = blocks_ref[0].astype(FULL)
    for at in range(1, blocks_ref.shape[0]):
        total += blocks_ref[at].astype(FULL)
    q_ref[...] = total[:, :columns]
    k_ref[...] = total[:, GROUP : GROUP + columns]
    v_ref[...] = total[:, 2 * GROUP : 2 * GROUP + columns]
    out_ref[...] = jnp.concatenate(
        [total[:, GROUP * i + columns : GROUP * (i + 1)] for i in range(3)], axis=1
    )
    packed = total[:, 3 * GROUP :]
    packed = packed + pltpu.roll(packed, TILE - 12, 1)
    wide = -(-12 * vector_rows // TILE) * TILE
    _, place_column = place_of(vector_rows, (TILE, wide), 1)
    select = jnp.where(place_column == lanes((TILE, wide), 0), 1.0, 0.0).astype(LOW)
    line = jnp.zeros((rows, wide), FULL)
    left = packed
    for _ in range(3):
        part = left.astype(LOW)
        left = left - part.astype(FULL)
        line += jnp.dot(part, select, preferred_element_type=FULL)
    place_row, _ = place_of(vector_rows, (rows, wide), 1)
    keep = place_row + index * vector_rows == lanes((rows, wide), 0)
    line = jnp.sum(jnp.where(keep, line, 0.0), axis=0, keepdims=True)
    for at, ref in enumerate(vector_refs):
        size = ref.shape[1]
        place = at * vector_rows
        ref[...] = pltpu.roll(line, wide - place, 1)[:, :size] if place else line[:, :size]


def shards(
    tokens,
    segments,
    q_weight,
    k_weight,
    v_weight,
    up_weight,
    out_weight,
    down_weight,
    q_bias,
    v_bias,
    out_bias,
    up_bias,
    down_bias,
    norm1_gain,
    norm1_shift,
    norm2_gain,
    norm2_shift,
    cotangent,
):
    my_index = lax.axis_index("tensor")
    dp_count = lax.axis_size("dp")
    local_len, width = tokens.shape[1:]
    half = 2 * local_len
    length = 4 * local_len
    shard_rows, head_cols = q_weight.shape
    hidden_cols = up_weight.shape[1]
    tokens = tokens[0]
    cotangent = cotangent[0]
    index = my_index.reshape(1)
    side_index = (lax.axis_index("dp") // (dp_count // 2)).reshape(1)

    vector_rows = q_bias.shape[0]
    line_size = -(-12 * vector_rows // TILE) * TILE
    line_count = line_size // TILE
    line = jnp.concatenate(
        [
            q_bias,
            v_bias,
            out_bias,
            down_bias,
            norm1_gain,
            norm1_shift,
            norm2_gain,
            norm2_shift,
            up_bias,
            jnp.zeros((line_size - 12 * vector_rows,), FULL),
        ]
    ).reshape(line_count, TILE)
    first_own = jnp.concatenate([q_weight, k_weight, v_weight, out_weight], axis=1)
    (first_block,) = call(
        first_block_kernel,
        [((dp_count // 2, shard_rows, 3 * GROUP + TILE), LOW)],
        line,
        first_own,
    )
    first_half = plane(first_block)
    tokens_far = swap(tokens, 2)
    second_own = jnp.concatenate([up_weight, down_weight], axis=1)
    second_side = side(second_own)
    tokens_pair = jnp.concatenate([tokens, tokens_far], axis=0)
    cotangent_far = swap(cotangent, 2)
    tokens_core = swap(tokens_pair, 1)
    segment_row = ordered_segments(segments[0], my_index)[None]
    (second_block,) = call(
        second_block_kernel,
        [((dp_count // 2, 2 * shard_rows, 2 * hidden_cols), LOW)],
        side_index,
        second_own,
        second_side,
        smem=1,
    )
    first_half, second_block = lax.optimization_barrier((first_half, second_block))
    first_other = side(first_half)
    lines = jnp.stack(
        [half_rows[:, : 2 * line_count, 3 * GROUP :] for half_rows in (first_half, first_other)]
    )
    lines = lines.reshape(2, dp_count // 2, 2, line_size).transpose(0, 2, 1, 3)
    lines = [lines] + [swap(lines, mask) for mask in (1, 2, 3)]
    segment_row = after(segment_row, cotangent_far)
    second_full = plane(second_block)

    qkv_rows, mixed_rows, log_totals, attn_send, attn_keep, rows, bias_up, first_full = call(
        forward_kernel,
        [
            ((length, 3 * GROUP), LOW),
            ((length, GROUP), LOW),
            ((8, length), FULL),
            ((half, width), LOW),
            ((half, width), FULL),
            ((8, width), FULL),
            ((1, hidden_cols), FULL),
            ((width, 3 * GROUP), LOW),
        ],
        jnp.concatenate([index, side_index]),
        tokens_pair,
        tokens_core,
        first_half.reshape(width // 2, -1),
        first_other.reshape(width // 2, -1),
        segment_row,
        *lines,
        smem=1,
        scratch=[pltpu.VMEM((length, 3 * GROUP), LOW), pltpu.SemaphoreType.DMA],
        away=(0,),
    )
    attn_chip = attn_keep + swap(attn_send, 1).astype(FULL)
    attn_far = swap(far_pack(attn_chip), 2)
    hidden_low, inv_first = call(
        first_norm_kernel,
        [((half, width), LOW), ((8, half), FULL)],
        tokens_pair,
        attn_chip,
        attn_far,
        rows,
    )
    hidden_core = swap(hidden_low, 1)
    active_other, slope_other, branch_send, up_full, down_full = call(
        feed_other_kernel,
        [
            ((half, hidden_cols), LOW),
            ((half, hidden_cols), LOW),
            ((half, width), LOW),
            ((width, hidden_cols), LOW),
            ((width, hidden_cols), LOW),
        ],
        hidden_core,
        second_full,
        bias_up,
    )
    branch_got = swap(branch_send, 1)
    active_near, slope_near, branch_keep = call(
        feed_near_kernel,
        [((half, hidden_cols), LOW), ((half, hidden_cols), LOW), ((half, width), FULL)],
        hidden_low,
        up_full,
        down_full,
        bias_up,
    )
    branch_chip = branch_keep + branch_got.astype(FULL)
    layer_output, branch_low, second_sums = call(
        second_norm_kernel,
        [((local_len, width), LOW), ((half, width), LOW), ((8, width), FULL)],
        hidden_low,
        branch_chip,
        swap(far_pack(branch_chip), 2),
        rows,
        cotangent,
        cotangent_far,
    )
    branch_core = swap(branch_low, 1)
    near_shapes = [((half, hidden_cols), LOW), ((half, width), FULL), ((1, hidden_cols), FULL)]
    upward_near, hidden_keep, up_sum_near = call(
        feed_backward_kernel, near_shapes, branch_low, up_full, down_full, slope_near
    )
    other_shapes = [near_shapes[0], ((half, width), LOW), near_shapes[2]]
    upward_other, hidden_send, up_sum_other = call(
        feed_backward_kernel,
        other_shapes,
        after(branch_core, upward_near),
        up_full,
        down_full,
        slope_other,
    )
    hidden_got = swap(hidden_send, 1)
    hidden_chip = hidden_keep + hidden_got.astype(FULL)
    hidden_sent = far_pack(hidden_chip)
    hidden_far = swap(hidden_sent, 2)
    (pair_block,) = call(
        feed_weights_kernel,
        [((dp_count // 2, 2 * shard_rows, 2 * hidden_cols), LOW)],
        hidden_low,
        hidden_core,
        branch_low,
        branch_core,
        active_near,
        active_other,
        upward_near,
        upward_other,
        scratch=[
            pltpu.VMEM((dp_count // 2, 2 * shard_rows, 2 * hidden_cols), LOW),
            pltpu.SemaphoreType.DMA((2,)),
        ],
        away=(0,),
    )
    pair_blocks = plane(pair_block)
    resid_grad, attended_low, given = call(
        first_norm_backward_kernel,
        [((local_len, width), FULL), ((half, width), LOW), ((8, width), FULL)],
        branch_low,
        hidden_chip,
        hidden_far,
        hidden_low,
        inv_first,
        rows,
        second_sums,
    )
    attended_core = swap(attended_low, 1)
    qkv_grad, input_send, input_keep, vector_sums = call(
        backward_kernel,
        [
            ((length, 3 * GROUP), LOW),
            ((half, width), LOW),
            ((half, width), FULL),
            ((16, width), FULL),
        ],
        index,
        attended_low,
        attended_core,
        qkv_rows,
        log_totals,
        first_full,
        segment_row,
        given,
        up_sum_near,
        up_sum_other,
        smem=1,
        scratch=[
            pltpu.VMEM((length, GROUP), LOW),
            pltpu.VMEM((length, TILE), FULL),
            pltpu.VMEM((length, TILE), FULL),
            pltpu.VMEM((width, TILE), FULL),
        ],
    )
    input_chip = input_keep + swap(input_send, 1).astype(FULL)
    input_sent = input_chip[local_len:].astype(LOW)
    input_far = swap(input_sent, 2)
    vector_near = [swap(vector_sums.astype(LOW), mask) for mask in (1, 2, 3)]
    (last_block,) = call(
        weights_kernel,
        [((width, 3 * GROUP + TILE), LOW)],
        tokens_pair,
        tokens_core,
        attended_low,
        attended_core,
        qkv_grad,
        mixed_rows,
        scratch=[pltpu.VMEM((width, 3 * GROUP), LOW), pltpu.SemaphoreType.DMA],
        away=(0,),
    )
    (last_block,) = call(
        vectors_kernel,
        [((width, 3 * GROUP + TILE), LOW)],
        last_block,
        vector_sums,
        *vector_near,
        scratch=[pltpu.VMEM((width, TILE), LOW), pltpu.SemaphoreType.DMA],
        away=(0,),
        far=(0,),
        aliases={0: 0},
    )
    last_block = after(last_block, input_far)
    last_blocks = spread(last_block.reshape(dp_count, shard_rows, 3 * GROUP + TILE))
    input_grad = resid_grad + (input_chip[:local_len] + input_far.astype(FULL))

    pair_keep, pair_send = call(
        plane_sum_kernel,
        [((shard_rows, 2 * hidden_cols), FULL), ((shard_rows, 2 * hidden_cols), LOW)],
        side_index,
        pair_blocks,
        smem=1,
    )
    pair_sum = pair_keep + side(pair_send).astype(FULL)
    q_grad, k_grad, v_grad, out_grad, *vectors = call(
        last_sum_kernel,
        [((shard_rows, head_cols), FULL)] * 4
        + [((1, vector_rows), FULL)] * 8
        + [((1, 4 * vector_rows), FULL)],
        index,
        last_blocks,
        smem=1,
    )
    vectors = [vector.reshape(-1) for vector in vectors]
    return (
        layer_output[None],
        input_grad[None],
        q_grad,
        k_grad,
        v_grad,
        pair_sum[:, :hidden_cols],
        out_grad,
        pair_sum[:, hidden_cols:],
        vectors[6],
        vectors[7],
        vectors[0],
        vectors[8],
        vectors[1],
        vectors[2],
        vectors[3],
        vectors[4],
        vectors[5],
    )


def solution(mesh):
    matrix = P("dp", "tensor")
    vector = P(("dp", "tensor"))
    rows = P("dp", "tensor", None)
    return jax.shard_map(
        shards,
        mesh=mesh,
        in_specs=(rows, P("dp", None)) + (matrix,) * 6 + (vector,) * 9 + (rows,),
        out_specs=(rows, rows) + (matrix,) * 6 + (vector,) * 9,
        check_vma=False,
    )
```
